32 devices in a mesh: dp: 8 (over z, y), tensor: 4 (over x, core).
Axes of the slice: x: 2, y: 2, z: 4, core: 2. Of those that a mesh axis runs over, the one named last changes fastest.
Arguments:
- tokens: bfloat16 [24, 1024, 512], P('dp', 'tensor'), may hold values from -6 to 6
- lengths: int32 [24], P('dp'), may hold values from 256 to 1024, as said below
- memory: bfloat16 [20, 512], replicated, may hold values from -6 to 6
- norm_gain: bfloat16 [2, 2, 512], replicated, may hold values from 0.25 to 1.75
- w_qkv: bfloat16 [2, 3, 512, 512], P(None, None, None, 'tensor'), may hold values from -0.25 to 0.25
- output_weight: bfloat16 [2, 512, 512], P(None, 'tensor'), may hold values from -4 to 4
- w_up: bfloat16 [2, 512, 2048], P(None, None, 'tensor'), may hold values from -0.25 to 0.25
- w_down: bfloat16 [2, 2048, 512], P(None, 'tensor'), may hold values from -0.125 to 0.125
- cot_tokens: bfloat16 [24, 1024, 512], P('dp', 'tensor'), may hold values from -6 to 6
- cot_memory: bfloat16 [24, 20, 512], P('dp'), may hold values from -6 to 6
Outputs:
- out_tokens: bfloat16 [24, 1024, 512], P('dp', 'tensor')
- out_memory: bfloat16 [24, 20, 512], P('dp')
- grad_tokens: float32 [24, 1024, 512], P('dp', 'tensor')
- grad_memory: float32 [20, 512], replicated
- grad_attn_gain: float32 [2, 512], replicated
- grad_ffn_gain: float32 [2, 512], replicated
- grad_qkv: float32 [2, 3, 512, 512], P(None, None, None, 'tensor')
- grad_out: float32 [2, 512, 512], P(None, 'tensor')
- grad_up: float32 [2, 512, 2048], P(None, None, 'tensor')
- grad_down: float32 [2, 2048, 512], P(None, 'tensor')
The draws below stay inside these ranges and needn't reach their ends.
Inputs may be any that keep to these rules, and one draw needn't show every extreme that they name: `lengths`: among the 3 sequences of every index of dp, at least one is longer than 768; some sequence has length 1024.
All inputs are finite; a program needn't handle non-finite values.
Results may differ from the reference program's by a relative error of at most 0.04.
Values may be sent and summed in bfloat16 or wider, within the bound.
No kernel may reach another device: no remote copies, remote signals or barrier semaphores. Data moves between devices by JAX's collectives and lax.ppermute only.
A program may use at most 192 MiB of HBM per device.

```python
import jax
import jax.numpy as jnp
from jax import lax

D = 512
H = 8
DH = 64
FF = 2048
M = 20
TLEN = 1024
SLOTS = 3
SEQS = 24
N_TENSOR = 4


def draw_lengths(key, part):
    key = jax.random.fold_in(key, 7)
    key_values, key_choice, key_long, key_full = jax.random.split(key, 4)
    groups = SEQS // SLOTS
    values = jax.random.randint(key_values, (groups, SLOTS), TLEN // 4, TLEN + 1)
    chosen = jax.random.randint(key_choice, (groups, 1), 0, SLOTS)
    long_values = jax.random.randint(key_long, (groups, 1), TLEN - TLEN // N_TENSOR + 1, TLEN + 1)
    slot_ids = jnp.arange(SLOTS)[None, :]
    values = jnp.where(slot_ids == chosen, long_values, values).reshape(SEQS)
    full_index = jax.random.randint(key_full, (), 0, SEQS)
    values = jnp.where(jnp.arange(SEQS) == full_index, TLEN, values)
    return values.astype(jnp.int32)


def block_scale(own_key, shape, cuts, smallest, top_value):
    gain, own = 1.0, jax.random.fold_in(own_key, 6)
    for dim, shards_of in cuts:
        steps = jnp.exp(jax.random.uniform(jax.random.fold_in(own, dim), (shards_of,), jnp.float32, smallest / len(cuts), top_value / len(cuts)))
        gain = gain * jnp.repeat(steps, shape[dim] // shards_of).reshape([-1 if axis == dim else 1 for axis in range(len(shape))])
    return gain


def noise(key, extent, scale, limit, pieces=(), kind=jnp.bfloat16):
    result = jax.random.normal(key, extent, jnp.float32) * scale
    if len(pieces) > 0:
        result = block_scale(key, extent, pieces, -0.22, 0.18) * result
    return jnp.clip(result, min=-limit, max=limit).astype(kind)


def setup_inputs(seed: int = 0) -> dict:
    splits = jax.random.split(jax.random.key(seed), 11)
    tokens = noise(splits[0], (SEQS, TLEN, D), 1.0, 6.0, ((0, 8), (1, 4)))
    lengths = draw_lengths(jax.random.fold_in(splits[10], 71), 0)
    memory = noise(splits[2], (M, D), 1.0, 6.0)
    norm_gain = jnp.clip(1.0 + 0.15 * jax.random.normal(splits[3], (2, 2, D), jnp.float32), 0.25, 1.75).astype(jnp.bfloat16)
    w_qkv = noise(splits[4], (2, 3, D, D), D ** -0.5, 0.25, ((3, 4),))
    output_weight = noise(splits[5], (2, D, D), 0.7, 4.0, ((1, 4),))
    w_up = noise(splits[6], (2, D, FF), D ** -0.5, 0.25, ((2, 4),))
    w_down = noise(splits[7], (2, FF, D), FF ** -0.5, 0.125, ((1, 4),))
    cot_tokens = noise(splits[8], (SEQS, TLEN, D), 1.0, 6.0, ((0, 8), (1, 4)))
    cot_memory = noise(splits[9], (SEQS, M, D), 1.0, 6.0, ((0, 8),))
    return dict(tokens=tokens, lengths=lengths, memory=memory, norm_gain=norm_gain, w_qkv=w_qkv, output_weight=output_weight, w_up=w_up, w_down=w_down, cot_tokens=cot_tokens, cot_memory=cot_memory)


@jax.custom_vjp
def low(v):
    return lax.optimization_barrier(v.astype(jnp.bfloat16)).astype(jnp.float32)

@jax.custom_vjp
def low_back(v):
    return v

def low_keep(v):
    return (low(v), None)

def low_pass(kept, grad):
    return (grad,)

def back_keep(v):
    return (v, None)

def back_low(kept, grad):
    return (low(grad),)
low.defvjp(low_keep, low_pass)
low_back.defvjp(back_keep, back_low)
precise = lax.Precision.HIGHEST

def normalize(state):
    center = lax.optimization_barrier(jnp.mean(state, axis=-1, keepdims=True))
    spread = lax.optimization_barrier(jnp.mean((state - center) ** 2, axis=-1, keepdims=True))
    return (state - center) * lax.rsqrt(spread + 1e-05)

def both_ways(value):
    return low(low_back(value))

def attend(queries, key_rows, value_rows, key_valid):
    scores = jnp.einsum('qhd,khd->hqk', queries, key_rows, precision=precise) * DH ** (-0.5)
    scores = jnp.where(key_valid[None, None, :], scores, -1e+30)
    scores = low_back(scores)
    weights = low(jax.nn.softmax(scores, axis=-1))
    attention_result = jnp.einsum('hqk,khd->qhd', weights, value_rows, precision=precise)
    return both_ways(attention_result)

def full_mixer(queries, key_rows, value_rows, key_valid):
    return attend(queries, key_rows, value_rows, key_valid)

def bottleneck_mixer(queries, key_rows, value_rows, key_valid):
    memory_part = attend(queries[:M], key_rows, value_rows, key_valid)
    token_part = attend(queries[M:], key_rows[:M], value_rows[:M], key_valid[:M])
    return jnp.concatenate([memory_part, token_part], axis=0)

def residual_block(state, key_valid, gain_pair, w_three, projection_weight, w_first, w_second, mixer):
    row_count = state.shape[0]
    normed = low(normalize(state) * gain_pair[0])
    head_list = []
    for proj_index in range(3):
        projected = jnp.dot(normed, w_three[proj_index], precision=precise)
        head_list.append(both_ways(projected).reshape(row_count, H, DH))
    attention_result = mixer(head_list[0], head_list[1], head_list[2], key_valid)
    state = state + low_back(jnp.dot(attention_result.reshape(row_count, D), projection_weight, precision=precise))
    normed = low(normalize(state) * gain_pair[1])
    hidden = low_back(jnp.dot(normed, w_first, precision=precise))
    active = low(jax.nn.gelu(hidden))
    return state + low_back(jnp.dot(active, w_second, precision=precise))

def one_sequence(params, sequence, length):
    memory_rows, gain_table, w_three, projection_weight, w_first, w_second = params
    state = jnp.concatenate([memory_rows, sequence], axis=0)
    key_valid = jnp.concatenate([jnp.ones((M,), dtype=bool), jnp.arange(TLEN, dtype=jnp.int32) < length])
    state = residual_block(state, key_valid, gain_table[0], w_three[0], projection_weight[0], w_first[0], w_second[0], full_mixer)
    state = residual_block(state, key_valid, gain_table[1], w_three[1], projection_weight[1], w_first[1], w_second[1], bottleneck_mixer)
    return (state[:M], state[M:])

def reference(tokens, lengths, memory, norm_gain, w_qkv, output_weight, w_up, w_down, cot_tokens, cot_memory):
    params = tuple((argument.astype(jnp.float32) for argument in (memory, norm_gain, w_qkv, output_weight, w_up, w_down)))
    tokens_float = tokens.astype(jnp.float32)

    def forward(params_in, tokens_in):

        def per_sequence(entry_pair):
            return jax.checkpoint(one_sequence)(params_in, entry_pair[0], entry_pair[1])
        return lax.map(per_sequence, (tokens_in, lengths))
    (out_memory, out_tokens), pullback = jax.vjp(forward, params, tokens_float)
    live_rows = (jnp.arange(TLEN, dtype=jnp.int32)[None, :] < lengths[:, None]).astype(jnp.float32)
    grad_params, grad_tokens = pullback((cot_memory.astype(jnp.float32), cot_tokens.astype(jnp.float32) * live_rows[:, :, None]))
    gain_grads = grad_params[1]
    return (out_tokens.astype(jnp.bfloat16), out_memory.astype(jnp.bfloat16), grad_tokens, grad_params[0], gain_grads[:, 0], gain_grads[:, 1], grad_params[2], grad_params[3], grad_params[4], grad_params[5])
```

```python
import jax
import jax.numpy as jnp
from jax import lax
from jax.sharding import PartitionSpec as P

DH = 64
M = 20
EPS = 1e-05
BF = jnp.bfloat16
F32 = jnp.float32


def move_tensor(value, mask):
    return lax.ppermute(value, "tensor", [(i, i ^ mask) for i in range(4)])


def move_dp(value, mask):
    size = lax.axis_size("dp")
    return lax.ppermute(value, "dp", [(i, i ^ mask) for i in range(size)])


def gather_blocks(block):
    far = move_tensor(block, 2)
    return [block, move_tensor(block, 1), far, move_tensor(far, 1)]


def gather_weights(block):
    half = block.shape[0] // 2
    bit = lax.axis_index("dp") % 2
    first = move_tensor(lax.dynamic_slice_in_dim(block, bit * half, half, 0), 2)
    second = move_dp(first, 1)
    low = jnp.where(bit == 0, first, second)
    high = jnp.where(bit == 0, second, first)
    far = jnp.concatenate([low, high], axis=0)
    return [block, move_tensor(block, 1), far, move_tensor(far, 1)]


def scatter_blocks(blocks):
    sent = [b.astype(BF) for b in blocks]
    got = move_tensor(jnp.stack([sent[1], sent[3]]), 1)
    far = (sent[2].astype(F32) + got[1].astype(F32)).astype(BF)
    near = sent[0].astype(F32) + got[0].astype(F32)
    return near + move_tensor(far, 2).astype(F32)


def sum_dp(value):
    size = lax.axis_size("dp")
    if size & (size - 1) or value.shape[0] % size:
        return lax.psum(value, "dp")
    index = lax.axis_index("dp")
    masks = []
    mask = 1
    while mask < size:
        masks.append(mask)
        mask *= 2
    for mask in masks:
        half = value.shape[0] // 2
        bit = (index // mask) % 2
        kept = lax.dynamic_slice_in_dim(value, bit * half, half, 0)
        sent = lax.dynamic_slice_in_dim(value, (1 - bit) * half, half, 0).astype(BF)
        value = kept + move_dp(sent, mask).astype(F32)
    value = value.astype(BF)
    for mask in reversed(masks):
        bit = (index // mask) % 2
        other = move_dp(value, mask)
        value = jnp.concatenate(
            [jnp.where(bit == 0, value, other), jnp.where(bit == 0, other, value)], axis=0
        )
    return value.astype(F32)


def sum_all(value):
    size = lax.axis_size("dp")
    if size & (size - 1):
        return lax.psum(value, ("dp", "tensor"))
    for mask in (1, 2):
        value = value + move_tensor(value, mask)
    mask = 1
    while mask < size:
        value = value + move_dp(value, mask)
        mask *= 2
    return value


def normalize(state):
    center = jnp.mean(state, axis=-1, keepdims=True)
    spread = jnp.mean((state - center) ** 2, axis=-1, keepdims=True)
    inverse = lax.rsqrt(spread + EPS)
    return ((state - center) * inverse, inverse)


def norm_backward(state, gain_row, grad_normed):
    normed, inverse = normalize(state)
    scaled = grad_normed * gain_row
    grad_state = inverse * (
        scaled
        - jnp.mean(scaled, axis=-1, keepdims=True)
        - normed * jnp.mean(scaled * normed, axis=-1, keepdims=True)
    )
    return (grad_state, grad_normed * normed)


def dot32(spec, a, b):
    return jnp.einsum(spec, a, b, preferred_element_type=F32)


def softmax_parts(scores):
    highest = jnp.max(scores, axis=-1, keepdims=True)
    raised = jnp.exp(scores - highest)
    return (highest, jnp.sum(raised, axis=-1, keepdims=True), raised)


def full_attention(query, key, value, valid):
    scores = dot32("qhd,khd->hqk", query, key) * DH**-0.5
    scores = jnp.where(valid[None, None, :], scores, -1e30)
    highest, total, raised = softmax_parts(scores)
    log_total = highest + jnp.log(total)
    weights = jnp.exp(scores - log_total).astype(BF)
    return (dot32("hqk,khd->qhd", weights, value), log_total)


def attention_gradients(query, key, value, valid, log_total, delta, grad):
    scores = dot32("qhd,khd->hqk", query, key) * DH**-0.5
    scores = jnp.where(valid[None, None, :], scores, -1e30)
    weights = jnp.exp(scores - log_total)
    grad_value = dot32("hqk,qhd->khd", weights.astype(BF), grad)
    grad_weights = dot32("qhd,khd->hqk", grad, value)
    grad_scores = (weights * (grad_weights - delta)).astype(BF)
    grad_query = dot32("hqk,khd->qhd", grad_scores, key) * DH**-0.5
    grad_key = dot32("hqk,qhd->khd", grad_scores, query) * DH**-0.5
    return (grad_query, grad_key, grad_value)


def gelu_parts(hidden):
    c = 0.7978845608028654
    a = 0.044715
    square = hidden * hidden
    t = jnp.tanh(c * hidden * (1.0 + a * square))
    active = 0.5 * hidden * (1.0 + t)
    slope = 0.5 * (1.0 + t) + 0.5 * hidden * (1.0 - t * t) * (c * (1.0 + 3.0 * a * square))
    return (active, slope)


def on_device(
    tokens, lengths, memory, norm_gain, w_qkv, output_weight, w_up, w_down, cot_tokens, cot_memory
):
    slots, local, width = tokens.shape
    n_tok = slots * local
    n_mem = slots * M
    n_pad = -(n_tok + n_mem) % 16
    rows = n_tok + n_mem + n_pad
    heads = w_qkv.shape[-1] // DH
    me = lax.axis_index("tensor")
    gain = norm_gain.astype(F32)
    owner = (me == 0).astype(F32)
    starts = [(me ^ j) * local for j in range(4)]
    positions = jnp.concatenate(
        [s + jnp.arange(local, dtype=jnp.int32) for s in starts]
    )
    valid_tok = positions[None, :] < lengths[:, None]
    valid_all = jnp.concatenate([valid_tok, jnp.ones((slots, M), bool)], axis=1)
    share = n_mem // 4
    mem_row = jnp.arange(n_mem + n_pad, dtype=jnp.int32)
    mem_once = (mem_row >= me * share) & ((mem_row < (me + 1) * share) | (me == 3))
    once = jnp.concatenate([jnp.ones((n_tok,), bool), mem_once])[:, None]

    def count_once(value):
        return jnp.where(once, value, jnp.zeros_like(value))

    def with_memory(tok, mem):
        return jnp.concatenate(
            [tok.reshape(n_tok, -1), mem.reshape(n_mem, -1), jnp.zeros((n_pad, tok.shape[-1]), tok.dtype)]
        )

    tok_blocks = gather_blocks(tokens)
    pack = [
        jnp.concatenate([output_weight[l], w_up[l], w_down[l]], axis=0) for l in range(2)
    ]
    weights0 = gather_weights(pack[0])
    qkv1 = [b.reshape(3, width, -1) for b in gather_weights(w_qkv[1].reshape(3 * width, -1))]
    weights1 = gather_weights(pack[1])
    packed = []
    for blocks in (weights0, weights1):
        o = output_weight.shape[1]
        u = w_up.shape[1]
        packed.append(
            (
                jnp.concatenate([b[:o] for b in blocks], axis=0),
                jnp.concatenate([b[o : o + u] for b in blocks], axis=1),
                jnp.concatenate([b[o + u :] for b in blocks], axis=0),
            )
        )
    qkv1 = jnp.concatenate(qkv1, axis=2)

    state_mem = jnp.broadcast_to(memory.astype(F32)[None], (slots, M, width))
    full = jnp.concatenate(tok_blocks + [jnp.broadcast_to(memory[None], (slots, M, width))], axis=1)
    normed0, _ = normalize(full.astype(F32))
    normed0_low = (normed0 * gain[0, 0]).astype(BF)
    projected = dot32("snd,tde->stne", normed0_low, w_qkv[0]).astype(BF)
    projected = projected.reshape(slots, 3, -1, heads, DH)
    att, log0 = lax.map(
        lambda e: full_attention(e[0][0], e[0][1], e[0][2], e[1]), (projected, valid_all)
    )
    att = att.astype(BF)
    flat = att.reshape(slots, -1, heads * DH)
    att_tok = [flat[:, j * local : (j + 1) * local] for j in range(4)]
    att_mem = flat[:, 4 * local :]
    out_blocks = [
        jnp.concatenate([att_tok[j].reshape(n_tok, -1), att_mem.reshape(n_mem, -1)], axis=0)
        for j in range(4)
    ]

    def exchange(blocks):
        far = move_tensor(jnp.stack([blocks[2], blocks[3]]), 2)
        return [blocks[0], move_tensor(blocks[1], 1), far[0], move_tensor(far[1], 1)]

    mixed0 = jnp.concatenate(exchange(out_blocks), axis=1)
    mixed0 = jnp.concatenate([mixed0, jnp.zeros((n_pad, width), BF)])

    state0 = with_memory(tokens, jnp.broadcast_to(memory[None], (slots, M, width))).astype(F32)

    def forward_rest(state, mixed, layer):
        out_w, up, down = packed[layer]
        state = state + dot32("rk,kd->rd", mixed, out_w)
        normed, _ = normalize(state)
        normed = (normed * gain[layer, 1]).astype(BF)
        hidden = dot32("rd,df->rf", normed, up)
        active = gelu_parts(hidden)[0].astype(BF)
        return (state, state + dot32("rf,fd->rd", active, down))

    mid0, state1 = forward_rest(state0, mixed0, 0)

    all_heads = width // DH
    normed1 = (normalize(state1)[0] * gain[1, 0]).astype(BF)
    proj1 = dot32("rd,tde->tre", normed1, qkv1).astype(BF)
    tok1 = proj1[:, :n_tok].reshape(3, slots, local, all_heads, DH)
    mem1 = proj1[:, n_tok : n_tok + n_mem].reshape(3, slots, M, all_heads, DH)
    scale = DH**-0.5
    scores = dot32("sqhd,skhd->shqk", tok1[0], mem1[1]) * scale
    highest, total, raised = softmax_parts(scores)
    log_tok = highest + jnp.log(total)
    out_tok = dot32("shqk,skhd->sqhd", jnp.exp(scores - log_tok).astype(BF), mem1[2])
    own_valid = jnp.concatenate(
        [valid_tok[:, :local], jnp.broadcast_to(me == 0, (slots, M))], axis=1
    )
    keys1 = jnp.concatenate([tok1[1], mem1[1]], axis=1)
    vals1 = jnp.concatenate([tok1[2], mem1[2]], axis=1)
    scores_mem = dot32("sqhd,skhd->shqk", mem1[0], keys1) * scale
    scores_mem = jnp.where(own_valid[:, None, None, :], scores_mem, -1e30)
    top, total, raised = softmax_parts(scores_mem)
    raised = jnp.where(own_valid[:, None, None, :], raised, 0.0)
    total = jnp.sum(raised, axis=-1, keepdims=True)
    part = dot32("shqk,skhd->shqd", raised.astype(BF), vals1)
    swaps = {1: [1, 0, 3, 2], 2: [2, 3, 0, 1]}
    group = jnp.concatenate([part, top, total], axis=-1)
    for mask in (1, 2):
        other = move_tensor(group, mask)
        other = other.reshape(slots, 4, heads, M, -1)
        other = jnp.stack([other[:, j] for j in swaps[mask]], axis=1)
        other = other.reshape(group.shape)
        peak = jnp.maximum(group[..., DH : DH + 1], other[..., DH : DH + 1])
        w_a = jnp.exp(group[..., DH : DH + 1] - peak)
        w_b = jnp.exp(other[..., DH : DH + 1] - peak)
        merged = group * w_a + other * w_b
        group = jnp.concatenate([merged[..., :DH], peak, merged[..., DH + 1 :]], axis=-1)
    total = group[..., DH + 1 :]
    out_mem = group[..., :DH] / total
    log_mem = group[..., DH : DH + 1] + jnp.log(total)
    out_mem = jnp.swapaxes(out_mem, 1, 2)
    mixed1 = with_memory(out_tok.reshape(slots, local, width), out_mem.reshape(slots, M, width)).astype(BF)
    mid1, state2 = forward_rest(state1, mixed1, 1)

    live = (starts[0] + jnp.arange(local, dtype=jnp.int32))[None, :] < lengths[:, None]
    cot = jnp.where(live[:, :, None], cot_tokens, jnp.zeros_like(cot_tokens))
    grad2 = with_memory(cot, cot_memory).astype(F32)

    def ffn_back(grad, mid, layer):
        out_w, up, down = packed[layer]
        normed, _ = normalize(mid)
        normed = (normed * gain[layer, 1]).astype(BF)
        hidden = dot32("rd,df->rf", normed, up)
        active, slope = gelu_parts(hidden)
        low = grad.astype(BF)
        grad_down = dot32("rf,rd->fd", active.astype(BF), count_once(low))
        grad_hidden = (dot32("rd,fd->rf", low, down) * slope).astype(BF)
        grad_up = dot32("rd,rf->df", count_once(normed), grad_hidden)
        grad_normed = dot32("rf,df->rd", grad_hidden, up)
        back, gain_rows = norm_backward(mid, gain[layer, 1], grad_normed)
        return (grad + back, jnp.sum(count_once(gain_rows), axis=0), grad_up, grad_down)

    def pack_blocks(grad_out, grad_up, grad_down):
        o = output_weight.shape[1]
        f = w_up.shape[2]
        return [
            jnp.concatenate(
                [
                    grad_out[j * o : (j + 1) * o],
                    grad_up[:, j * f : (j + 1) * f],
                    grad_down[j * f : (j + 1) * f],
                ],
                axis=0,
            )
            for j in range(4)
        ]

    grad_mid1, gain_f1, grad_up1, grad_down1 = ffn_back(grad2, mid1, 1)
    low = grad_mid1.astype(BF)
    grad_out1 = dot32("ra,rd->ad", mixed1, count_once(low))
    grad_mixed = dot32("rd,ad->ra", low, packed[1][0]).astype(BF)
    gm_tok = grad_mixed[:n_tok].reshape(slots, local, all_heads, DH)
    gm_mem = grad_mixed[n_tok : n_tok + n_mem].reshape(slots, M, all_heads, DH)
    weights = jnp.exp(scores - log_tok)
    gv_mem = dot32("shqk,sqhd->skhd", weights.astype(BF), gm_tok)
    gw = dot32("sqhd,skhd->shqk", gm_tok, mem1[2])
    gs = (weights * (gw - jnp.sum(weights * gw, axis=-1, keepdims=True))).astype(BF)
    gq_tok = dot32("shqk,skhd->sqhd", gs, mem1[1]) * scale
    gk_mem = dot32("shqk,sqhd->skhd", gs, tok1[0]) * scale
    weights = jnp.where(own_valid[:, None, None, :], jnp.exp(scores_mem - log_mem), 0.0)
    delta = jnp.sum(out_mem * gm_mem.astype(F32), axis=-1)
    delta = jnp.swapaxes(delta, 1, 2)[..., None]
    gv = dot32("shqk,sqhd->skhd", weights.astype(BF), gm_mem)
    gw = dot32("sqhd,skhd->shqk", gm_mem, vals1)
    gs = (weights * (gw - delta)).astype(BF)
    gq_mem = dot32("shqk,skhd->sqhd", gs, keys1) * scale
    gk = dot32("shqk,sqhd->skhd", gs, mem1[0]) * scale
    grads_tok = [gq_tok, gk[:, :local], gv[:, :local]]
    grads_mem = [gq_mem, gk_mem + gk[:, local:], gv_mem + gv[:, local:]]
    grad_proj = jnp.stack(
        [
            with_memory(a.reshape(slots, local, width), b.reshape(slots, M, width))
            for a, b in zip(grads_tok, grads_mem)
        ]
    ).astype(BF)
    grad_qkv1 = dot32("rd,tre->tde", normed1, grad_proj)
    grad_normed = dot32("tre,tde->rd", grad_proj, qkv1)
    part_mem = grad_normed[n_tok:]
    for mask in (1, 2):
        part_mem = part_mem + move_tensor(part_mem, mask)
    grad_normed = jnp.concatenate([grad_normed[:n_tok], part_mem])
    back, gain_rows = norm_backward(state1, gain[1, 0], grad_normed)
    gain_a1 = jnp.sum(count_once(gain_rows), axis=0)
    grad1 = grad_mid1 + back

    sum1 = scatter_blocks(pack_blocks(grad_out1, grad_up1, grad_down1))
    sum1 = sum_dp(sum1)
    e = w_qkv.shape[-1]
    sum1q = scatter_blocks([grad_qkv1[:, :, j * e : (j + 1) * e].reshape(-1, e) for j in range(4)])
    sum1q = sum_dp(sum1q)

    grad_mid0, gain_f0, grad_up0, grad_down0 = ffn_back(grad1, mid0, 0)
    low = grad_mid0.astype(BF)
    grad_out0 = dot32("ra,rd->ad", mixed0, count_once(low))
    grad_mixed = dot32("rd,ad->ra", low, packed[0][0]).astype(BF)
    gm_blocks = [grad_mixed[:n_tok, j * e : (j + 1) * e].reshape(slots, local, e) for j in range(4)]
    gm_tok = exchange(gm_blocks)
    gm_mem = grad_mixed[n_tok : n_tok + n_mem, :e].reshape(slots, M, e)
    gm = jnp.concatenate(gm_tok + [gm_mem], axis=1).reshape(slots, -1, heads, DH)
    sum0 = scatter_blocks(pack_blocks(grad_out0, grad_up0, grad_down0))
    sum0 = sum_dp(sum0)

    delta = jnp.sum(gm.astype(F32) * att.astype(F32), axis=-1)
    delta = jnp.swapaxes(delta, 1, 2)[..., None]

    def back_one(entry):
        proj, valid, log_total, delta_one, grad = entry
        grads = attention_gradients(proj[0], proj[1], proj[2], valid, log_total, delta_one, grad)
        return jnp.stack(grads).astype(BF)

    grad_proj = lax.map(back_one, (projected, valid_all, log0, delta, gm))
    grad_proj = grad_proj.reshape(slots, 3, -1, e)
    grad_qkv0 = dot32("snd,stne->tde", normed0_low, grad_proj)
    grad_normed = dot32("stne,tde->snd", grad_proj, w_qkv[0])
    gain_a0 = jnp.sum(grad_normed * normed0, axis=(0, 1))
    mem_normed = jnp.sum(grad_normed[:, 4 * local :], axis=0)
    sum0q = sum_dp(grad_qkv0.reshape(-1, e))
    tok_normed = scatter_blocks(
        [grad_normed[:, j * local : (j + 1) * local] for j in range(4)]
    )
    back, _ = norm_backward(tokens.astype(F32), gain[0, 0], tok_normed)
    grad_tokens = grad_mid0[:n_tok].reshape(slots, local, width) + back
    mem_direct = jnp.sum(grad_mid0[n_tok : n_tok + n_mem].reshape(slots, M, width), axis=0) * owner

    small = jnp.concatenate(
        [mem_normed, mem_direct, jnp.stack([gain_a0, gain_a1, gain_f0, gain_f1])], axis=0
    )
    small = sum_all(small)
    back, _ = norm_backward(memory.astype(F32), gain[0, 0], small[:M])
    grad_memory = small[M : 2 * M] + back
    gains = small[2 * M :]

    out_mem = state2[n_tok : n_tok + n_mem].astype(BF)
    out_mem = jnp.where(me % 2 == 0, out_mem, move_tensor(out_mem, 1))
    out_mem = jnp.where(me // 2 == 0, out_mem, move_tensor(out_mem, 2))

    o = output_weight.shape[1]
    u = w_up.shape[1]
    return (
        state2[:n_tok].reshape(slots, local, width).astype(BF),
        out_mem.reshape(slots, M, width),
        grad_tokens,
        grad_memory,
        gains[0:2],
        gains[2:4],
        jnp.stack([sum0q.reshape(3, width, e), sum1q.reshape(3, width, e)]),
        jnp.stack([sum0[:o], sum1[:o]]),
        jnp.stack([sum0[o : o + u], sum1[o : o + u]]),
        jnp.stack([sum0[o + u :], sum1[o + u :]]),
    )


def solution(mesh):
    return jax.shard_map(
        on_device,
        mesh=mesh,
        in_specs=(
            P("dp", "tensor", None),
            P("dp"),
            P(),
            P(),
            P(None, None, None, "tensor"),
            P(None, "tensor", None),
            P(None, None, "tensor"),
            P(None, "tensor", None),
            P("dp", "tensor", None),
            P("dp", None, None),
        ),
        out_specs=(
            P("dp", "tensor", None),
            P("dp", None, None),
            P("dp", "tensor", None),
            P(),
            P(),
            P(),
            P(None, None, None, "tensor"),
            P(None, "tensor", None),
            P(None, None, "tensor"),
            P(None, "tensor", None),
        ),
        check_vma=False,
    )
```

```python
import functools

import jax
import jax.numpy as jnp
from jax import lax
from jax.experimental import pallas as pl
from jax.experimental.pallas import tpu as pltpu
from jax.sharding import PartitionSpec as P

DH = 64
M = 20
SEG = 32
HW = 2 * DH
EPS = 1e-05
SCALE = DH**-0.5
FAR = -1e30
BF = jnp.bfloat16
F32 = jnp.float32


def move_tensor(value, mask):
    return lax.ppermute(value, "tensor", [(i, i ^ mask) for i in range(4)])


def move_dp(value, mask):
    size = lax.axis_size("dp")
    return lax.ppermute(value, "dp", [(i, i ^ mask) for i in range(size)])


def gather_blocks(block):
    far = move_tensor(block, 2)
    return [block, move_tensor(block, 1), far, move_tensor(far, 1)]


def gather_weights(block):
    half = block.shape[0] // 2
    bit = lax.axis_index("dp") % 2
    first = move_tensor(lax.dynamic_slice_in_dim(block, bit * half, half, 0), 2)
    second = move_dp(first, 1)
    low = jnp.where(bit == 0, first, second)
    high = jnp.where(bit == 0, second, first)
    far = jnp.concatenate([low, high], axis=0)
    return [block, move_tensor(block, 1), far, move_tensor(far, 1)]


def scatter_blocks(kept, sent):
    got = move_tensor(sent, 1)
    far = (kept[1].astype(F32) + got[1].astype(F32)).astype(BF)
    near = kept[0].astype(F32) + got[0].astype(F32)
    return near + move_tensor(far, 2).astype(F32)


def sum_dp(value):
    size = lax.axis_size("dp")
    if size & (size - 1) or value.shape[0] % size:
        return lax.psum(value, "dp")
    index = lax.axis_index("dp")
    masks = []
    mask = 1
    while mask < size:
        masks.append(mask)
        mask *= 2
    for mask in masks:
        half = value.shape[0] // 2
        bit = (index // mask) % 2
        kept = lax.dynamic_slice_in_dim(value, bit * half, half, 0)
        sent = lax.dynamic_slice_in_dim(value, (1 - bit) * half, half, 0).astype(BF)
        value = kept + move_dp(sent, mask).astype(F32)
    value = value.astype(BF)
    for mask in reversed(masks):
        bit = (index // mask) % 2
        other = move_dp(value, mask)
        value = jnp.concatenate(
            [jnp.where(bit == 0, value, other), jnp.where(bit == 0, other, value)], axis=0
        )
    return value.astype(F32)


def sum_all(value):
    size = lax.axis_size("dp")
    if size & (size - 1):
        return lax.psum(value, ("dp", "tensor"))
    for mask in (1, 2):
        value = value + move_tensor(value, mask)
    mask = 1
    while mask < size:
        value = value + move_dp(value, mask)
        mask *= 2
    return value


def nn(a, b):
    return lax.dot_general(a, b, (((1,), (0,)), ((), ())), preferred_element_type=F32)


def nt(a, b):
    return lax.dot_general(a, b, (((1,), (1,)), ((), ())), preferred_element_type=F32)


def tn(a, b):
    return lax.dot_general(a, b, (((0,), (0,)), ((), ())), preferred_element_type=F32)


def normalize(state):
    center = jnp.mean(state, axis=-1, keepdims=True)
    shifted = state - center
    spread = jnp.mean(shifted * shifted, axis=-1, keepdims=True)
    inverse = lax.rsqrt(spread + EPS)
    return (shifted * inverse, inverse)


def norm_backward(normed, inverse, gain_row, grad_normed):
    scaled = grad_normed * gain_row
    return inverse * (
        scaled
        - jnp.mean(scaled, axis=-1, keepdims=True)
        - normed * jnp.mean(scaled * normed, axis=-1, keepdims=True)
    )


def gelu_parts(hidden, with_slope):
    c = 0.7978845608028654
    a = 0.044715
    square = hidden * hidden
    t = jnp.tanh(hidden * (c + (c * a) * square))
    up = 0.5 + 0.5 * t
    active = hidden * up
    if not with_slope:
        return active
    slope = up + hidden * (0.5 - 0.5 * t * t) * (c + (3.0 * c * a) * square)
    return (active, slope)


def iota(shape, axis):
    return lax.broadcasted_iota(jnp.int32, shape, axis)


def call(kernel, out_shape, cost, *operands, scratch=(), name=None):
    specs = [
        pl.BlockSpec(memory_space=pltpu.SMEM if o.dtype == jnp.int32 else pltpu.VMEM)
        for o in operands
    ]
    moved = sum(o.size * o.dtype.itemsize for o in operands)
    moved += sum(o.size * o.dtype.itemsize for o in jax.tree.leaves(out_shape))
    return pl.pallas_call(
        kernel,
        out_shape=out_shape,
        in_specs=specs,
        out_specs=jax.tree.map(lambda _: pl.BlockSpec(memory_space=pltpu.VMEM), out_shape),
        scratch_shapes=list(scratch),
        compiler_params=pltpu.CompilerParams(vmem_limit_bytes=58 * 1024 * 1024),
        cost_estimate=pl.CostEstimate(flops=cost, bytes_accessed=moved, transcendentals=0),
        name=name,
    )(*operands)


def like(*shape, dtype=BF):
    return jax.ShapeDtypeStruct(shape, dtype)


def head_lanes(rows, h):
    lane = iota((rows, HW), 1)
    inside = (lane >= h * DH) & (lane < (h + 1) * DH)
    return lane - (1 - h) * DH, inside


def attention0_kernel(
    local, valid_ref, x0, x1, x2, x3, mem, gain, w, own, near, far, qa, ka, va, vt, pt, q_s
):
    keys = 4 * local + SEG
    tokens = [x0, x1, x2, x3]
    blocks = [(j * local, local, tokens[j]) for j in range(4)] + [(4 * local, SEG, mem)]
    for j, (start, size, ref) in enumerate(blocks):
        normed, _ = normalize(ref[...].astype(F32))
        normed = (normed * gain[...]).astype(BF)
        proj = nn(normed, w[...]).astype(BF)
        q = proj[:, :HW] * jnp.asarray(SCALE, BF)
        k = proj[:, HW : 2 * HW]
        v = proj[:, 2 * HW :]
        at = pl.ds(start, size)
        q_s[at, :] = q
        va[at, :] = v
        row = iota((size, HW), 0)
        valid = row < (valid_ref[j] if j < 4 else M)
        bias = jnp.where(valid, 0.0, FAR).astype(BF)
        for h in range(2):
            spare, inside = head_lanes(size, h)
            extra = jnp.where(spare == 0, bias, jnp.where((spare >= 1) & (spare <= 3), 1.0, 0.0).astype(BF))
            ka[h, at, :] = jnp.where(inside, k, extra)
    pad = q_s.shape[0] - keys
    q_s[pl.ds(keys, pad), :] = jnp.zeros((pad, HW), BF)
    pt[:, pl.ds(keys, pad), :] = jnp.zeros((2, pad, pt.shape[2]), BF)
    vt[:, pl.ds(0, keys)] = va[...].astype(F32).T.astype(BF)
    vt[:, pl.ds(keys, pad)] = jnp.zeros((HW, pad), BF)

    def chunk(start, size):
        at = pl.ds(start, size)
        outs, logs, qs = [], [], []
        for h in range(2):
            spare, inside = head_lanes(size, h)
            q = jnp.where(inside, q_s[at, :], jnp.where(spare == 0, 1.0, 0.0).astype(BF))
            qs.append(q)
            st = nt(ka[h], q)
            top = jnp.max(st, axis=0, keepdims=True)
            p = jnp.exp(st - top)
            total = jnp.sum(p, axis=0, keepdims=True)
            pt[h, pl.ds(0, keys), pl.ds(0, size)] = p.astype(BF)
            o = nn(vt[pl.ds(h * DH, DH), :], pt[h, :, pl.ds(0, size)])
            outs.append(o / total)
            logs.append(jnp.broadcast_to(top + jnp.log(total), (DH, size)))
        out = jnp.concatenate(outs, axis=0).T.astype(BF)
        log = jnp.concatenate(logs, axis=0).T
        for h in range(2):
            spare, inside = head_lanes(size, h)
            col = -log[:, h * DH : h * DH + 1]
            hi = col.astype(BF).astype(F32)
            mid = (col - hi).astype(BF).astype(F32)
            low = col - hi - mid
            extra = jnp.where(spare == 1, hi, jnp.where(spare == 2, mid, jnp.where(spare == 3, low, 0.0)))
            qa[h, at, :] = jnp.where(inside | (spare == 0), qs[h], extra.astype(BF))
        return out

    for j in range(4):
        out = chunk(j * local, local)
        target = [own, near, far.at[0], far.at[1]][j]
        target[pl.ds(0, local), :] = out
    out = chunk(4 * local, HW)[:SEG]
    for target in (own, near, far.at[0], far.at[1]):
        target[pl.ds(local, SEG), :] = out


def attention0(valid, blocks, mem, gain, w):
    local, width = blocks[0].shape
    keys = 4 * local + SEG
    queries = 4 * local + HW
    piece = local + SEG
    cost = 2 * keys * width * 3 * HW + 8 * keys * keys * HW
    return call(
        functools.partial(attention0_kernel, local),
        (
            like(piece, HW),
            like(piece, HW),
            like(2, piece, HW),
            like(2, queries, HW),
            like(2, keys, HW),
            like(keys, HW),
        ),
        cost,
        valid,
        *blocks,
        mem,
        gain,
        w,
        scratch=[
            pltpu.VMEM((HW, queries), BF),
            pltpu.VMEM((2, queries, max(local, HW)), BF),
            pltpu.VMEM((queries, HW), BF),
        ],
        name="attention0",
    )


def attention0_back_kernel(
    local, x0, x1, x2, x3, mem, gain, w, qa, ka, va,
    o_own, o_near, o_far, g_own, g_near, g_far,
    kept, sent, grad_w, mem_normed, gain_sum,
    grads, va_s, da_s, d_s, kt, ds_s, acc_v, acc_k,
):
    keys = 4 * local + SEG
    queries = 4 * local + HW
    pad = queries - keys
    pieces = [
        (0, local, g_own, o_own, 0),
        (local, local, g_near, o_near, 0),
        (2 * local, local, g_far.at[0], o_far.at[0], 0),
        (3 * local, local, g_far.at[1], o_far.at[1], 0),
        (4 * local, SEG, g_own, o_own, local),
    ]
    d_s[pl.ds(keys, pad), :] = jnp.zeros((pad, HW), BF)
    da_s[:, pl.ds(keys, pad), :] = jnp.zeros((2, pad, HW), BF)
    ds_s[:, pl.ds(keys, pad), :] = jnp.zeros((2, pad, ds_s.shape[2]), BF)
    for start, size, g, o, offset in pieces:
        at = pl.ds(start, size)
        grad = g[pl.ds(offset, size), :]
        product = grad.astype(F32) * o[pl.ds(offset, size), :].astype(F32)
        d_s[at, :] = grad
        for h in range(2):
            spare, inside = head_lanes(size, h)
            col = -jnp.sum(jnp.where(inside, product, 0.0), axis=-1, keepdims=True)
            hi = col.astype(BF).astype(F32)
            extra = jnp.where(spare == 0, hi, jnp.where(spare == 1, col - hi, 0.0))
            da_s[h, at, :] = jnp.where(inside, grad, extra.astype(BF))
    for h in range(2):
        spare, inside = head_lanes(keys, h)
        ones = jnp.where((spare == 0) | (spare == 1), 1.0, 0.0).astype(BF)
        va_s[h] = jnp.where(inside, va[...], ones)
    first = iota((keys, HW), 1) < DH
    kt[:, pl.ds(0, keys)] = jnp.where(first, ka[0], ka[1]).astype(F32).T.astype(BF)
    kt[:, pl.ds(keys, pad)] = jnp.zeros((HW, pad), BF)

    def chunk(start, size, fresh):
        at = pl.ds(start, size)
        turned = []
        for h in range(2):
            p = jnp.exp(nt(ka[h], qa[h, at, :]))
            dp = nt(va_s[h], da_s[h, at, :])
            ds = (p * dp).astype(BF)
            ds_s[h, pl.ds(0, keys), pl.ds(0, size)] = ds
            add_v = nn(p.astype(BF), d_s[at, :])
            add_k = nn(ds, qa[h, at, :])
            if fresh:
                acc_v[h] = add_v
                acc_k[h] = add_k
            else:
                acc_v[h] += add_v
                acc_k[h] += add_k
            turned.append(nn(kt[pl.ds(h * DH, DH), :], ds_s[h, :, pl.ds(0, size)]))
        dq = jnp.concatenate(turned, axis=0).T * SCALE
        return dq.astype(BF)

    for j in range(4):
        grads[pl.ds(j * local, local), :HW] = chunk(j * local, local, j == 0)
    grads[pl.ds(4 * local, SEG), :HW] = chunk(4 * local, HW, False)[:SEG]
    grads[:, HW : 2 * HW] = jnp.where(first, acc_k[0], acc_k[1]).astype(BF)
    grads[:, 2 * HW :] = jnp.where(first, acc_v[0], acc_v[1]).astype(BF)

    tokens = [x0, x1, x2, x3]
    total_w = None
    total_gain = None
    for j in range(5):
        size = local if j < 4 else SEG
        ref = tokens[j] if j < 4 else mem
        normed, _ = normalize(ref[...].astype(F32))
        low = (normed * gain[...]).astype(BF)
        part = grads[pl.ds(j * local, size), :]
        add_w = tn(low, part)
        grad_normed = nt(part, w[...])
        add_gain = jnp.sum(grad_normed * normed, axis=0, keepdims=True)
        total_w = add_w if j == 0 else total_w + add_w
        total_gain = add_gain if j == 0 else total_gain + add_gain
        if j == 4:
            mem_normed[...] = grad_normed
        else:
            target = [kept.at[0], sent.at[0], kept.at[1], sent.at[1]][j]
            target[...] = grad_normed.astype(BF)
    grad_w[...] = total_w
    gain_sum[...] = total_gain


def attention0_back(blocks, mem, gain, w, saved, outs, grads):
    local, width = blocks[0].shape
    keys = 4 * local + SEG
    queries = 4 * local + HW
    cost = 4 * keys * width * 3 * HW + 20 * keys * keys * HW
    return call(
        functools.partial(attention0_back_kernel, local),
        (
            like(2, local, width),
            like(2, local, width),
            like(width, 3 * HW, dtype=F32),
            like(SEG, width, dtype=F32),
            like(1, width, dtype=F32),
        ),
        cost,
        *blocks,
        mem,
        gain,
        w,
        *saved,
        *outs,
        *grads,
        scratch=[
            pltpu.VMEM((keys, 3 * HW), BF),
            pltpu.VMEM((2, keys, HW), BF),
            pltpu.VMEM((2, queries, HW), BF),
            pltpu.VMEM((queries, HW), BF),
            pltpu.VMEM((HW, queries), BF),
            pltpu.VMEM((2, queries, max(local, HW)), BF),
            pltpu.VMEM((2, keys, HW), F32),
            pltpu.VMEM((2, keys, HW), F32),
        ],
        name="attention0_back",
    )


def ffn0_kernel(slots, local, tokens, mem, gain, *refs):
    mixed_in, weights = refs[: 4 * slots], refs[4 * slots : 4 * slots + 4]
    mid, end, hid, mixed, normed_s = refs[4 * slots + 4 :]
    piece = local + SEG
    for s in range(slots):
        for j in range(4):
            mixed[pl.ds(s * piece, piece), pl.ds(j * HW, HW)] = mixed_in[4 * s + j][...]
        at = pl.ds(s * piece, piece)
        state = jnp.concatenate([tokens[s], mem[...]], axis=0).astype(F32)
        for j in range(4):
            state += nn(mixed_in[4 * s + j][...], weights[j][pl.ds(0, HW), :])
        mid[at, :] = state
        end[at, :] = state
        normed_s[at, :] = (normalize(state)[0] * gain[...]).astype(BF)
    width = gain.shape[1]
    inner = (weights[0].shape[0] - HW - width)
    for j in range(4):
        hidden = nn(normed_s[...], weights[j][pl.ds(HW, width), :])
        hid[j] = hidden.astype(BF)
        active = gelu_parts(hidden, False).astype(BF)
        end[...] += nn(active, weights[j][pl.ds(HW + width, inner), :])


def ffn0(tokens, mem, gain, mixed, weights):
    slots, local, width = tokens.shape
    rows = slots * (local + SEG)
    inner = weights[0].shape[0] - HW - width
    return call(
        functools.partial(ffn0_kernel, slots, local),
        (
            like(rows, width, dtype=F32),
            like(rows, width, dtype=F32),
            like(4, rows, inner),
            like(rows, width),
        ),
        2 * rows * width * (width + 8 * inner),
        tokens,
        mem,
        gain,
        *mixed,
        *weights,
        scratch=[pltpu.VMEM((rows, width), BF)],
        name="ffn0",
    )


def ffn_back_core(
    weights, low, low_once, hidden_of, normed, normed_once, kept, sent, with_output
):
    width = normed.shape[1]
    inner = weights[0].shape[0] - HW - width
    total, output = None, None
    for j in range(4):
        up = weights[j][pl.ds(HW, width), :]
        down = weights[j][pl.ds(HW + width, inner), :]
        active, slope = gelu_parts(hidden_of(j), True)
        active = active.astype(BF)
        if with_output:
            add = nn(active, down)
            output = add if j == 0 else output + add
        grad_hidden = (nt(low, down) * slope).astype(BF)
        target = (kept if j % 2 == 0 else sent).at[j // 2]
        target[pl.ds(HW, width), :] = tn(normed_once, grad_hidden).astype(BF)
        target[pl.ds(HW + width, inner), :] = tn(active, low_once).astype(BF)
        add = nt(grad_hidden, up)
        total = add if j == 0 else total + add
    return (total, output)


def once_rows(share_ref, slots, local, value):
    piece = local + SEG
    parts = []
    for s in range(slots):
        parts.append(value[s * piece : s * piece + local])
        tail = value[s * piece + local : (s + 1) * piece]
        parts.append(jnp.where(share_ref[s] > 0, tail, jnp.zeros_like(tail)))
    return jnp.concatenate(parts, axis=0)


def ffn1_kernel(slots, local, share_ref, live_ref, gain, state, out_tok, cot, cot_mem, *refs):
    parts, weights = refs[:4], refs[4:8]
    (res_tok, res_mem, kept, sent, grad_mid, gain_sum, mixed, logs) = refs[8:16]
    normed_s, end_s, low_s = refs[16:]
    piece = local + SEG
    width = gain.shape[1]
    rows = slots * piece
    inner = weights[0].shape[0] - HW - width
    heads = width // DH
    lane = iota((SEG, HW), 1)
    for s in range(slots):
        seg = pl.ds(s * SEG, SEG)
        scale = {}
        log = jnp.zeros((SEG, HW), F32)
        for h in range(heads):
            source = [2 * ((h // 2) ^ j) + h % 2 for j in range(4)]
            tops = [parts[j][seg, pl.ds(width, HW)][:, source[j] : source[j] + 1] for j in range(4)]
            sums = [
                parts[j][seg, pl.ds(width, HW)][:, heads + source[j] : heads + source[j] + 1]
                for j in range(4)
            ]
            peak = functools.reduce(jnp.maximum, tops)
            raised = [jnp.exp(t - peak) for t in tops]
            total = functools.reduce(jnp.add, [r * t for r, t in zip(raised, sums)])
            scale[h] = [r / total for r in raised]
            log = jnp.where(lane == h, peak + jnp.log(total), log)
        logs[seg, :] = log
        for b in range(4):
            merged = jnp.zeros((SEG, HW), F32)
            for j in range(4):
                factor = jnp.where(lane < DH, scale[2 * b][j], scale[2 * b + 1][j])
                merged += factor * parts[j][seg, pl.ds((b ^ j) * HW, HW)]
            mixed[pl.ds(s * piece + local, SEG), pl.ds(b * HW, HW)] = merged.astype(BF)
        at = pl.ds(s * piece, local)
        mixed[at, :] = out_tok[s]
        live = iota((local, 1), 0) < live_ref[s]
        low_s[at, :] = jnp.where(live, cot[s], jnp.zeros_like(cot[s]))
        low_s[pl.ds(s * piece + local, SEG), :] = cot_mem[s]
    mid = state[...]
    for j in range(4):
        mid += nn(mixed[:, pl.ds(j * HW, HW)], weights[j][pl.ds(0, HW), :])
    end_s[...] = mid
    mid_normed, inverse = normalize(mid)
    normed = (mid_normed * gain[...]).astype(BF)
    normed_s[...] = mid_normed
    low = low_s[...]

    grad_normed, output = ffn_back_core(
        weights,
        low,
        once_rows(share_ref, slots, local, low),
        lambda j: nn(normed, weights[j][pl.ds(HW, width), :]),
        normed,
        once_rows(share_ref, slots, local, normed),
        kept,
        sent,
        True,
    )
    end_s[...] += output
    mid_normed = normed_s[...]
    gain_sum[...] = jnp.sum(
        once_rows(share_ref, slots, local, grad_normed * mid_normed), axis=0, keepdims=True
    )
    grad_mid[...] = low_s[...].astype(F32) + norm_backward(
        mid_normed, inverse, gain[...], grad_normed
    )
    for s in range(slots):
        res_tok[s] = end_s[pl.ds(s * piece, local), :].astype(BF)
        res_mem[s] = end_s[pl.ds(s * piece + local, SEG), :].astype(BF)


def ffn1(share, live, gain, state, out_tok, cot, cot_mem, parts, weights):
    slots, local, width = cot.shape
    rows = slots * (local + SEG)
    inner = weights[0].shape[0] - HW - width
    return call(
        functools.partial(ffn1_kernel, slots, local),
        (
            like(slots, local, width),
            like(slots, SEG, width),
            like(2, HW + width + inner, width),
            like(2, HW + width + inner, width),
            like(rows, width, dtype=F32),
            like(1, width, dtype=F32),
            like(rows, width),
            like(slots * SEG, HW, dtype=F32),
        ),
        2 * rows * width * (width + 24 * inner),
        share,
        live,
        gain,
        state,
        out_tok,
        cot,
        cot_mem,
        *parts,
        *weights,
        scratch=[
            pltpu.VMEM((rows, width), F32),
            pltpu.VMEM((rows, width), F32),
            pltpu.VMEM((rows, width), BF),
        ],
        name="ffn1",
    )


def ffn0_back_kernel(
    slots, local, share_ref, gain, gain_attn, grad_in, mem_grad, state, mid, hid, mixed, *refs
):
    weights = refs[:4]
    kept, sent, grad_tok, grad_mem, gain_sum, d_own, d_near, d_far, low_s, grad_s = refs[4:]
    piece = local + SEG
    width = gain.shape[1]
    rows = slots * piece
    inner = weights[0].shape[0] - HW - width
    grad_s[...] = grad_in[...]
    for s in range(slots):
        at = pl.ds(s * piece + local, SEG)
        normed, inverse = normalize(state[at, :])
        grad_s[at, :] = grad_in[at, :] + norm_backward(
            normed, inverse, gain_attn[...], mem_grad[pl.ds(s * SEG, SEG), :]
        )
    low_s[...] = grad_s[...].astype(BF)
    low = low_s[...]
    mid_normed, inverse = normalize(mid[...])
    normed = (mid_normed * gain[...]).astype(BF)
    grad_normed, _ = ffn_back_core(
        weights,
        low,
        once_rows(share_ref, slots, local, low),
        lambda j: hid[j].astype(F32),
        normed,
        once_rows(share_ref, slots, local, normed),
        kept,
        sent,
        False,
    )
    mid_normed, inverse = normalize(mid[...])
    gain_sum[...] = jnp.sum(
        once_rows(share_ref, slots, local, grad_normed * mid_normed), axis=0, keepdims=True
    )
    grad = grad_s[...] + norm_backward(mid_normed, inverse, gain[...], grad_normed)
    total = jnp.zeros((SEG, width), F32)
    for s in range(slots):
        grad_tok[s] = grad[s * piece : s * piece + local]
        total += grad[s * piece + local : (s + 1) * piece]
    grad_mem[...] = total
    low_s[...] = grad.astype(BF)
    low = low_s[...]
    grad_out = tn(mixed[...], once_rows(share_ref, slots, local, low))
    for j in range(4):
        target = (kept if j % 2 == 0 else sent).at[j // 2]
        target[pl.ds(0, HW), :] = grad_out[j * HW : (j + 1) * HW].astype(BF)
        back = nt(low, weights[j][pl.ds(0, HW), :]).astype(BF)
        for s in range(slots):
            if j == 0:
                d_own[s] = back[s * piece : (s + 1) * piece]
            elif j == 1:
                d_near[s] = back[s * piece : s * piece + local]
            else:
                d_far[s, j - 2] = back[s * piece : s * piece + local]


def ffn0_back(slots, local, share, gain, gain_attn, grad_in, mem_grad, state, mid, hid, mixed, weights):
    rows, width = grad_in.shape
    inner = weights[0].shape[0] - HW - width
    return call(
        functools.partial(ffn0_back_kernel, slots, local),
        (
            like(2, HW + width + inner, width),
            like(2, HW + width + inner, width),
            like(slots, local, width, dtype=F32),
            like(SEG, width, dtype=F32),
            like(1, width, dtype=F32),
            like(slots, local + SEG, HW),
            like(slots, local, HW),
            like(slots, 2, local, HW),
        ),
        2 * rows * width * (2 * width + 16 * inner),
        share,
        gain,
        gain_attn,
        grad_in,
        mem_grad,
        state,
        mid,
        hid,
        mixed,
        *weights,
        scratch=[pltpu.VMEM((rows, width), BF), pltpu.VMEM((rows, width), F32)],
        name="ffn0_back",
    )


def spread_heads(target, value):
    size, width = value.shape
    lane = iota((size, width), 1) // DH
    for h in range(width // DH):
        target[pl.ds(h * size, size), :] = jnp.where(lane == h, value, jnp.zeros_like(value))


def fold_heads(value, size):
    width = value.shape[1]
    lane = iota((size, width), 1) // DH
    total = jnp.zeros((size, width), value.dtype)
    for h in range(width // DH):
        total += jnp.where(lane == h, value[h * size : (h + 1) * size], 0.0)
    return total


def memory_valid(local, rows, live, owner):
    lane = iota((rows, local + SEG), 1)
    return (lane < live) | ((lane >= local) & (lane < local + M) & (owner > 0))


def attention1_kernel(slots, local, live_ref, owner_ref, state, gain, *refs):
    w = refs[:4]
    q_o, k_o, v_o, probs, out_tok, part, spread_k, spread_v = refs[4:]
    piece = local + SEG
    width = gain.shape[1]
    heads = width // DH
    normed = (normalize(state[...])[0] * gain[...]).astype(BF)
    for j in range(4):
        proj = nn(normed, w[j][...]).astype(BF)
        lanes = pl.ds(j * HW, HW)
        q_o[:, lanes] = proj[:, :HW] * jnp.asarray(SCALE, BF)
        k_o[:, lanes] = proj[:, HW : 2 * HW]
        v_o[:, lanes] = proj[:, 2 * HW :]
    for s in range(slots):
        tok = pl.ds(s * piece, local)
        seg = pl.ds(s * piece + local, SEG)
        both = pl.ds(s * piece, piece)
        spread_heads(spread_k, k_o[seg, :])
        spread_heads(spread_v, v_o[seg, :])
        st = nt(spread_k[...], q_o[tok, :])
        st = jnp.where(iota((heads * SEG, local), 0) % SEG < M, st, FAR)
        st = st.reshape(heads, SEG, local)
        p = jnp.exp(st - jnp.max(st, axis=1, keepdims=True))
        p = p / jnp.sum(p, axis=1, keepdims=True)
        p = p.reshape(heads * SEG, local).T
        probs[s] = p
        out_tok[s] = nn(p.astype(BF), spread_v[...]).astype(BF)
        spread_heads(spread_k, q_o[seg, :])
        scores = nt(spread_k[...], k_o[both, :])
        valid = memory_valid(local, heads * SEG, live_ref[s], owner_ref[0])
        scores = jnp.where(valid, scores, FAR)
        top = jnp.max(scores, axis=1, keepdims=True)
        p = jnp.where(valid, jnp.exp(scores - top), 0.0)
        total = jnp.sum(p, axis=1, keepdims=True)
        here = pl.ds(s * SEG, SEG)
        part[here, pl.ds(0, width)] = fold_heads(nn(p.astype(BF), v_o[both, :]), SEG)
        lane = iota((SEG, HW), 1)
        extra = jnp.zeros((SEG, HW), F32)
        for h in range(heads):
            extra = jnp.where(lane == h, top[h * SEG : (h + 1) * SEG], extra)
            extra = jnp.where(lane == heads + h, total[h * SEG : (h + 1) * SEG], extra)
        part[here, pl.ds(width, HW)] = extra


def attention1(slots, local, live, owner, state, gain, w):
    rows, width = state.shape
    spread = (width // DH) * SEG
    return call(
        functools.partial(attention1_kernel, slots, local),
        (
            like(rows, width),
            like(rows, width),
            like(rows, width),
            like(slots, local, spread, dtype=F32),
            like(slots, local, width),
            like(slots * SEG, width + HW, dtype=F32),
        ),
        2 * rows * width * 3 * width + 8 * rows * width * spread,
        live,
        owner,
        state,
        gain,
        *w,
        scratch=[pltpu.VMEM((spread, width), BF), pltpu.VMEM((spread, width), BF)],
        name="attention1",
    )


def attention1_back_kernel(
    slots, local, share_ref, live_ref, owner_ref, gain, grad_mid, state, mixed, logs, q, k, v, probs, *refs
):
    weights, w = refs[:4], refs[4:8]
    (out_kept, out_sent, qkv_kept, qkv_sent, grad_end, mem_grad, gain_sum) = refs[8:15]
    grads, back, spread_a, spread_b, spread_o = refs[15:]
    piece = local + SEG
    rows = slots * piece
    width = gain.shape[1]
    heads = width // DH
    spread = heads * SEG
    low = grad_mid[...].astype(BF)
    grad_out = tn(mixed[...], once_rows(share_ref, slots, local, low))
    for j in range(4):
        target = (out_kept if j % 2 == 0 else out_sent).at[j // 2]
        target[...] = grad_out[j * HW : (j + 1) * HW].astype(BF)
        back[:, pl.ds(j * HW, HW)] = nt(low, weights[j][pl.ds(0, HW), :]).astype(BF)
    same = (iota((spread, spread), 0) // SEG == iota((spread, spread), 1) // SEG).astype(BF)

    def put(i, at, value):
        value = value.astype(BF)
        for j in range(4):
            grads[at, pl.ds(j * 3 * HW + i * HW, HW)] = value[:, j * HW : (j + 1) * HW]

    for s in range(slots):
        tok = pl.ds(s * piece, local)
        seg = pl.ds(s * piece + local, SEG)
        both = pl.ds(s * piece, piece)
        spread_heads(spread_a, k[seg, :])
        spread_heads(spread_b, v[seg, :])
        p = probs[s]
        dp = nt(back[tok, :], spread_b[...])
        product = p * dp
        hi = product.astype(BF)
        rest = (product - hi.astype(F32)).astype(BF)
        ds = (p * (dp - nn(hi, same) - nn(rest, same))).astype(BF)
        put(0, tok, nn(ds, spread_a[...]) * SCALE)
        mem_k = fold_heads(tn(ds, q[tok, :]), SEG)
        mem_v = fold_heads(tn(p.astype(BF), back[tok, :]), SEG)
        spread_heads(spread_a, q[seg, :])
        spread_heads(spread_b, back[seg, :])
        spread_heads(spread_o, mixed[seg, :])
        scores = nt(spread_a[...], k[both, :])
        log = jnp.concatenate([logs[pl.ds(s * SEG, SEG), :][:, h : h + 1] for h in range(heads)], axis=0)
        valid = memory_valid(local, spread, live_ref[s], owner_ref[0])
        p = jnp.where(valid, jnp.exp(jnp.where(valid, scores, FAR) - log), 0.0)
        delta = jnp.sum(
            spread_b[...].astype(F32) * spread_o[...].astype(F32), axis=1, keepdims=True
        )
        ds = (p * (nt(spread_b[...], v[both, :]) - delta)).astype(BF)
        put(0, seg, fold_heads(nn(ds, k[both, :]), SEG) * SCALE)
        grad_k = tn(ds, spread_a[...])
        grad_v = tn(p.astype(BF), spread_b[...])
        put(1, tok, grad_k[:local])
        put(2, tok, grad_v[:local])
        put(1, seg, grad_k[local:] + mem_k)
        put(2, seg, grad_v[local:] + mem_v)
    normed, inverse = normalize(state[...])
    low = (normed * gain[...]).astype(BF)
    total = None
    for j in range(4):
        part = grads[:, pl.ds(j * 3 * HW, 3 * HW)]
        target = (qkv_kept if j % 2 == 0 else qkv_sent).at[j // 2]
        target[...] = tn(low, part).astype(BF)
        add = nt(part, w[j][...])
        total = add if j == 0 else total + add
    gain_sum[...] = jnp.sum(total * normed, axis=0, keepdims=True)
    moved = grad_mid[...] + norm_backward(normed, inverse, gain[...], total)
    for s in range(slots):
        tok = pl.ds(s * piece, local)
        seg = pl.ds(s * piece + local, SEG)
        grad_end[tok, :] = moved[s * piece : s * piece + local]
        grad_end[seg, :] = grad_mid[seg, :]
        mem_grad[pl.ds(s * SEG, SEG), :] = total[s * piece + local : (s + 1) * piece]


def attention1_back(
    slots, local, share, live, owner, gain, grad_mid, state, mixed, logs, q, k, v, probs, weights, w
):
    rows, width = state.shape
    spread = (width // DH) * SEG
    return call(
        functools.partial(attention1_back_kernel, slots, local),
        (
            like(2, HW, width),
            like(2, HW, width),
            like(2, width, 3 * HW),
            like(2, width, 3 * HW),
            like(rows, width, dtype=F32),
            like(slots * SEG, width, dtype=F32),
            like(1, width, dtype=F32),
        ),
        2 * rows * width * 8 * width + 20 * rows * width * spread,
        share,
        live,
        owner,
        gain,
        grad_mid,
        state,
        mixed,
        logs,
        q,
        k,
        v,
        probs,
        *weights,
        *w,
        scratch=[
            pltpu.VMEM((rows, 3 * width), BF),
            pltpu.VMEM((rows, width), BF),
            pltpu.VMEM((spread, width), BF),
            pltpu.VMEM((spread, width), BF),
            pltpu.VMEM((spread, width), BF),
        ],
        name="attention1_back",
    )


def on_device(
    tokens, lengths, memory, norm_gain, w_qkv, output_weight, w_up, w_down, cot_tokens, cot_memory
):
    slots, local, width = tokens.shape
    me = lax.axis_index("tensor")
    gain = norm_gain.astype(F32).reshape(2, 2, 1, width)
    block = jnp.arange(4, dtype=jnp.int32)
    valid = jnp.clip(lengths[:, None] - (me ^ block)[None, :] * local, 0, local)
    live = valid[:, 0]
    owner = (me == 0).astype(jnp.int32)[None]
    share = (jnp.arange(slots, dtype=jnp.int32) % 4 == me).astype(jnp.int32)
    mem = jnp.pad(memory, ((0, SEG - M), (0, 0)))
    cot_mem = jnp.pad(cot_memory, ((0, 0), (0, SEG - M), (0, 0)))

    tok_blocks = [gather_blocks(tokens[s]) for s in range(slots)]
    w_attn = [jnp.swapaxes(w_qkv[l], 0, 1).reshape(width, 3 * HW) for l in range(2)]
    pack = [jnp.concatenate([output_weight[l], w_up[l], w_down[l]], axis=0) for l in range(2)]
    weights0 = gather_weights(pack[0])
    attn1 = gather_weights(w_attn[1])
    weights1 = gather_weights(pack[1])

    saved, outs, mixed_in = [], [], []
    for s in range(slots):
        own, near, far, qa, ka, va = attention0(valid[s], tok_blocks[s], mem, gain[0, 0], w_attn[0])
        saved.append((qa, ka, va))
        outs.append((own, near, far))
        got = move_tensor(far, 2)
        mixed_in += [own, move_tensor(near, 1), got[0], move_tensor(got[1], 1)]
    mid0, state1, hid0, mixed0 = ffn0(tokens, mem, gain[0, 1], mixed_in, weights0)
    q1, k1, v1, probs, out_tok, part = attention1(slots, local, live, owner, state1, gain[1, 0], attn1)
    parts = gather_blocks(part)
    res_tok, res_mem, kept1, sent1, grad_mid1, gain_f1, mixed1, logs = ffn1(
        share, live, gain[1, 1], state1, out_tok, cot_tokens, cot_mem, parts, weights1
    )

    out_kept, out_sent, qkv_kept, qkv_sent, grad1, mem_part, gain_a1 = attention1_back(
        slots, local, share, live, owner, gain[1, 0], grad_mid1, state1, mixed1, logs, q1, k1, v1, probs,
        weights1, attn1,
    )
    for mask in (1, 2):
        mem_part = mem_part + move_tensor(mem_part, mask)
    sum1 = sum_dp(scatter_blocks(kept1[:, HW:], sent1[:, HW:]))
    sum1o = sum_dp(scatter_blocks(out_kept, out_sent))
    sum1q = sum_dp(scatter_blocks(qkv_kept, qkv_sent))
    kept0, sent0, grad_tok, grad_mem, gain_f0, d_own, d_near, d_far = ffn0_back(
        slots, local, share, gain[0, 1], gain[1, 0], grad1, mem_part, state1, mid0, hid0, mixed0, weights0
    )
    sum0 = sum_dp(scatter_blocks(kept0, sent0))
    near_all = move_tensor(d_near, 1)
    far_all = move_tensor(d_far, 2)
    grad_qkv0, mem_normed, gain_a0, rows = 0.0, 0.0, 0.0, []
    for s in range(slots):
        far = jnp.stack([far_all[s, 0], move_tensor(far_all[s, 1], 1)])
        kept, sent, add_w, add_mem, add_gain = attention0_back(
            tok_blocks[s], mem, gain[0, 0], w_attn[0], saved[s], outs[s], (d_own[s], near_all[s], far)
        )
        grad_qkv0 = grad_qkv0 + add_w
        mem_normed = mem_normed + add_mem
        gain_a0 = gain_a0 + add_gain
        total = scatter_blocks(kept, sent)
        normed, inverse = normalize(tokens[s].astype(F32))
        rows.append(grad_tok[s] + norm_backward(normed, inverse, gain[0, 0], total))
    sum0q = sum_dp(grad_qkv0)
    mem_direct = jnp.where(me == 0, grad_mem, 0.0)
    small = jnp.concatenate([mem_normed, mem_direct, gain_a0, gain_a1, gain_f0, gain_f1], axis=0)
    small = sum_all(small)
    normed, inverse = normalize(memory.astype(F32))
    grad_memory = small[SEG : SEG + M] + norm_backward(normed, inverse, gain[0, 0], small[:M])
    gains = small[2 * SEG :]

    res_mem = res_mem[:, :M]
    res_mem = jnp.where(me % 2 == 0, res_mem, move_tensor(res_mem, 1))
    res_mem = jnp.where(me // 2 == 0, res_mem, move_tensor(res_mem, 2))

    def split_qkv(value):
        return jnp.swapaxes(value.reshape(width, 3, HW), 0, 1)

    return (
        res_tok,
        res_mem,
        jnp.stack(rows),
        grad_memory,
        gains[0:2],
        gains[2:4],
        jnp.stack([split_qkv(sum0q), split_qkv(sum1q)]),
        jnp.stack([sum0[:HW], sum1o]),
        jnp.stack([sum0[HW : HW + width], sum1[:width]]),
        jnp.stack([sum0[HW + width :], sum1[width:]]),
    )


def solution(mesh):
    return jax.shard_map(
        on_device,
        mesh=mesh,
        in_specs=(
            P("dp", "tensor", None),
            P("dp"),
            P(),
            P(),
            P(None, None, None, "tensor"),
            P(None, "tensor", None),
            P(None, None, "tensor"),
            P(None, "tensor", None),
            P("dp", "tensor", None),
            P("dp", None, None),
        ),
        out_specs=(
            P("dp", "tensor", None),
            P("dp", None, None),
            P("dp", "tensor", None),
            P(),
            P(),
            P(),
            P(None, None, None, "tensor"),
            P(None, "tensor", None),
            P(None, None, "tensor"),
            P(None, "tensor", None),
        ),
        check_vma=False,
    )
```

```python
import functools

import jax
import jax.numpy as jnp
from jax import lax
from jax.experimental import pallas as pl
from jax.experimental.pallas import tpu as pltpu
from jax.sharding import PartitionSpec as P

DH = 64
M = 20
SEG = 32
HW = 2 * DH
EPS = 1e-05
SCALE = DH**-0.5
FAR = -1e30
BF = jnp.bfloat16
F32 = jnp.float32


def exchange(value, axis, mask):
    return lax.ppermute(value, axis, [(i, i ^ mask) for i in range(lax.axis_size(axis))])


class Chain:
    def __init__(self, generator):
        self.generator = generator
        self.arrived = None
        self.result = None
        self.wanted = []
        self.done = False

    def ask(self):
        try:
            self.wanted = self.generator.send(self.arrived)
        except StopIteration as stop:
            self.result = stop.value
            self.wanted = []
            self.done = True


def fence(inputs, *chains):
    chains = [c for c in chains if not c.done]
    for chain in chains:
        chain.ask()
    leaving = [[item[0] for item in chain.wanted] for chain in chains]
    if inputs is not None:
        inputs, leaving = lax.optimization_barrier((inputs, leaving))
    for chain, arrays in zip(chains, leaving):
        chain.arrived = [
            exchange(array, item[1], item[2]) for array, item in zip(arrays, chain.wanted)
        ]
    return inputs


def land(outputs, *chains):
    chains = [c for c in chains if not c.done]
    outputs, arrived = lax.optimization_barrier((outputs, [c.arrived for c in chains]))
    for chain, arrays in zip(chains, arrived):
        chain.arrived = arrays
    return outputs


def finish(*chains):
    while not all(c.done for c in chains):
        fence(None, *chains)


def gather_chain(block):
    near, far = yield [(block, "tensor", 1), (block, "tensor", 2)]
    (last,) = yield [(far, "tensor", 1)]
    return [block, near, far, last]


def weights_chain(block):
    half = block.shape[0] // 2
    bit = lax.axis_index("dp") % 2
    first, near = yield [
        (lax.dynamic_slice_in_dim(block, bit * half, half, 0), "tensor", 2),
        (block, "tensor", 1),
    ]
    (second,) = yield [(first, "dp", 1)]
    far = jnp.concatenate(
        [jnp.where(bit == 0, first, second), jnp.where(bit == 0, second, first)], axis=0
    )
    (last,) = yield [(far, "tensor", 1)]
    return [block, near, far, last]


def split_chain(near, far, last):
    far, last, near = yield [(far, "tensor", 2), (last, "tensor", 2), (near, "tensor", 1)]
    (last,) = yield [(last, "tensor", 1)]
    return [near, far, last]


def added(a, b):
    return (a.astype(F32) + b.astype(F32)).astype(BF)


def core_chain(kept, sent):
    (got,) = yield [(sent, "tensor", 1)]
    return (added(kept[0], got[0]), added(kept[1], got[1]))


def rows_chain(kept, sent):
    near, far = yield from core_chain(kept, sent)
    (got,) = yield [(far, "tensor", 2)]
    return near.astype(F32) + got.astype(F32)


def dp_masks():
    size = lax.axis_size("dp")
    masks = []
    while 1 << len(masks) < size:
        masks.append(1 << len(masks))
    return masks


def dp_bit(mask):
    return (lax.axis_index("dp") // mask) % 2


def part(value, mask, other=False):
    half = value.shape[0] // 2
    bit = dp_bit(mask)
    return lax.dynamic_slice_in_dim(value, ((1 - bit) if other else bit) * half, half, 0)


def joined(value, got, mask):
    first = dp_bit(mask) == 0
    return jnp.concatenate([jnp.where(first, value, got), jnp.where(first, got, value)], axis=0)


def halving(value, masks):
    for mask in masks:
        (got,) = yield [(part(value, mask, True), "dp", mask)]
        value = added(part(value, mask), got)
    return value


def doubling(value, masks):
    for mask in reversed(masks):
        (got,) = yield [(value, "dp", mask)]
        value = joined(value, got, mask)
    return value


def cross_steps(near, far):
    half = near.shape[0] // 2
    near_a, near_b = near[:half], near[half:]
    far_a, far_b = far[:half], far[half:]
    pair = jnp.stack([part(near_b, 1, True), part(far_b, 1, True)])
    got_a, got_b = yield [(far_a, "tensor", 2), (pair, "dp", 1)]
    near_a = added(near_a, got_a)
    near_b = added(part(near_b, 1), got_b[0])
    far_b = added(part(far_b, 1), got_b[1])
    got_a, got_b = yield [(part(near_a, 1, True), "dp", 1), (far_b, "tensor", 2)]
    return jnp.concatenate([added(part(near_a, 1), got_a), added(near_b, got_b)], axis=0)


def cross_joined(value, got):
    half = value.shape[0] // 2
    return jnp.concatenate([joined(value[:half], got[:half], 1), joined(value[half:], got[half:], 1)])


def cross_chain(near, far):
    masks = dp_masks()[1:]
    value = yield from cross_steps(near, far)
    value = yield from halving(value, masks)
    value = yield from doubling(value, masks)
    (got,) = yield [(value, "dp", 1)]
    return cross_joined(value, got)


def last_chain(grad, small, late):
    masks = dp_masks()[1:]
    got = yield [
        (part(grad, 1, True), "dp", 1),
        (small, "tensor", 1),
        (small, "tensor", 2),
        (small, "tensor", 3),
    ]
    grad = added(part(grad, 1), got[0])
    small = (small + got[1]) + (got[2] + got[3])
    finish(late)
    first, second = grad.shape[0], late.result.shape[0]
    value = jnp.concatenate([grad, late.result, small.astype(BF)])
    value = yield from halving(value, masks)
    value = yield from doubling(value, masks)
    (got,) = yield [(value, "dp", 1)]
    return (
        joined(value[:first], got[:first], 1),
        value[first + second :].astype(F32) + got[first + second :].astype(F32),
        cross_joined(value[first : first + second], got[first : first + second]),
    )


def nn(a, b):
    return lax.dot_general(a, b, (((1,), (0,)), ((), ())), preferred_element_type=F32)


def nt(a, b):
    return lax.dot_general(a, b, (((1,), (1,)), ((), ())), preferred_element_type=F32)


def tn(a, b):
    return lax.dot_general(a, b, (((0,), (0,)), ((), ())), preferred_element_type=F32)


def normalize(state):
    center = jnp.mean(state, axis=-1, keepdims=True)
    shifted = state - center
    spread = jnp.mean(shifted * shifted, axis=-1, keepdims=True)
    inverse = lax.rsqrt(spread + EPS)
    return (shifted * inverse, inverse)


def norm_backward(normed, inverse, gain_row, grad_normed):
    scaled = grad_normed * gain_row
    return inverse * (
        scaled
        - jnp.mean(scaled, axis=-1, keepdims=True)
        - normed * jnp.mean(scaled * normed, axis=-1, keepdims=True)
    )


def gelu_parts(hidden, with_slope):
    c = 0.7978845608028654
    a = 0.044715
    square = hidden * hidden
    t = jnp.tanh(hidden * (c + (c * a) * square))
    up = 0.5 + 0.5 * t
    active = hidden * up
    if not with_slope:
        return active
    slope = up + hidden * (0.5 - 0.5 * t * t) * (c + (3.0 * c * a) * square)
    return (active, slope)


def iota(shape, axis):
    return lax.broadcasted_iota(jnp.int32, shape, axis)


class Far:
    def __init__(self, array, shape=None, pieces=None):
        self.array = array
        self.shape = array.shape if shape is None else shape
        self.pieces = [((), ())] if pieces is None else pieces


class Away:
    def __init__(self, *shape, dtype=BF, blocks=False, before=None):
        self.shape = shape
        self.dtype = dtype
        self.blocks = blocks
        self.before = before
        self.skip = 0 if before is None else before.shape[1]
        self.whole = shape if before is None else (shape[0], shape[1] + self.skip) + shape[2:]


def at(ref, index):
    return ref.at[index] if index else ref


class Incoming:
    def __init__(self, ref, copies):
        self.ref = ref
        self.copies = copies
        self.shape = ref.shape
        for copy in copies:
            copy.start()

    def wait(self):
        for copy in self.copies:
            copy.wait()
        self.copies = []

    def __getitem__(self, index):
        self.wait()
        return self.ref[index]


class Outgoing:
    def __init__(self, ref, copies):
        self.ref = ref
        self.copies = copies
        self.sent = [False] * len(copies)
        self.last_slots = range(4) if len(copies) > 1 else (1,)

    def __setitem__(self, index, value):
        self.ref[index] = value

    def __getitem__(self, index):
        return self.ref[index]

    def send(self, block=None):
        for j, copy in enumerate(self.copies):
            if not self.sent[j] and block in (None, j):
                copy.start()
                self.sent[j] = True


def call(kernel, results, cost, *operands, scratch=(), name=None, limit=60):
    me = lax.axis_index("tensor").astype(jnp.int32)
    operands = (me ^ jnp.arange(4, dtype=jnp.int32),) + operands
    arrays = [o.array if isinstance(o, Far) else o for o in operands]
    through = [r for r in results if isinstance(r, Away) and r.before is not None]
    arrays += [r.before for r in through]
    specs, buffers, count = [], [], 0
    for o in operands:
        if isinstance(o, Far):
            specs.append(pl.BlockSpec(memory_space=pltpu.HBM))
            buffers.append(pltpu.VMEM(o.shape, o.array.dtype))
            count += len(o.pieces)
        else:
            space = pltpu.SMEM if o.dtype == jnp.int32 else pltpu.VMEM
            specs.append(pl.BlockSpec(memory_space=space))
    specs += [pl.BlockSpec(memory_space=pltpu.HBM) for _ in through]
    count += 2 * len(through)
    out_specs = []
    for r in results:
        away = isinstance(r, Away)
        out_specs.append(pl.BlockSpec(memory_space=pltpu.HBM if away else pltpu.VMEM))
        if away:
            if r.before is not None:
                buffers.append(pltpu.VMEM(r.before.shape, r.dtype))
            buffers.append(pltpu.VMEM(r.shape, r.dtype))
            count += r.shape[0] if r.blocks else 1

    def body(*refs):
        ins = refs[: len(operands)]
        passed = list(refs[len(operands) : len(arrays)])
        outs = refs[len(arrays) : len(arrays) + len(results)]
        rest = list(refs[len(arrays) + len(results) :])
        sem = rest.pop()
        used = iter(range(count))
        local_buffers = iter(rest[: len(buffers)])
        given = []
        for o, ref in zip(operands, ins):
            if isinstance(o, Far):
                buffer = next(local_buffers)
                ref = Incoming(
                    buffer,
                    [
                        pltpu.make_async_copy(at(ref, src), at(buffer, dst), sem.at[next(used)])
                        for src, dst in o.pieces
                    ],
                )
            given.append(ref)
        taken, waiting = [], []
        for r, ref in zip(results, outs):
            if isinstance(r, Away):
                if r.before is not None:
                    held = next(local_buffers)
                    target = ref.at[:, pl.ds(0, r.skip)]
                    held = [
                        pltpu.make_async_copy(passed.pop(0), held, sem.at[next(used)]),
                        pltpu.make_async_copy(held, target, sem.at[next(used)]),
                    ]
                    held[0].start()
                    waiting.append(held)
                buffer = next(local_buffers)
                pairs = [(buffer, ref)]
                if r.blocks:
                    own_rows = pl.ds(r.skip, r.shape[1])
                    pairs = [(buffer.at[j], ref.at[ins[0][j], own_rows]) for j in range(r.shape[0])]
                ref = Outgoing(
                    buffer, [pltpu.make_async_copy(a, b, sem.at[next(used)]) for a, b in pairs]
                )
            taken.append(ref)
        kernel(*given[1:], *taken, *rest[len(buffers) :])
        for ref in given:
            if isinstance(ref, Incoming):
                ref.wait()
        for arriving, leaving in waiting:
            arriving.wait()
            leaving.start()
        for ref in taken:
            if isinstance(ref, Outgoing):
                ref.send()
        for ref in taken:
            if isinstance(ref, Outgoing):
                for copy in ref.copies:
                    copy.wait()
        for _, leaving in waiting:
            leaving.wait()

    moved = sum(o.size * o.dtype.itemsize for o in arrays)
    return pl.pallas_call(
        body,
        out_shape=[
            jax.ShapeDtypeStruct(r.whole if isinstance(r, Away) else r.shape, r.dtype) for r in results
        ],
        in_specs=specs,
        out_specs=out_specs,
        scratch_shapes=buffers + list(scratch) + [pltpu.SemaphoreType.DMA((max(count, 1),))],
        compiler_params=pltpu.CompilerParams(vmem_limit_bytes=limit * 1024 * 1024),
        cost_estimate=pl.CostEstimate(flops=cost, bytes_accessed=moved, transcendentals=0),
        name=name,
    )(*arrays)


def like(*shape, dtype=BF):
    return jax.ShapeDtypeStruct(shape, dtype)


def qkv_pieces(sources):
    return [
        (tuple(prefix) + (i,), (slice(None), pl.ds((3 * j + i) * HW, HW)))
        for j, prefix in enumerate(sources)
        for i in range(3)
    ]


def gain_row(gain_ref, layer, which):
    return gain_ref[layer, pl.ds(which, 1), :].astype(F32)


def pad_rows(scratch, value):
    scratch[...] = jnp.zeros_like(scratch)
    scratch[pl.ds(0, value.shape[0]), :] = value.astype(F32)


def head_lanes(rows, h):
    lane = iota((rows, HW), 1)
    inside = (lane >= h * DH) & (lane < (h + 1) * DH)
    return lane - (1 - h) * DH, inside


def attention0_kernel(
    local, valid_ref, mem, gain, x0, x1, x2, x3, w, own, near, far, last, qa, ka, va, vh, mem_s
):
    keys = 4 * local + SEG
    tokens = [x0, x1, x2, x3]
    pad_rows(mem_s, mem[...])
    blocks = [(j * local, local, tokens[j]) for j in range(4)] + [(4 * local, SEG, mem_s)]
    for j, (start, size, ref) in enumerate(blocks):
        normed, _ = normalize(ref[...].astype(F32))
        normed = (normed * gain_row(gain, 0, 0)).astype(BF)
        proj = nn(normed, w[...]).astype(BF)
        q = proj[:, :HW] * jnp.asarray(SCALE, BF)
        k = proj[:, HW : 2 * HW]
        v = proj[:, 2 * HW :]
        rows = pl.ds(start, size)
        va[rows, :] = v
        valid = iota((size, HW), 0) < (valid_ref[j] if j < 4 else M)
        bias = jnp.where(valid, 0.0, FAR).astype(BF)
        for h in range(2):
            spare, inside = head_lanes(size, h)
            one = jnp.where(spare == 0, 1.0, 0.0).astype(BF)
            extra = jnp.where((spare >= 1) & (spare <= 3), 1.0, 0.0).astype(BF)
            ka[h, rows, :] = jnp.where(inside, k, jnp.where(spare == 0, bias, extra))
            qa[h, rows, :] = jnp.where(inside, q, one)
            vh[h, rows, :] = jnp.where(inside, v, one)
    ka.send()
    va.send()

    def chunk(start, size):
        rows = pl.ds(start, size)
        out = None
        for h in range(2):
            spare, inside = head_lanes(size, h)
            q = qa[h, rows, :]
            scores = nt(q, ka[h])
            top = jnp.max(scores, axis=1, keepdims=True)
            o = nn(jnp.exp(scores - top).astype(BF), vh[h])
            total = o[:, (1 - h) * DH : (1 - h) * DH + 1]
            col = -(top + jnp.log(total))
            hi = col.astype(BF).astype(F32)
            mid = (col - hi).astype(BF).astype(F32)
            low = col - hi - mid
            extra = jnp.where(spare == 1, hi, jnp.where(spare == 2, mid, jnp.where(spare == 3, low, 0.0)))
            qa[h, rows, :] = jnp.where(inside | (spare == 0), q, extra.astype(BF))
            o = o / total
            out = o if h == 0 else jnp.where(inside, o, out)
        return out.astype(BF)

    out = chunk(4 * local, SEG)
    rows = pl.ds(local, SEG)
    for target in (own, near, far, last):
        target[rows, :] = out
    rows = pl.ds(0, local)
    out = chunk(2 * local, 2 * local)
    far[rows, :] = out[:local]
    last[rows, :] = out[local:]
    far.send()
    last.send()
    out = chunk(0, 2 * local)
    own[rows, :] = out[:local]
    near[rows, :] = out[local:]


def attention0(s, valid, tokens, blocks, memory, gain, w_qkv):
    slots, local, width = tokens.shape
    keys = 4 * local + SEG
    piece = local + SEG
    cost = 2 * keys * width * 3 * HW + 16 * keys * keys * HW
    return call(
        functools.partial(attention0_kernel, local),
        (
            Away(piece, HW),
            Away(piece, HW),
            Away(piece, HW),
            Away(piece, HW),
            Away(2, keys, HW),
            Away(2, keys, HW),
            Away(keys, HW),
        ),
        cost,
        valid,
        memory,
        gain,
        Far(tokens, (local, width), [((s,), ())]),
        *[Far(b) for b in blocks],
        Far(w_qkv, (width, 3 * HW), qkv_pieces([(0,)])),
        scratch=[pltpu.VMEM((2, keys, HW), BF), pltpu.VMEM((SEG, width), F32)],
        name="attention0",
    )


def attention0_back_kernel(
    local, first_call, mem, gain, before_mem, before_gain, g_own, g_near, g_far, g_last,
    o_own, o_near, o_far, o_last, va, ka, qa, x1, x3, x0, x2, w, before_w,
    kept, sent, grad_w, mem_normed, gain_sum,
    grads, va_s, da_s, d_s, acc_v, acc_k, mem_s,
):
    keys = 4 * local + SEG
    pad_rows(mem_s, mem[...])
    own = pl.ds(0, local)
    pieces = [
        (0, g_own[own, :], o_own[own, :]),
        (local, g_near[own, :], o_near[own, :]),
        (2 * local, g_far[own, :], o_far[own, :]),
        (3 * local, g_last[own, :], o_last[own, :]),
    ]
    tail = pl.ds(local, SEG)
    parts = [g[tail, :].astype(F32) for g in (g_own, g_near, g_far, g_last)]
    grad = ((parts[0] + parts[1]) + (parts[2] + parts[3])).astype(BF)
    pieces.append((4 * local, grad, o_own[tail, :]))
    for start, grad, out in pieces:
        size = grad.shape[0]
        rows = pl.ds(start, size)
        product = grad.astype(F32) * out.astype(F32)
        d_s[rows, :] = grad
        for h in range(2):
            spare, inside = head_lanes(size, h)
            col = -jnp.sum(jnp.where(inside, product, 0.0), axis=-1, keepdims=True)
            hi = col.astype(BF).astype(F32)
            extra = jnp.where(spare == 0, hi, jnp.where(spare == 1, col - hi, 0.0))
            da_s[h, rows, :] = jnp.where(inside, grad, extra.astype(BF))
    for h in range(2):
        spare, inside = head_lanes(keys, h)
        ones = jnp.where((spare == 0) | (spare == 1), 1.0, 0.0).astype(BF)
        va_s[h] = jnp.where(inside, va[...], ones)
    first = iota((keys, HW), 1) < DH
    key = jnp.where(first, ka[0], ka[1])

    def chunk(start, size, fresh):
        rows = pl.ds(start, size)
        turned = []
        for h in range(2):
            p = jnp.exp(nt(ka[h], qa[h, rows, :]))
            dp = nt(va_s[h], da_s[h, rows, :])
            ds = (p * dp).astype(BF)
            add_v = nn(p.astype(BF), d_s[rows, :])
            add_k = nn(ds, qa[h, rows, :])
            if fresh:
                acc_v[h] = add_v
                acc_k[h] = add_k
            else:
                acc_v[h] += add_v
                acc_k[h] += add_k
            turned.append(tn(ds, key))
        out = jnp.where(iota((size, HW), 1) < DH, turned[0], turned[1]) * SCALE
        grads[rows, :HW] = out.astype(BF)

    chunk(0, 2 * local, True)
    chunk(2 * local, 2 * local, False)
    chunk(4 * local, SEG, False)
    grads[:, HW : 2 * HW] = jnp.where(first, acc_k[0], acc_k[1]).astype(BF)
    grads[:, 2 * HW :] = jnp.where(first, acc_v[0], acc_v[1]).astype(BF)

    tokens = [x0, x1, x2, x3]
    total_w = None if first_call else before_w[...]
    total_gain = None if first_call else before_gain[...]
    for j in (1, 3, 0, 2, 4):
        size = local if j < 4 else SEG
        ref = tokens[j] if j < 4 else mem_s
        normed, _ = normalize(ref[...].astype(F32))
        low = (normed * gain_row(gain, 0, 0)).astype(BF)
        part = grads[pl.ds(j * local, size), :]
        add_w = tn(part, low)
        grad_normed = nt(part, w[...])
        add_gain = jnp.sum(grad_normed * normed, axis=0, keepdims=True)
        total_w = add_w if total_w is None else total_w + add_w
        total_gain = add_gain if total_gain is None else total_gain + add_gain
        if j == 4:
            mem_normed[...] = grad_normed if first_call else grad_normed + before_mem[...]
        else:
            target = kept if j % 2 == 0 else sent
            target[j // 2] = grad_normed.astype(BF)
            if j == 3:
                sent.send()
            if j == 2:
                kept.send()
    grad_w[...] = total_w
    gain_sum[...] = total_gain


def attention0_back(s, tokens, blocks, memory, gain, w_qkv, saved, outs, moved, before):
    slots, local, width = tokens.shape
    keys = 4 * local + SEG
    cost = 4 * keys * width * 3 * HW + 40 * keys * keys * HW
    first_call = before is None
    if first_call:
        before = [jnp.zeros((8, HW), F32)] * 3
    before_w, before_mem, before_gain = before
    qa, ka, va = saved
    block = (local + SEG, HW)
    return call(
        functools.partial(attention0_back_kernel, local, first_call),
        (
            Away(2, local, width),
            Away(2, local, width),
            Away(3 * HW, width, dtype=F32),
            like(SEG, width, dtype=F32),
            like(1, width, dtype=F32),
        ),
        cost,
        memory,
        gain,
        before_mem,
        before_gain,
        *[Far(g, block, [((s,), ())]) for g in moved],
        *[Far(o) for o in outs],
        Far(va),
        Far(ka),
        Far(qa),
        Far(blocks[0]),
        Far(blocks[2]),
        Far(tokens, (local, width), [((s,), ())]),
        Far(blocks[1]),
        Far(w_qkv, (width, 3 * HW), qkv_pieces([(0,)])),
        Far(before_w),
        scratch=[
            pltpu.VMEM((keys, 3 * HW), BF),
            pltpu.VMEM((2, keys, HW), BF),
            pltpu.VMEM((2, keys, HW), BF),
            pltpu.VMEM((keys, HW), BF),
            pltpu.VMEM((2, keys, HW), F32),
            pltpu.VMEM((2, keys, HW), F32),
            pltpu.VMEM((SEG, width), F32),
        ],
        name="attention0_back",
    )


def ffn0_kernel(slots, local, mem, gain, *refs):
    tokens, own, refs = refs[0], refs[1 : 1 + slots], refs[1 + slots :]
    moved, weights = refs[: 3 * slots], refs[3 * slots : 4 + 3 * slots]
    mid, end, hid0, hid1, hid2, hid3, mixed, normed_s, mem_s = refs[4 + 3 * slots :]
    hid = [hid0, hid1, hid2, hid3]
    piece = local + SEG
    width = gain.shape[2]
    inner = weights[0].shape[0] - HW - width
    pad_rows(mem_s, mem[...])
    for s in range(slots):
        rows = pl.ds(s * piece, piece)
        state = jnp.concatenate([tokens[s].astype(F32), mem_s[...]], axis=0)
        for j in range(4):
            out = own[s][...] if j == 0 else moved[3 * s + j - 1][...]
            mixed[rows, pl.ds(j * HW, HW)] = out
            state += nn(out, weights[j][pl.ds(0, HW), :])
        mid[rows, :] = state
        end[rows, :] = state
        normed_s[rows, :] = (normalize(state)[0] * gain_row(gain, 0, 1)).astype(BF)
    mid.send()
    mixed.send()
    for j in range(4):
        hid[j][...] = nn(normed_s[...], weights[j][pl.ds(HW, width), :]).astype(BF)
        hid[j].send()
    for j in range(4):
        active = gelu_parts(hid[j][...].astype(F32), False).astype(BF)
        end[...] += nn(active, weights[j][pl.ds(HW + width, inner), :])


def ffn0(tokens, memory, gain, own, moved, weights):
    slots, local, width = tokens.shape
    rows = slots * (local + SEG)
    inner = weights[0].shape[0] - HW - width
    return call(
        functools.partial(ffn0_kernel, slots, local),
        (
            Away(rows, width, dtype=F32),
            Away(rows, width, dtype=F32),
            Away(rows, inner),
            Away(rows, inner),
            Away(rows, inner),
            Away(rows, inner),
            Away(rows, width),
        ),
        2 * rows * width * (width + 8 * inner),
        memory,
        gain,
        Far(tokens),
        *[Far(o) for o in own],
        *[Far(m) for m in moved],
        *[Far(w) for w in weights],
        scratch=[pltpu.VMEM((rows, width), BF), pltpu.VMEM((SEG, width), F32)],
        name="ffn0",
    )


def ffn_back_core(weights, low, low_once, hidden_of, normed, normed_once, targets, with_output):
    width = normed.shape[1]
    inner = weights[targets[0][0]].shape[0] - HW - width
    total, output = None, None
    for j, target, slot in targets:
        up = weights[j][pl.ds(HW, width), :]
        down = weights[j][pl.ds(HW + width, inner), :]
        active, slope = gelu_parts(hidden_of(j), True)
        active = active.astype(BF)
        if with_output:
            add = nn(active, down)
            output = add if output is None else output + add
        grad_hidden = (nt(low, down) * slope).astype(BF)
        target[slot, pl.ds(0, width), :] = tn(normed_once, grad_hidden).astype(BF)
        target[slot, pl.ds(width, inner), :] = tn(active, low_once).astype(BF)
        if slot in target.last_slots:
            target.send(slot if len(target.copies) > 1 else None)
        add = nt(grad_hidden, up)
        total = add if total is None else total + add
    return (total, output)


def once_rows(share_ref, slots, local, value):
    piece = local + SEG
    parts = []
    for s in range(slots):
        parts.append(value[s * piece : s * piece + local])
        tail = value[s * piece + local : (s + 1) * piece]
        parts.append(jnp.where(share_ref[s] > 0, tail, jnp.zeros_like(tail)))
    return jnp.concatenate(parts, axis=0)


def ffn1_kernel(slots, local, share_ref, live_ref, gain, cot_mem, *refs):
    parts, out_tok, cot, state, weights = refs[:4], refs[4], refs[5], refs[6], refs[7:11]
    res_tok, res_mem, grads, grad_mid, gain_sum, mixed, logs = refs[11:18]
    normed_s, end_s, low_s, mem_s = refs[18:]
    piece = local + SEG
    width = gain.shape[2]
    heads = width // DH
    gain_f = gain_row(gain, 1, 1)
    lane = iota((SEG, HW), 1)
    mixed_rows = []
    for s in range(slots):
        seg = pl.ds(s * SEG, SEG)
        scale = {}
        log = jnp.zeros((SEG, HW), F32)
        extras = [parts[j][seg, pl.ds(width, HW)] for j in range(4)]
        for h in range(heads):
            source = [2 * ((h // 2) ^ j) + h % 2 for j in range(4)]
            tops = [extras[j][:, source[j] : source[j] + 1] for j in range(4)]
            sums = [extras[j][:, heads + source[j] : heads + source[j] + 1] for j in range(4)]
            peak = functools.reduce(jnp.maximum, tops)
            raised = [jnp.exp(t - peak) for t in tops]
            total = functools.reduce(jnp.add, [r * t for r, t in zip(raised, sums)])
            scale[h] = [r / total for r in raised]
            log = jnp.where(lane == h, peak + jnp.log(total), log)
        logs[seg, :] = log
        for b in range(4):
            merged = jnp.zeros((SEG, HW), F32)
            for j in range(4):
                factor = jnp.where(lane < DH, scale[2 * b][j], scale[2 * b + 1][j])
                merged += factor * parts[j][seg, pl.ds((b ^ j) * HW, HW)]
            mixed[pl.ds(s * piece + local, SEG), pl.ds(b * HW, HW)] = merged.astype(BF)
        rows = pl.ds(s * piece, local)
        mixed[rows, :] = out_tok[s]
        live = iota((local, 1), 0) < live_ref[s]
        low_s[rows, :] = jnp.where(live, cot[s], jnp.zeros_like(cot[s]))
        pad_rows(mem_s, cot_mem[s])
        low_s[pl.ds(s * piece + local, SEG), :] = mem_s[...].astype(BF)
    mixed.send()
    mid = state[...]
    for j in range(4):
        mid += nn(mixed[:, pl.ds(j * HW, HW)], weights[j][pl.ds(0, HW), :])
    end_s[...] = mid
    mid_normed, inverse = normalize(mid)
    normed = (mid_normed * gain_f).astype(BF)
    normed_s[...] = mid_normed
    low = low_s[...]
    grad_normed, output = ffn_back_core(
        weights,
        low,
        once_rows(share_ref, slots, local, low),
        lambda j: nn(normed, weights[j][pl.ds(HW, width), :]),
        normed,
        once_rows(share_ref, slots, local, normed),
        [(j, grads, j) for j in range(4)],
        True,
    )
    end_s[...] += output
    for s in range(slots):
        res_tok[s] = end_s[pl.ds(s * piece, local), :].astype(BF)
        res_mem[s] = end_s[pl.ds(s * piece + local, SEG), :].astype(BF)
    res_tok.send()
    mid_normed = normed_s[...]
    gain_sum[...] = jnp.sum(
        once_rows(share_ref, slots, local, grad_normed * mid_normed), axis=0, keepdims=True
    )
    grad_mid[...] = low_s[...].astype(F32) + norm_backward(mid_normed, inverse, gain_f, grad_normed)


def ffn1(share, live, gain, state, out_tok, cot, cot_mem, parts, weights):
    slots, local, width = cot.shape
    rows = slots * (local + SEG)
    inner = weights[0].shape[0] - HW - width
    return call(
        functools.partial(ffn1_kernel, slots, local),
        (
            Away(slots, local, width),
            like(slots, SEG, width),
            Away(4, width + inner, width, blocks=True),
            Away(rows, width, dtype=F32),
            like(1, width, dtype=F32),
            Away(rows, width),
            like(slots * SEG, HW, dtype=F32),
        ),
        2 * rows * width * (width + 24 * inner),
        share,
        live,
        gain,
        cot_mem,
        *[Far(p) for p in parts],
        Far(out_tok),
        Far(cot),
        Far(state),
        *[Far(w) for w in weights],
        scratch=[
            pltpu.VMEM((rows, width), F32),
            pltpu.VMEM((rows, width), F32),
            pltpu.VMEM((rows, width), BF),
            pltpu.VMEM((SEG, width), F32),
        ],
        name="ffn1",
    )


def ffn0_back_sent_kernel(gain, grad_in, mid, hid_near, hid_last, w_near, w_last, sent, normed_sum):
    low = grad_in[...].astype(BF)
    normed = (normalize(mid[...])[0] * gain_row(gain, 0, 1)).astype(BF)
    hidden = {1: hid_near, 3: hid_last}
    normed_sum[...], _ = ffn_back_core(
        {1: w_near, 3: w_last},
        low,
        low,
        lambda j: hidden[j][...].astype(F32),
        normed,
        normed,
        [(1, sent, 0), (3, sent, 1)],
        False,
    )


def ffn0_back_sent(gain, grad_in, mid, hid, weights):
    rows, width = grad_in.shape
    inner = weights[0].shape[0] - HW - width
    return call(
        ffn0_back_sent_kernel,
        (Away(2, width + inner, width), Away(rows, width, dtype=F32)),
        2 * rows * width * (8 * inner),
        gain,
        Far(grad_in),
        Far(mid),
        Far(hid[1]),
        Far(hid[3]),
        Far(weights[1]),
        Far(weights[3]),
        name="ffn0_back_sent",
    )


def ffn0_back_kept_kernel(
    slots, local, gain, grad_in, mid, hid_own, hid_far, w0, w2, w1, w3, normed_sum, mixed,
    kept, out_kept, out_sent, grad_tok, grad_mem, gain_sum, *moving
):
    weights = [w0, w1, w2, w3]
    piece = local + SEG
    width = gain.shape[2]
    low = grad_in[...].astype(BF)
    mid_normed, inverse = normalize(mid[...])
    normed = (mid_normed * gain_row(gain, 0, 1)).astype(BF)
    hidden = {0: hid_own, 2: hid_far}
    grad_normed, _ = ffn_back_core(
        weights,
        low,
        low,
        lambda j: hidden[j][...].astype(F32),
        normed,
        normed,
        [(0, kept, 0), (2, kept, 1)],
        False,
    )
    grad_normed += normed_sum[...]
    grad = grad_in[...] + norm_backward(mid_normed, inverse, gain_row(gain, 0, 1), grad_normed)
    low = grad.astype(BF)
    for j in (3, 2, 1, 0):
        back = nt(low, weights[j][pl.ds(0, HW), :]).astype(BF)
        for s in range(slots):
            moving[j][s] = back[s * piece : (s + 1) * piece]
        moving[j].send()
    gain_sum[...] = jnp.sum(grad_normed * mid_normed, axis=0, keepdims=True)
    total = jnp.zeros((SEG, width), F32)
    for s in range(slots):
        grad_tok[s] = grad[s * piece : s * piece + local]
        total += grad[s * piece + local : (s + 1) * piece]
    grad_mem[...] = total
    grad_out = tn(mixed[...], low)
    for j in range(4):
        target = out_kept if j % 2 == 0 else out_sent
        target[j // 2] = grad_out[j * HW : (j + 1) * HW].astype(BF)


def ffn0_back_kept(slots, local, gain, grad_in, normed_sum, mid, hid, mixed, weights):
    rows, width = grad_in.shape
    inner = weights[0].shape[0] - HW - width
    return call(
        functools.partial(ffn0_back_kept_kernel, slots, local),
        (
            Away(2, width + inner, width),
            Away(2, HW, width),
            Away(2, HW, width),
            Away(slots, local, width, dtype=F32),
            like(SEG, width, dtype=F32),
            like(1, width, dtype=F32),
            *[Away(slots, local + SEG, HW) for _ in range(4)],
        ),
        2 * rows * width * (2 * width + 8 * inner),
        gain,
        Far(grad_in),
        Far(mid),
        Far(hid[0]),
        Far(hid[2]),
        Far(weights[0]),
        Far(weights[2]),
        *[Far(weights[j], (HW, width), [((pl.ds(0, HW),), ())]) for j in (1, 3)],
        Far(normed_sum),
        Far(mixed),
        name="ffn0_back_kept",
    )


def spread_heads(target, value):
    size, width = value.shape
    lane = iota((size, width), 1) // DH
    for h in range(width // DH):
        target[pl.ds(h * size, size), :] = jnp.where(lane == h, value, jnp.zeros_like(value))


def fold_heads(value, size):
    width = value.shape[1]
    lane = iota((size, width), 1) // DH
    total = jnp.zeros((size, width), value.dtype)
    for h in range(width // DH):
        total += jnp.where(lane == h, value[h * size : (h + 1) * size], 0.0)
    return total


def memory_valid(local, rows, live, owner):
    lane = iota((rows, local + SEG), 1)
    return (lane < live) | ((lane >= local) & (lane < local + M) & (owner > 0))


def attention1_kernel(slots, local, live_ref, owner_ref, gain, state, *refs):
    w = refs[:4]
    q_o, k_o, v_o, probs, out_tok, part, spread_k, spread_v = refs[4:]
    piece = local + SEG
    width = gain.shape[2]
    heads = width // DH
    normed = (normalize(state[...])[0] * gain_row(gain, 1, 0)).astype(BF)
    for j in range(4):
        proj = nn(normed, w[j][...]).astype(BF)
        lanes = pl.ds(j * HW, HW)
        q_o[:, lanes] = proj[:, :HW] * jnp.asarray(SCALE, BF)
        k_o[:, lanes] = proj[:, HW : 2 * HW]
        v_o[:, lanes] = proj[:, 2 * HW :]
    for ref in (q_o, k_o, v_o):
        ref.send()
    for s in range(slots):
        tok = pl.ds(s * piece, local)
        seg = pl.ds(s * piece + local, SEG)
        both = pl.ds(s * piece, piece)
        spread_heads(spread_k, q_o[seg, :])
        scores = nt(spread_k[...], k_o[both, :])
        valid = memory_valid(local, heads * SEG, live_ref[s], owner_ref[0])
        scores = jnp.where(valid, scores, FAR)
        top = jnp.max(scores, axis=1, keepdims=True)
        p = jnp.where(valid, jnp.exp(scores - top), 0.0)
        total = jnp.sum(p, axis=1, keepdims=True)
        here = pl.ds(s * SEG, SEG)
        part[here, pl.ds(0, width)] = fold_heads(nn(p.astype(BF), v_o[both, :]), SEG)
        lane = iota((SEG, HW), 1)
        extra = jnp.zeros((SEG, HW), F32)
        for h in range(heads):
            extra = jnp.where(lane == h, top[h * SEG : (h + 1) * SEG], extra)
            extra = jnp.where(lane == heads + h, total[h * SEG : (h + 1) * SEG], extra)
        part[here, pl.ds(width, HW)] = extra
    part.send()
    for s in range(slots):
        tok = pl.ds(s * piece, local)
        seg = pl.ds(s * piece + local, SEG)
        spread_heads(spread_k, k_o[seg, :])
        spread_heads(spread_v, v_o[seg, :])
        st = nt(spread_k[...], q_o[tok, :])
        st = jnp.where(iota((heads * SEG, local), 0) % SEG < M, st, FAR)
        st = st.reshape(heads, SEG, local)
        p = jnp.exp(st - jnp.max(st, axis=1, keepdims=True))
        p = p / jnp.sum(p, axis=1, keepdims=True)
        p = p.reshape(heads * SEG, local).T
        probs[s] = p
        out_tok[s] = nn(p.astype(BF), spread_v[...]).astype(BF)


def far_qkv(block, width):
    pieces = [((pl.ds(i * width, width),), (slice(None), pl.ds(i * HW, HW))) for i in range(3)]
    return Far(block, (width, 3 * HW), pieces)


def attention1(slots, local, live, owner, state, gain, w):
    rows, width = state.shape
    spread = (width // DH) * SEG
    return call(
        functools.partial(attention1_kernel, slots, local),
        (
            Away(rows, width),
            Away(rows, width),
            Away(rows, width),
            Away(slots, local, spread, dtype=F32),
            Away(slots, local, width),
            Away(slots * SEG, width + HW, dtype=F32),
        ),
        2 * rows * width * 3 * width + 8 * rows * width * spread,
        live,
        owner,
        gain,
        Far(state),
        *[far_qkv(x, width) for x in w],
        scratch=[pltpu.VMEM((spread, width), BF), pltpu.VMEM((spread, width), BF)],
        name="attention1",
    )


def attention1_back_kernel(
    slots, local, share_ref, live_ref, owner_ref, gain, logs, grad_mid, *refs
):
    weights, (k, v, probs, q, mixed, state), w = refs[:4], refs[4:10], refs[10:14]
    refs = refs[6:]
    grads, grad_end, gain_sum, back, spread_a, spread_b, spread_o = refs[8:]
    piece = local + SEG
    width = gain.shape[2]
    heads = width // DH
    spread = heads * SEG
    low = grad_mid[...].astype(BF)
    for j in range(4):
        back[:, pl.ds(j * HW, HW)] = nt(low, weights[j][pl.ds(0, HW), :]).astype(BF)
    same = (iota((spread, spread), 0) // SEG == iota((spread, spread), 1) // SEG).astype(BF)

    def put(i, at, value):
        value = value.astype(BF)
        for j in range(4):
            grads[at, pl.ds(j * 3 * HW + i * HW, HW)] = value[:, j * HW : (j + 1) * HW]

    for s in range(slots):
        tok = pl.ds(s * piece, local)
        seg = pl.ds(s * piece + local, SEG)
        both = pl.ds(s * piece, piece)
        spread_heads(spread_a, k[seg, :])
        spread_heads(spread_b, v[seg, :])
        p = probs[s]
        dp = nt(back[tok, :], spread_b[...])
        product = p * dp
        hi = product.astype(BF)
        rest = (product - hi.astype(F32)).astype(BF)
        ds = (p * (dp - nn(hi, same) - nn(rest, same))).astype(BF)
        put(0, tok, nn(ds, spread_a[...]) * SCALE)
        mem_k = fold_heads(tn(ds, q[tok, :]), SEG)
        mem_v = fold_heads(tn(p.astype(BF), back[tok, :]), SEG)
        spread_heads(spread_a, q[seg, :])
        spread_heads(spread_b, back[seg, :])
        spread_heads(spread_o, mixed[seg, :])
        scores = nt(spread_a[...], k[both, :])
        log = jnp.concatenate([logs[pl.ds(s * SEG, SEG), :][:, h : h + 1] for h in range(heads)], axis=0)
        valid = memory_valid(local, spread, live_ref[s], owner_ref[0])
        p = jnp.where(valid, jnp.exp(jnp.where(valid, scores, FAR) - log), 0.0)
        delta = jnp.sum(
            spread_b[...].astype(F32) * spread_o[...].astype(F32), axis=1, keepdims=True
        )
        ds = (p * (nt(spread_b[...], v[both, :]) - delta)).astype(BF)
        put(0, seg, fold_heads(nn(ds, k[both, :]), SEG) * SCALE)
        grad_k = tn(ds, spread_a[...])
        grad_v = tn(p.astype(BF), spread_b[...])
        put(1, tok, grad_k[:local])
        put(2, tok, grad_v[:local])
        put(1, seg, grad_k[local:] + mem_k)
        put(2, seg, grad_v[local:] + mem_v)
    grads.send()
    normed, inverse = normalize(state[...])
    total = None
    for j in range(4):
        add = nt(grads[:, pl.ds(j * 3 * HW, 3 * HW)], w[j][...])
        total = add if j == 0 else total + add
    gain_sum[...] = jnp.sum(total * normed, axis=0, keepdims=True)
    grad_end[...] = once_rows(share_ref, slots, local, grad_mid[...]) + norm_backward(
        normed, inverse, gain_row(gain, 1, 0), total
    )


def attention1_back(
    slots, local, share, live, owner, gain, grad_mid, state, mixed, logs, q, k, v, probs, weights, w
):
    rows, width = state.shape
    spread = (width // DH) * SEG
    return call(
        functools.partial(attention1_back_kernel, slots, local),
        (
            Away(rows, 3 * width),
            Away(rows, width, dtype=F32),
            like(1, width, dtype=F32),
        ),
        2 * rows * width * 4 * width + 20 * rows * width * spread,
        share,
        live,
        owner,
        gain,
        logs,
        Far(grad_mid),
        *[Far(x, (HW, width), [((pl.ds(0, HW),), ())]) for x in weights],
        *[Far(x) for x in (k, v, probs, q, mixed, state)],
        *[far_qkv(x, width) for x in w],
        scratch=[
            pltpu.VMEM((rows, width), BF),
            pltpu.VMEM((spread, width), BF),
            pltpu.VMEM((spread, width), BF),
            pltpu.VMEM((spread, width), BF),
        ],
        name="attention1_back",
    )


def attention1_weights_kernel(slots, local, share_ref, gain, grad_mid, mixed, state, grads, out):
    low = once_rows(share_ref, slots, local, grad_mid[...].astype(BF))
    grad_out = tn(mixed[...], low)
    normed = (normalize(state[...])[0] * gain_row(gain, 1, 0)).astype(BF)
    for j in range(4):
        out[j, pl.ds(0, HW), :] = grad_out[j * HW : (j + 1) * HW].astype(BF)
        out[j, pl.ds(HW, 3 * HW), :] = tn(grads[:, pl.ds(j * 3 * HW, 3 * HW)], normed).astype(BF)
        out.send(j)


def attention1_weights(slots, local, share, gain, grad_mid, state, mixed, grads, before):
    rows, width = state.shape
    return call(
        functools.partial(attention1_weights_kernel, slots, local),
        (Away(4, 4 * HW, width, blocks=True, before=before),),
        2 * rows * width * 4 * width,
        share,
        gain,
        Far(grad_mid),
        Far(mixed),
        Far(state),
        Far(grads),
        name="attention1_weights",
    )


def on_device(
    tokens, lengths, memory, norm_gain, w_qkv, output_weight, w_up, w_down, cot_tokens, cot_memory
):
    slots, local, width = tokens.shape
    me = lax.axis_index("tensor")
    block = jnp.arange(4, dtype=jnp.int32)
    valid = jnp.clip(lengths[:, None] - (me ^ block)[None, :] * local, 0, local)
    live = valid[:, 0]
    owner = (me == 0).astype(jnp.int32)[None]
    share = (jnp.arange(slots, dtype=jnp.int32) % 4 == me).astype(jnp.int32)

    tok = [Chain(gather_chain(tokens[s])) for s in range(slots)]
    fence(None, tok[0])
    plain = land((output_weight, w_up, w_down, w_qkv), tok[0])
    pack = [jnp.concatenate([w[l] for w in plain[:3]], axis=0) for l in range(2)]
    move0 = Chain(weights_chain(pack[0]))
    move1 = Chain(weights_chain(pack[1]))
    move_attn = Chain(weights_chain(plain[3][1].reshape(3 * width, HW)))
    saved, outs, out_moves = [], [], []
    beside = [[move0], [move_attn], [move0, move_attn, move1]]
    in_flight = [[move0], [move0, move_attn], [move0, move_attn, move1]]
    for s in range(slots):
        finish(tok[s])
        going = tok[s + 1 : s + 2] + beside[s] + out_moves
        received = fence(tok[s].result[1:], *going)
        result = attention0(s, valid[s], tokens, received, memory, norm_gain, w_qkv)
        *out, qa, ka, va = land(result, *tok[s + 1 : s + 2], *in_flight[s], *out_moves)
        saved.append((qa, ka, va))
        outs.append(out)
        out_moves.append(Chain(split_chain(*out[1:])))
    tok_blocks = [t.result[1:] for t in tok]
    fence(None, *out_moves)
    finish(move0, *out_moves)
    weights0 = move0.result
    moved = [m for s in range(slots) for m in out_moves[s].result]
    moved = fence(moved, move_attn, move1)
    result = ffn0(tokens, memory, norm_gain, [o[0] for o in outs], moved, weights0)
    mid0, state1, *hid0, mixed0 = land(result, move_attn, move1)
    finish(move_attn)
    attn1 = move_attn.result
    state1 = fence(state1, move1)
    q1, k1, v1, probs, out_tok, parts = attention1(slots, local, live, owner, state1, norm_gain, attn1)
    parts = Chain(gather_chain(parts))
    finish(parts, move1)
    weights1 = move1.result
    res_tok, res_mem, grads1, grad_mid1, gain_f1, mixed1, logs = ffn1(
        share, live, norm_gain, state1, out_tok, cot_tokens, cot_memory, parts.result, weights1
    )

    proj1, grad1, gain_a1 = attention1_back(
        slots, local, share, live, owner, norm_gain, grad_mid1, state1, mixed1, logs, q1, k1, v1, probs,
        weights1, attn1,
    )
    (grads1,) = attention1_weights(
        slots, local, share, norm_gain, grad_mid1, state1, mixed1, proj1, grads1
    )
    grad1, grads1 = lax.optimization_barrier((grad1, grads1))
    sum1 = lax.psum_scatter(grads1, "tensor", scatter_dimension=0, tiled=False)
    sent0, normed_sum = ffn0_back_sent(norm_gain, grad1, mid0, hid0, weights0)
    sum0 = Chain(core_chain([None, None], sent0))
    normed_sum = fence(normed_sum, sum0)
    kept0, out_kept, out_sent, grad_tok, grad_mem, gain_f0, d_own, *d_moving = land(
        ffn0_back_kept(slots, local, norm_gain, grad1, normed_sum, mid0, hid0, mixed0, weights0), sum0
    )
    d_move = Chain(split_chain(*d_moving))
    late = Chain(core_chain(out_kept, out_sent))
    fence(None, d_move)
    got = sum0.arrived[0]
    sum0 = Chain(cross_chain(added(kept0[0], got[0]), added(kept0[1], got[1])))
    finish(d_move)
    moved = [d_own, *d_move.result]
    before, row_sums = None, []
    for s in range(slots):
        if s == 1:
            finish(late)
            late = Chain(cross_steps(*late.result))
        moved = fence(moved, sum0, late, *row_sums)
        result = attention0_back(
            s, tokens, tok_blocks[s], memory, norm_gain, w_qkv, saved[s], outs[s], moved, before
        )
        if s == 0:
            result, sum1 = lax.optimization_barrier((result, sum1))
            sum1 = lax.psum(sum1, "dp")
        kept, sent, *before = land(result, sum0, late, *row_sums)
        row_sums.append(Chain(rows_chain(kept, sent)))
    grad_qkv0, mem_normed, gain_a0 = before
    small = [mem_normed[:M], grad_mem[:M], gain_a0, gain_a1, gain_f0, gain_f1]
    small.append(jnp.zeros((-(2 * M + 4) % 64, width), F32))
    last = Chain(last_chain(grad_qkv0.astype(BF), jnp.concatenate(small, axis=0), late))
    finish(last, *row_sums, sum0)
    sum0q, small, late = last.result
    sum0 = sum0.result
    rows = []
    for s in range(slots):
        normed, inverse = normalize(tokens[s].astype(F32))
        gain = norm_gain[0, 0].astype(F32)
        rows.append(grad_tok[s] + norm_backward(normed, inverse, gain, row_sums[s].result))
    normed, inverse = normalize(memory.astype(F32))
    grad_memory = small[M : 2 * M] + norm_backward(normed, inverse, gain, small[:M])
    gains = small[2 * M : 2 * M + 4]

    res_mem = res_mem[:, :M]
    res_mem = jnp.where(me % 2 == 0, res_mem, exchange(res_mem, "tensor", 1))
    res_mem = jnp.where(me // 2 == 0, res_mem, exchange(res_mem, "tensor", 2))

    def split_qkv(value):
        return jnp.swapaxes(value.reshape(3, HW, width), 1, 2)

    return (
        res_tok,
        res_mem,
        jnp.stack(rows),
        grad_memory,
        gains[0:2],
        gains[2:4],
        jnp.stack([split_qkv(sum0q), split_qkv(sum1[2 * width + HW :])]).astype(F32),
        jnp.stack([late, sum1[2 * width : 2 * width + HW]]).astype(F32),
        jnp.stack([sum0[:width], sum1[:width]]).astype(F32),
        jnp.stack([sum0[width:], sum1[width : 2 * width]]).astype(F32),
    )


def solution(mesh):
    return jax.shard_map(
        on_device,
        mesh=mesh,
        in_specs=(
            P("dp", "tensor", None),
            P("dp"),
            P(),
            P(),
            P(None, None, None, "tensor"),
            P(None, "tensor", None),
            P(None, None, "tensor"),
            P(None, "tensor", None),
            P("dp", "tensor", None),
            P("dp", None, None),
        ),
        out_specs=(
            P("dp", "tensor", None),
            P("dp", None, None),
            P("dp", "tensor", None),
            P(),
            P(),
            P(),
            P(None, None, None, "tensor"),
            P(None, "tensor", None),
            P(None, None, "tensor"),
            P(None, "tensor", None),
        ),
        check_vma=False,
    )
```

```python
import functools

import jax
import jax.numpy as jnp
from jax import lax
from jax.experimental import pallas as pl
from jax.experimental.pallas import tpu as pltpu
from jax.sharding import PartitionSpec as P

DH = 64
M = 20
SEG = 32
HW = 2 * DH
EPS = 1e-05
SCALE = DH**-0.5
FAR = -1e30
BF = jnp.bfloat16
F32 = jnp.float32


def exchange(value, axis, mask):
    return lax.ppermute(value, axis, [(i, i ^ mask) for i in range(lax.axis_size(axis))])


class Chain:
    def __init__(self, generator):
        self.generator = generator
        self.arrived = None
        self.result = None
        self.wanted = []
        self.done = False

    def ask(self):
        try:
            self.wanted = self.generator.send(self.arrived)
        except StopIteration as stop:
            self.result = stop.value
            self.wanted = []
            self.done = True


def fence(inputs, *chains):
    chains = [c for c in chains if not c.done]
    for chain in chains:
        chain.ask()
    leaving = [[item[0] for item in chain.wanted] for chain in chains]
    if inputs is not None:
        inputs, leaving = lax.optimization_barrier((inputs, leaving))
    for chain, arrays in zip(chains, leaving):
        chain.arrived = [
            exchange(array, item[1], item[2]) for array, item in zip(arrays, chain.wanted)
        ]
    return inputs


def land(outputs, *chains):
    chains = [c for c in chains if not c.done]
    outputs, arrived = lax.optimization_barrier((outputs, [c.arrived for c in chains]))
    for chain, arrays in zip(chains, arrived):
        chain.arrived = arrays
    return outputs


def finish(*chains):
    while not all(c.done for c in chains):
        fence(None, *chains)


def far_chain(block):
    (far,) = yield [(block, "tensor", 2)]
    (last,) = yield [(far, "tensor", 1)]
    return [far, last]


def gather_chain(block):
    near, far = yield [(block, "tensor", 1), (block, "tensor", 2)]
    (last,) = yield [(far, "tensor", 1)]
    return [block, near, far, last]


def weights_chain(block):
    half = block.shape[0] // 2
    bit = lax.axis_index("dp") % 2
    (first,) = yield [(lax.dynamic_slice_in_dim(block, bit * half, half, 0), "tensor", 2)]
    (second,) = yield [(first, "dp", 1)]
    far = jnp.concatenate(
        [jnp.where(bit == 0, first, second), jnp.where(bit == 0, second, first)], axis=0
    )
    last, near = yield [(far, "tensor", 1), (block, "tensor", 1)]
    return [block, near, far, last]


def split_chain(near, pair):
    pair, near = yield [(pair, "tensor", 2), (near, "tensor", 1)]
    (other,) = yield [(pair, "tensor", 1)]
    return [near, pair, other]


def added(a, b):
    return (a.astype(F32) + b.astype(F32)).astype(BF)


def core_chain(kept, sent):
    (got,) = yield [(sent, "tensor", 1)]
    return (added(kept[0], got[0]), added(kept[1], got[1]))


def rows_chain(kept, sent):
    near, far = yield from core_chain(kept, sent)
    (got,) = yield [(far, "tensor", 2)]
    return added(near, got)


def dp_masks():
    size = lax.axis_size("dp")
    masks = []
    while 1 << len(masks) < size:
        masks.append(1 << len(masks))
    return masks


def dp_bit(mask):
    return (lax.axis_index("dp") // mask) % 2


def part(value, mask, other=False):
    half = value.shape[0] // 2
    bit = dp_bit(mask)
    return lax.dynamic_slice_in_dim(value, ((1 - bit) if other else bit) * half, half, 0)


def joined(value, got, mask):
    first = dp_bit(mask) == 0
    return jnp.concatenate([jnp.where(first, value, got), jnp.where(first, got, value)], axis=0)


def reduced(value, masks, whole):
    halves = masks[: len(masks) - whole]
    for mask in halves:
        (got,) = yield [(part(value, mask, True), "dp", mask)]
        value = added(part(value, mask), got)
    for mask in masks[len(halves) :]:
        (got,) = yield [(value, "dp", mask)]
        value = added(value, got)
    for mask in reversed(halves):
        (got,) = yield [(value, "dp", mask)]
        value = joined(value, got, mask)
    return value


def cross_steps(near, far):
    half = near.shape[0] // 2
    near_a, near_b = near[:half], near[half:]
    far_a, far_b = far[:half], far[half:]
    pair = jnp.stack([part(near_b, 1, True), part(far_b, 1, True)])
    got_a, got_b = yield [(far_a, "tensor", 2), (pair, "dp", 1)]
    near_a = added(near_a, got_a)
    near_b = added(part(near_b, 1), got_b[0])
    far_b = added(part(far_b, 1), got_b[1])
    got_a, got_b = yield [(part(near_a, 1, True), "dp", 1), (far_b, "tensor", 2)]
    return jnp.concatenate([added(part(near_a, 1), got_a), added(near_b, got_b)], axis=0)


def cross_joined(value, got):
    half = value.shape[0] // 2
    return jnp.concatenate([joined(value[:half], got[:half], 1), joined(value[half:], got[half:], 1)])


def cross_chain(near, far):
    value = yield from cross_steps(near, far)
    value = yield from reduced(value, dp_masks()[1:], 1)
    (got,) = yield [(value, "dp", 1)]
    return cross_joined(value, got)


def halved(value):
    (got,) = yield [(part(value, 1, True), "dp", 1)]
    return added(part(value, 1), got)


def two_halves(first, second):
    rows = first.shape[0]
    value = jnp.concatenate([first, second])
    value = yield from reduced(value, dp_masks()[1:], 1)
    (got,) = yield [(value, "dp", 1)]
    return jnp.concatenate([joined(value[:rows], got[:rows], 1), joined(value[rows:], got[rows:], 1)])


def last_chain(grad, small):
    (got,) = yield [(small, "tensor", 1)]
    small = small + got
    got, far = yield [(part(grad, 1, True), "dp", 1), (small, "tensor", 2)]
    grad = added(part(grad, 1), got)
    small = small + far
    rows = grad.shape[0]
    value = jnp.concatenate([grad, small.astype(BF)])
    masks = dp_masks()[1:]
    value = yield from reduced(value, masks, len(masks))
    (got,) = yield [(value, "dp", 1)]
    return (joined(value[:rows], got[:rows], 1), value[rows:].astype(F32) + got[rows:].astype(F32))


def nn(a, b):
    return lax.dot_general(a, b, (((1,), (0,)), ((), ())), preferred_element_type=F32)


def nt(a, b):
    return lax.dot_general(a, b, (((1,), (1,)), ((), ())), preferred_element_type=F32)


def tn(a, b):
    return lax.dot_general(a, b, (((0,), (0,)), ((), ())), preferred_element_type=F32)


def normalize(state):
    center = jnp.mean(state, axis=-1, keepdims=True)
    shifted = state - center
    spread = jnp.mean(shifted * shifted, axis=-1, keepdims=True)
    inverse = lax.rsqrt(spread + EPS)
    return (shifted * inverse, inverse)


def norm_backward(normed, inverse, gain_row, grad_normed):
    scaled = grad_normed * gain_row
    return inverse * (
        scaled
        - jnp.mean(scaled, axis=-1, keepdims=True)
        - normed * jnp.mean(scaled * normed, axis=-1, keepdims=True)
    )


def gelu_parts(hidden, with_slope):
    c = 0.7978845608028654
    a = 0.044715
    square = hidden * hidden
    t = jnp.tanh(hidden * (c + (c * a) * square))
    up = 0.5 + 0.5 * t
    active = hidden * up
    if not with_slope:
        return active
    slope = up + hidden * (0.5 - 0.5 * t * t) * (c + (3.0 * c * a) * square)
    return (active, slope)


def iota(shape, axis):
    return lax.broadcasted_iota(jnp.int32, shape, axis)


class Far:
    def __init__(self, array, shape=None, pieces=None):
        self.array = array
        self.shape = array.shape if shape is None else shape
        self.pieces = [((), ())] if pieces is None else pieces


class Away:
    def __init__(self, *shape, dtype=BF):
        self.shape = shape
        self.dtype = dtype


def at(ref, index):
    return ref.at[index] if index else ref


class Incoming:
    def __init__(self, ref, copies):
        self.ref = ref
        self.copies = copies
        self.shape = ref.shape
        for copy in copies:
            copy.start()

    def wait(self):
        for copy in self.copies:
            copy.wait()
        self.copies = []

    def __getitem__(self, index):
        self.wait()
        return self.ref[index]


class Outgoing:
    def __init__(self, ref, copy):
        self.ref = ref
        self.copy = copy
        self.sent = False

    def __setitem__(self, index, value):
        self.ref[index] = value

    def __getitem__(self, index):
        return self.ref[index]

    def send(self):
        if not self.sent:
            self.copy.start()
        self.sent = True


def call(kernel, results, cost, *operands, scratch=(), name=None, limit=60):
    arrays = [o.array if isinstance(o, Far) else o for o in operands]
    specs, buffers, count = [], [], 0
    for o in operands:
        if isinstance(o, Far):
            specs.append(pl.BlockSpec(memory_space=pltpu.HBM))
            buffers.append(pltpu.VMEM(o.shape, o.array.dtype))
            count += len(o.pieces)
        else:
            space = pltpu.SMEM if o.dtype == jnp.int32 else pltpu.VMEM
            specs.append(pl.BlockSpec(memory_space=space))
    out_specs = []
    for r in results:
        away = isinstance(r, Away)
        out_specs.append(pl.BlockSpec(memory_space=pltpu.HBM if away else pltpu.VMEM))
        if away:
            buffers.append(pltpu.VMEM(r.shape, r.dtype))
            count += 1

    def body(*refs):
        ins = refs[: len(operands)]
        outs = refs[len(operands) : len(operands) + len(results)]
        rest = list(refs[len(operands) + len(results) :])
        sem = rest.pop()
        used = iter(range(count))
        local_buffers = iter(rest[: len(buffers)])
        given = []
        for o, ref in zip(operands, ins):
            if isinstance(o, Far):
                buffer = next(local_buffers)
                ref = Incoming(
                    buffer,
                    [
                        pltpu.make_async_copy(at(ref, src), at(buffer, dst), sem.at[next(used)])
                        for src, dst in o.pieces
                    ],
                )
            given.append(ref)
        taken = []
        for r, ref in zip(results, outs):
            if isinstance(r, Away):
                buffer = next(local_buffers)
                ref = Outgoing(buffer, pltpu.make_async_copy(buffer, ref, sem.at[next(used)]))
            taken.append(ref)
        kernel(*given, *taken, *rest[len(buffers) :])
        for ref in given:
            if isinstance(ref, Incoming):
                ref.wait()
        for ref in taken:
            if isinstance(ref, Outgoing):
                ref.send()
        for ref in taken:
            if isinstance(ref, Outgoing):
                ref.copy.wait()

    moved = sum(o.size * o.dtype.itemsize for o in arrays)
    return pl.pallas_call(
        body,
        out_shape=[jax.ShapeDtypeStruct(r.shape, r.dtype) for r in results],
        in_specs=specs,
        out_specs=out_specs,
        scratch_shapes=buffers + list(scratch) + [pltpu.SemaphoreType.DMA((max(count, 1),))],
        compiler_params=pltpu.CompilerParams(vmem_limit_bytes=limit * 1024 * 1024),
        cost_estimate=pl.CostEstimate(flops=cost // 64, bytes_accessed=moved // 64, transcendentals=0),
        name=name,
    )(*arrays)


def like(*shape, dtype=BF):
    return jax.ShapeDtypeStruct(shape, dtype)


def qkv_pieces(sources):
    return [
        (tuple(prefix) + (i,), (slice(None), pl.ds((3 * j + i) * HW, HW)))
        for j, prefix in enumerate(sources)
        for i in range(3)
    ]


def gain_row(gain_ref, layer, which):
    return gain_ref[layer, pl.ds(which, 1), :].astype(F32)


def pad_rows(scratch, value):
    scratch[...] = jnp.zeros_like(scratch)
    scratch[pl.ds(0, value.shape[0]), :] = value.astype(F32)


def head_lanes(rows, h):
    lane = iota((rows, HW), 1)
    inside = (lane >= h * DH) & (lane < (h + 1) * DH)
    return lane - (1 - h) * DH, inside


def attention0_kernel(
    local, valid_ref, mem, gain, x0, x1, x2, x3, w, own, near, pair, qa, ka, va, vh, mem_s
):
    keys = 4 * local + SEG
    tokens = [x0, x1, x2, x3]
    pad_rows(mem_s, mem[...])
    blocks = [(j * local, local, tokens[j]) for j in range(4)] + [(4 * local, SEG, mem_s)]
    for j, (start, size, ref) in enumerate(blocks):
        normed, _ = normalize(ref[...].astype(F32))
        normed = (normed * gain_row(gain, 0, 0)).astype(BF)
        proj = nn(normed, w[...]).astype(BF)
        q = proj[:, :HW] * jnp.asarray(SCALE, BF)
        k = proj[:, HW : 2 * HW]
        v = proj[:, 2 * HW :]
        rows = pl.ds(start, size)
        va[rows, :] = v
        valid = iota((size, HW), 0) < (valid_ref[j] if j < 4 else M)
        bias = jnp.where(valid, 0.0, FAR).astype(BF)
        for h in range(2):
            spare, inside = head_lanes(size, h)
            one = jnp.where(spare == 0, 1.0, 0.0).astype(BF)
            extra = jnp.where((spare >= 1) & (spare <= 3), 1.0, 0.0).astype(BF)
            ka[h, rows, :] = jnp.where(inside, k, jnp.where(spare == 0, bias, extra))
            qa[h, rows, :] = jnp.where(inside, q, one)
            vh[h, rows, :] = jnp.where(inside, v, one)
    ka.send()
    va.send()

    def chunk(start, size):
        rows = pl.ds(start, size)
        out = None
        for h in range(2):
            spare, inside = head_lanes(size, h)
            q = qa[h, rows, :]
            scores = nt(q, ka[h])
            top = jnp.max(scores, axis=1, keepdims=True)
            o = nn(jnp.exp(scores - top).astype(BF), vh[h])
            total = o[:, (1 - h) * DH : (1 - h) * DH + 1]
            col = -(top + jnp.log(total))
            hi = col.astype(BF).astype(F32)
            mid = (col - hi).astype(BF).astype(F32)
            low = col - hi - mid
            extra = jnp.where(spare == 1, hi, jnp.where(spare == 2, mid, jnp.where(spare == 3, low, 0.0)))
            qa[h, rows, :] = jnp.where(inside | (spare == 0), q, extra.astype(BF))
            o = o / total
            out = o if h == 0 else jnp.where(inside, o, out)
        return out.astype(BF)

    out = chunk(4 * local, SEG)
    rows = pl.ds(local, SEG)
    own[rows, :] = out
    near[rows, :] = out
    pair[0, rows, :] = out
    pair[1, rows, :] = out
    rows = pl.ds(0, local)
    out = chunk(2 * local, 2 * local)
    pair[0, rows, :] = out[:local]
    pair[1, rows, :] = out[local:]
    pair.send()
    out = chunk(0, 2 * local)
    own[rows, :] = out[:local]
    near[rows, :] = out[local:]


def pack_weights(out, up, down, qkv):
    parts = [up, down, jnp.concatenate([out[:, i * HW : (i + 1) * HW] for i in range(4)], axis=0)]
    return jnp.concatenate(parts + [qkv[i] for i in range(3)], axis=1)


def packed_out(width):
    lanes = pl.ds(2 * width, HW)
    return [((pl.ds(i * HW, HW), lanes), (pl.ds(0, HW), pl.ds(i * HW, HW))) for i in range(4)]


def packed_ffn(width):
    pieces = [
        ((slice(None), pl.ds(i * width, width)), (pl.ds(HW + i * width, width), slice(None)))
        for i in range(2)
    ]
    return packed_out(width) + pieces


def packed(block, only_out=False):
    width = block.shape[0]
    if only_out:
        return Far(block, (HW, width), packed_out(width))
    return Far(block, (HW + 2 * width, width), packed_ffn(width))


def packed_qkv(block):
    width = block.shape[0]
    return Far(block, (width, 3 * HW), [((slice(None), pl.ds(2 * width + HW, 3 * HW)), ())])


def token_blocks(s, tokens, blocks):
    shape = tokens.shape[1:]
    near, far, last = blocks
    own = Far(tokens, shape, [((s,), ())])
    return [own, Far(near, shape, [((s,), ())]), Far(far), Far(last)]


def attention0(s, valid, tokens, blocks, memory, gain, w_qkv):
    _, local, width = tokens.shape
    keys = 4 * local + SEG
    piece = local + SEG
    cost = 2 * keys * width * 3 * HW + 16 * keys * keys * HW
    return call(
        functools.partial(attention0_kernel, local),
        (
            Away(piece, HW),
            Away(piece, HW),
            Away(2, piece, HW),
            Away(2, keys, HW),
            Away(2, keys, HW),
            Away(keys, HW),
        ),
        cost,
        valid,
        memory,
        gain,
        *token_blocks(s, tokens, blocks),
        Far(w_qkv, (width, 3 * HW), qkv_pieces([(0,)])),
        scratch=[pltpu.VMEM((2, keys, HW), BF), pltpu.VMEM((SEG, width), F32)],
        name="attention0",
    )


def attention0_back_kernel(
    local, first_call, mem, gain, before_mem, before_gain, g_own, g_near, g_far, g_last,
    o_own, o_near, o_pair, va, ka, qa, x1, x3, x0, x2, w, before_w,
    kept, sent, grad_w, mem_normed, gain_sum,
    grads, va_s, da_s, d_s, acc_v, acc_k, mem_s,
):
    keys = 4 * local + SEG
    pad_rows(mem_s, mem[...])
    own = pl.ds(0, local)
    pieces = [
        (0, g_own[own, :], o_own[own, :]),
        (local, g_near[own, :], o_near[own, :]),
        (2 * local, g_far[own, :], o_pair[0, own, :]),
        (3 * local, g_last[own, :], o_pair[1, own, :]),
    ]
    tail = pl.ds(local, SEG)
    parts = [g[tail, :].astype(F32) for g in (g_own, g_near, g_far, g_last)]
    grad = ((parts[0] + parts[1]) + (parts[2] + parts[3])).astype(BF)
    pieces.append((4 * local, grad, o_own[tail, :]))
    for start, grad, out in pieces:
        size = grad.shape[0]
        rows = pl.ds(start, size)
        product = grad.astype(F32) * out.astype(F32)
        d_s[rows, :] = grad
        for h in range(2):
            spare, inside = head_lanes(size, h)
            col = -jnp.sum(jnp.where(inside, product, 0.0), axis=-1, keepdims=True)
            hi = col.astype(BF).astype(F32)
            extra = jnp.where(spare == 0, hi, jnp.where(spare == 1, col - hi, 0.0))
            da_s[h, rows, :] = jnp.where(inside, grad, extra.astype(BF))
    for h in range(2):
        spare, inside = head_lanes(keys, h)
        ones = jnp.where((spare == 0) | (spare == 1), 1.0, 0.0).astype(BF)
        va_s[h] = jnp.where(inside, va[...], ones)
    first = iota((keys, HW), 1) < DH
    key = jnp.where(first, ka[0], ka[1])

    def chunk(start, size, fresh):
        rows = pl.ds(start, size)
        turned = []
        for h in range(2):
            p = jnp.exp(nt(ka[h], qa[h, rows, :]))
            dp = nt(va_s[h], da_s[h, rows, :])
            ds = (p * dp).astype(BF)
            add_v = nn(p.astype(BF), d_s[rows, :])
            add_k = nn(ds, qa[h, rows, :])
            if fresh:
                acc_v[h] = add_v
                acc_k[h] = add_k
            else:
                acc_v[h] += add_v
                acc_k[h] += add_k
            turned.append(tn(ds, key))
        out = jnp.where(iota((size, HW), 1) < DH, turned[0], turned[1]) * SCALE
        grads[rows, :HW] = out.astype(BF)

    chunk(0, 2 * local, True)
    chunk(2 * local, 2 * local, False)
    chunk(4 * local, SEG, False)
    grads[:, HW : 2 * HW] = jnp.where(first, acc_k[0], acc_k[1]).astype(BF)
    grads[:, 2 * HW :] = jnp.where(first, acc_v[0], acc_v[1]).astype(BF)

    tokens = [x0, x1, x2, x3]
    total_w = None if first_call else before_w[...]
    total_gain = None if first_call else before_gain[...]
    for j in (1, 3, 0, 2, 4):
        size = local if j < 4 else SEG
        ref = tokens[j] if j < 4 else mem_s
        normed, _ = normalize(ref[...].astype(F32))
        low = (normed * gain_row(gain, 0, 0)).astype(BF)
        part = grads[pl.ds(j * local, size), :]
        add_w = tn(part, low)
        grad_normed = nt(part, w[...])
        add_gain = jnp.sum(grad_normed * normed, axis=0, keepdims=True)
        total_w = add_w if total_w is None else total_w + add_w
        total_gain = add_gain if total_gain is None else total_gain + add_gain
        if j == 4:
            mem_normed[...] = grad_normed if first_call else grad_normed + before_mem[...]
        else:
            target = kept if j % 2 == 0 else sent
            target[j // 2] = grad_normed.astype(BF)
            if j == 3:
                sent.send()
            if j == 2:
                kept.send()
    grad_w[...] = total_w
    gain_sum[...] = total_gain


def attention0_back(s, tokens, blocks, memory, gain, w_qkv, saved, outs, moved, before):
    slots, local, width = tokens.shape
    keys = 4 * local + SEG
    cost = 4 * keys * width * 3 * HW + 40 * keys * keys * HW
    first_call = before is None
    if first_call:
        before = [jnp.zeros((8, HW), F32)] * 3
    before_w, before_mem, before_gain = before
    qa, ka, va = saved
    block = (local + SEG, HW)
    return call(
        functools.partial(attention0_back_kernel, local, first_call),
        (
            Away(2, local, width),
            Away(2, local, width),
            Away(3 * HW, width, dtype=F32),
            like(SEG, width, dtype=F32),
            like(1, width, dtype=F32),
        ),
        cost,
        memory,
        gain,
        before_mem,
        before_gain,
        *[Far(g, block, [((s,), ())]) for g in moved[:2]],
        Far(moved[2], block, [((0, s), ())]),
        Far(moved[3], block, [((1, s), ())]),
        *[Far(o) for o in outs],
        Far(va),
        Far(ka),
        Far(qa),
        *[token_blocks(s, tokens, blocks)[j] for j in (1, 3, 0, 2)],
        Far(w_qkv, (width, 3 * HW), qkv_pieces([(0,)])),
        Far(before_w),
        scratch=[
            pltpu.VMEM((keys, 3 * HW), BF),
            pltpu.VMEM((2, keys, HW), BF),
            pltpu.VMEM((2, keys, HW), BF),
            pltpu.VMEM((keys, HW), BF),
            pltpu.VMEM((2, keys, HW), F32),
            pltpu.VMEM((2, keys, HW), F32),
            pltpu.VMEM((SEG, width), F32),
        ],
        name="attention0_back",
    )


def ffn0_kernel(slots, local, mem, gain, *refs):
    tokens, own, refs = refs[0], refs[1 : 1 + slots], refs[1 + slots :]
    moved, weights = refs[: 3 * slots], refs[3 * slots : 4 + 3 * slots]
    mid, end, hid0, hid1, hid2, hid3, mixed, normed_s, mem_s = refs[4 + 3 * slots :]
    hid = [hid0, hid1, hid2, hid3]
    piece = local + SEG
    width = gain.shape[2]
    inner = weights[0].shape[0] - HW - width
    pad_rows(mem_s, mem[...])
    for s in range(slots):
        rows = pl.ds(s * piece, piece)
        state = jnp.concatenate([tokens[s].astype(F32), mem_s[...]], axis=0)
        for j in range(4):
            out = own[s][...] if j == 0 else moved[3 * s + j - 1][...]
            mixed[rows, pl.ds(j * HW, HW)] = out
            state += nn(out, weights[j][pl.ds(0, HW), :])
        mid[rows, :] = state
        end[rows, :] = state
        normed_s[rows, :] = (normalize(state)[0] * gain_row(gain, 0, 1)).astype(BF)
    mid.send()
    mixed.send()
    for j in range(4):
        hid[j][...] = nn(normed_s[...], weights[j][pl.ds(HW, width), :]).astype(BF)
        hid[j].send()
    for j in range(4):
        active = gelu_parts(hid[j][...].astype(F32), False).astype(BF)
        end[...] += nn(active, weights[j][pl.ds(HW + width, inner), :])


def ffn0(tokens, memory, gain, own, moved, weights):
    slots, local, width = tokens.shape
    rows = slots * (local + SEG)
    inner = width
    return call(
        functools.partial(ffn0_kernel, slots, local),
        (
            Away(rows, width, dtype=F32),
            Away(rows, width, dtype=F32),
            Away(rows, inner),
            Away(rows, inner),
            Away(rows, inner),
            Away(rows, inner),
            Away(rows, width),
        ),
        2 * rows * width * (width + 8 * inner),
        memory,
        gain,
        Far(tokens),
        *[Far(o) for o in own],
        *[
            Far(m, (local + SEG, HW), [((j,), ())] if m.ndim == 3 else None)
            for near, pair, other in moved
            for m, j in ((near, None), (pair, 0), (other, 1))
        ],
        *[packed(w) for w in weights],
        scratch=[pltpu.VMEM((rows, width), BF), pltpu.VMEM((SEG, width), F32)],
        name="ffn0",
    )


def ffn_back_core(weights, low, low_once, hidden_of, normed, normed_once, targets, with_output):
    width = normed.shape[1]
    inner = weights[targets[0][0]].shape[0] - HW - width
    total, output = None, None
    for j, target, slot in targets:
        up = weights[j][pl.ds(HW, width), :]
        down = weights[j][pl.ds(HW + width, inner), :]
        active, slope = gelu_parts(hidden_of(j), True)
        active = active.astype(BF)
        if with_output:
            add = nn(active, down)
            output = add if output is None else output + add
        grad_hidden = (nt(low, down) * slope).astype(BF)
        target[slot, pl.ds(0, width), :] = tn(normed_once, grad_hidden).astype(BF)
        target[slot, pl.ds(width, inner), :] = tn(active, low_once).astype(BF)
        if slot == 1:
            target.send()
        add = nt(grad_hidden, up)
        total = add if total is None else total + add
    return (total, output)


def once_rows(share_ref, slots, local, value):
    piece = local + SEG
    parts = []
    for s in range(slots):
        parts.append(value[s * piece : s * piece + local])
        tail = value[s * piece + local : (s + 1) * piece]
        parts.append(jnp.where(share_ref[s] > 0, tail, jnp.zeros_like(tail)))
    return jnp.concatenate(parts, axis=0)


def ffn1_kernel(slots, local, share_ref, live_ref, gain, cot_mem, *refs):
    parts, out_tok, cot, state, weights = refs[:4], refs[4], refs[5], refs[6], refs[7:11]
    (res_tok, res_mem, kept, sent, grad_mid, gain_sum, mixed, logs) = refs[11:19]
    normed_s, end_s, low_s, mem_s = refs[19:]
    piece = local + SEG
    width = gain.shape[2]
    heads = width // DH
    gain_f = gain_row(gain, 1, 1)
    lane = iota((SEG, HW), 1)
    mixed_rows = []
    for s in range(slots):
        seg = pl.ds(s * SEG, SEG)
        scale = {}
        log = jnp.zeros((SEG, HW), F32)
        extras = [parts[j][seg, pl.ds(width, HW)] for j in range(4)]
        for h in range(heads):
            source = [2 * ((h // 2) ^ j) + h % 2 for j in range(4)]
            tops = [extras[j][:, source[j] : source[j] + 1] for j in range(4)]
            sums = [extras[j][:, heads + source[j] : heads + source[j] + 1] for j in range(4)]
            peak = functools.reduce(jnp.maximum, tops)
            raised = [jnp.exp(t - peak) for t in tops]
            total = functools.reduce(jnp.add, [r * t for r, t in zip(raised, sums)])
            scale[h] = [r / total for r in raised]
            log = jnp.where(lane == h, peak + jnp.log(total), log)
        logs[seg, :] = log
        for b in range(4):
            merged = jnp.zeros((SEG, HW), F32)
            for j in range(4):
                factor = jnp.where(lane < DH, scale[2 * b][j], scale[2 * b + 1][j])
                merged += factor * parts[j][seg, pl.ds((b ^ j) * HW, HW)]
            mixed[pl.ds(s * piece + local, SEG), pl.ds(b * HW, HW)] = merged.astype(BF)
        rows = pl.ds(s * piece, local)
        mixed[rows, :] = out_tok[s]
        live = iota((local, 1), 0) < live_ref[s]
        low_s[rows, :] = jnp.where(live, cot[s], jnp.zeros_like(cot[s]))
        pad_rows(mem_s, cot_mem[s])
        low_s[pl.ds(s * piece + local, SEG), :] = mem_s[...].astype(BF)
    mixed.send()
    mid = state[...]
    for j in range(4):
        mid += nn(mixed[:, pl.ds(j * HW, HW)], weights[j][pl.ds(0, HW), :])
    end_s[...] = mid
    mid_normed, inverse = normalize(mid)
    normed = (mid_normed * gain_f).astype(BF)
    normed_s[...] = mid_normed
    low = low_s[...]
    grad_normed, output = ffn_back_core(
        weights,
        low,
        once_rows(share_ref, slots, local, low),
        lambda j: nn(normed, weights[j][pl.ds(HW, width), :]),
        normed,
        once_rows(share_ref, slots, local, normed),
        [(1, sent, 0), (3, sent, 1), (0, kept, 0), (2, kept, 1)],
        True,
    )
    end_s[...] += output
    for s in range(slots):
        res_tok[s] = end_s[pl.ds(s * piece, local), :].astype(BF)
        res_mem[s] = end_s[pl.ds(s * piece + local, SEG), :].astype(BF)
    res_tok.send()
    mid_normed = normed_s[...]
    gain_sum[...] = jnp.sum(
        once_rows(share_ref, slots, local, grad_normed * mid_normed), axis=0, keepdims=True
    )
    grad_mid[...] = low_s[...].astype(F32) + norm_backward(mid_normed, inverse, gain_f, grad_normed)


def ffn1(share, live, gain, state, out_tok, cot, cot_mem, parts, weights):
    slots, local, width = cot.shape
    rows = slots * (local + SEG)
    inner = weights[0].shape[0] - HW - width
    return call(
        functools.partial(ffn1_kernel, slots, local),
        (
            Away(slots, local, width),
            like(slots, SEG, width),
            Away(2, width + inner, width),
            Away(2, width + inner, width),
            Away(rows, width, dtype=F32),
            like(1, width, dtype=F32),
            Away(rows, width),
            like(slots * SEG, HW, dtype=F32),
        ),
        2 * rows * width * (width + 24 * inner),
        share,
        live,
        gain,
        cot_mem,
        *[Far(p) for p in parts],
        Far(out_tok),
        Far(cot),
        Far(state),
        *[Far(w) for w in weights],
        scratch=[
            pltpu.VMEM((rows, width), F32),
            pltpu.VMEM((rows, width), F32),
            pltpu.VMEM((rows, width), BF),
            pltpu.VMEM((SEG, width), F32),
        ],
        name="ffn1",
    )


def ffn0_back_sent_kernel(gain, grad_in, mid, hid_near, hid_last, w_near, w_last, sent, normed_sum):
    low = grad_in[...].astype(BF)
    normed = (normalize(mid[...])[0] * gain_row(gain, 0, 1)).astype(BF)
    hidden = {1: hid_near, 3: hid_last}
    normed_sum[...], _ = ffn_back_core(
        {1: w_near, 3: w_last},
        low,
        low,
        lambda j: hidden[j][...].astype(F32),
        normed,
        normed,
        [(1, sent, 0), (3, sent, 1)],
        False,
    )


def ffn0_back_sent(gain, grad_in, mid, hid, weights):
    rows, width = grad_in.shape
    inner = width
    return call(
        ffn0_back_sent_kernel,
        (Away(2, width + inner, width), Away(rows, width, dtype=F32)),
        2 * rows * width * (8 * inner),
        gain,
        Far(grad_in),
        Far(mid),
        Far(hid[1]),
        Far(hid[3]),
        packed(weights[1]),
        packed(weights[3]),
        name="ffn0_back_sent",
    )


def ffn0_back_kept_kernel(
    slots, local, gain, grad_in, mid, hid_own, hid_far, w0, w2, w1, w3, normed_sum, mixed,
    kept, out_kept, out_sent, grad_tok, grad_mem, gain_sum, d_own, d_near, d_pair
):
    weights = [w0, w1, w2, w3]
    piece = local + SEG
    width = gain.shape[2]
    low = grad_in[...].astype(BF)
    mid_normed, inverse = normalize(mid[...])
    normed = (mid_normed * gain_row(gain, 0, 1)).astype(BF)
    hidden = {0: hid_own, 2: hid_far}
    grad_normed, _ = ffn_back_core(
        weights,
        low,
        low,
        lambda j: hidden[j][...].astype(F32),
        normed,
        normed,
        [(0, kept, 0), (2, kept, 1)],
        False,
    )
    grad_normed += normed_sum[...]
    grad = grad_in[...] + norm_backward(mid_normed, inverse, gain_row(gain, 0, 1), grad_normed)
    low = grad.astype(BF)
    for j in (3, 2, 1, 0):
        back = nt(low, weights[j][pl.ds(0, HW), :]).astype(BF)
        for s in range(slots):
            value = back[s * piece : (s + 1) * piece]
            if j >= 2:
                d_pair[j - 2, s] = value
            else:
                (d_own, d_near)[j][s] = value
        if j < 3:
            (d_own, d_near, d_pair)[j].send()
    gain_sum[...] = jnp.sum(grad_normed * mid_normed, axis=0, keepdims=True)
    total = jnp.zeros((SEG, width), F32)
    for s in range(slots):
        grad_tok[s] = grad[s * piece : s * piece + local]
        total += grad[s * piece + local : (s + 1) * piece]
    grad_mem[...] = total
    grad_out = tn(mixed[...], low)
    for j in range(4):
        target = out_kept if j % 2 == 0 else out_sent
        target[j // 2] = grad_out[j * HW : (j + 1) * HW].astype(BF)


def ffn0_back_kept(slots, local, gain, grad_in, normed_sum, mid, hid, mixed, weights):
    rows, width = grad_in.shape
    inner = width
    return call(
        functools.partial(ffn0_back_kept_kernel, slots, local),
        (
            Away(2, width + inner, width),
            Away(2, HW, width),
            Away(2, HW, width),
            Away(slots, local, width, dtype=F32),
            like(SEG, width, dtype=F32),
            like(1, width, dtype=F32),
            Away(slots, local + SEG, HW),
            Away(slots, local + SEG, HW),
            Away(2, slots, local + SEG, HW),
        ),
        2 * rows * width * (2 * width + 8 * inner),
        gain,
        Far(grad_in),
        Far(mid),
        Far(hid[0]),
        Far(hid[2]),
        packed(weights[0]),
        packed(weights[2]),
        *[packed(weights[j], True) for j in (1, 3)],
        Far(normed_sum),
        Far(mixed),
        name="ffn0_back_kept",
    )


def spread_heads(target, value):
    size, width = value.shape
    lane = iota((size, width), 1) // DH
    for h in range(width // DH):
        target[pl.ds(h * size, size), :] = jnp.where(lane == h, value, jnp.zeros_like(value))


def fold_heads(value, size):
    width = value.shape[1]
    lane = iota((size, width), 1) // DH
    total = jnp.zeros((size, width), value.dtype)
    for h in range(width // DH):
        total += jnp.where(lane == h, value[h * size : (h + 1) * size], 0.0)
    return total


def memory_valid(local, rows, live, owner):
    lane = iota((rows, local + SEG), 1)
    return (lane < live) | ((lane >= local) & (lane < local + M) & (owner > 0))


def attention1_kernel(slots, local, live_ref, owner_ref, gain, state, *refs):
    w = refs[:4]
    q_o, k_o, v_o, probs, out_tok, part, spread_k, spread_v = refs[4:]
    piece = local + SEG
    width = gain.shape[2]
    heads = width // DH
    normed = (normalize(state[...])[0] * gain_row(gain, 1, 0)).astype(BF)
    for j in range(4):
        proj = nn(normed, w[j][...]).astype(BF)
        lanes = pl.ds(j * HW, HW)
        q_o[:, lanes] = proj[:, :HW] * jnp.asarray(SCALE, BF)
        k_o[:, lanes] = proj[:, HW : 2 * HW]
        v_o[:, lanes] = proj[:, 2 * HW :]
    for ref in (q_o, k_o, v_o):
        ref.send()
    for s in range(slots):
        tok = pl.ds(s * piece, local)
        seg = pl.ds(s * piece + local, SEG)
        both = pl.ds(s * piece, piece)
        spread_heads(spread_k, q_o[seg, :])
        scores = nt(spread_k[...], k_o[both, :])
        valid = memory_valid(local, heads * SEG, live_ref[s], owner_ref[0])
        scores = jnp.where(valid, scores, FAR)
        top = jnp.max(scores, axis=1, keepdims=True)
        p = jnp.where(valid, jnp.exp(scores - top), 0.0)
        total = jnp.sum(p, axis=1, keepdims=True)
        here = pl.ds(s * SEG, SEG)
        part[here, pl.ds(0, width)] = fold_heads(nn(p.astype(BF), v_o[both, :]), SEG)
        lane = iota((SEG, HW), 1)
        extra = jnp.zeros((SEG, HW), F32)
        for h in range(heads):
            extra = jnp.where(lane == h, top[h * SEG : (h + 1) * SEG], extra)
            extra = jnp.where(lane == heads + h, total[h * SEG : (h + 1) * SEG], extra)
        part[here, pl.ds(width, HW)] = extra
    part.send()
    for s in range(slots):
        tok = pl.ds(s * piece, local)
        seg = pl.ds(s * piece + local, SEG)
        spread_heads(spread_k, k_o[seg, :])
        spread_heads(spread_v, v_o[seg, :])
        st = nt(spread_k[...], q_o[tok, :])
        st = jnp.where(iota((heads * SEG, local), 0) % SEG < M, st, FAR)
        st = st.reshape(heads, SEG, local)
        p = jnp.exp(st - jnp.max(st, axis=1, keepdims=True))
        p = p / jnp.sum(p, axis=1, keepdims=True)
        p = p.reshape(heads * SEG, local).T
        probs[s] = p
        out_tok[s] = nn(p.astype(BF), spread_v[...]).astype(BF)


def attention1(slots, local, live, owner, state, gain, w):
    rows, width = state.shape
    spread = (width // DH) * SEG
    return call(
        functools.partial(attention1_kernel, slots, local),
        (
            Away(rows, width),
            Away(rows, width),
            Away(rows, width),
            Away(slots, local, spread, dtype=F32),
            Away(slots, local, width),
            Away(slots * SEG, width + HW, dtype=F32),
        ),
        2 * rows * width * 3 * width + 8 * rows * width * spread,
        live,
        owner,
        gain,
        Far(state),
        *[packed_qkv(x) for x in w],
        scratch=[pltpu.VMEM((spread, width), BF), pltpu.VMEM((spread, width), BF)],
        name="attention1",
    )


def attention1_back_kernel(
    slots, local, share_ref, live_ref, owner_ref, gain, logs, grad_mid, *refs
):
    weights, (k, v, probs, q, mixed, state), w = refs[:4], refs[4:10], refs[10:14]
    refs = refs[6:]
    grads, grad_end, gain_sum, back, spread_a, spread_b, spread_o = refs[8:]
    piece = local + SEG
    width = gain.shape[2]
    heads = width // DH
    spread = heads * SEG
    low = grad_mid[...].astype(BF)
    for j in range(4):
        back[:, pl.ds(j * HW, HW)] = nt(low, weights[j][pl.ds(0, HW), :]).astype(BF)
    same = (iota((spread, spread), 0) // SEG == iota((spread, spread), 1) // SEG).astype(BF)

    def put(i, at, value):
        value = value.astype(BF)
        for j in range(4):
            grads[at, pl.ds(j * 3 * HW + i * HW, HW)] = value[:, j * HW : (j + 1) * HW]

    for s in range(slots):
        tok = pl.ds(s * piece, local)
        seg = pl.ds(s * piece + local, SEG)
        both = pl.ds(s * piece, piece)
        spread_heads(spread_a, k[seg, :])
        spread_heads(spread_b, v[seg, :])
        p = probs[s]
        dp = nt(back[tok, :], spread_b[...])
        product = p * dp
        hi = product.astype(BF)
        rest = (product - hi.astype(F32)).astype(BF)
        ds = (p * (dp - nn(hi, same) - nn(rest, same))).astype(BF)
        put(0, tok, nn(ds, spread_a[...]) * SCALE)
        mem_k = fold_heads(tn(ds, q[tok, :]), SEG)
        mem_v = fold_heads(tn(p.astype(BF), back[tok, :]), SEG)
        spread_heads(spread_a, q[seg, :])
        spread_heads(spread_b, back[seg, :])
        spread_heads(spread_o, mixed[seg, :])
        scores = nt(spread_a[...], k[both, :])
        log = jnp.concatenate([logs[pl.ds(s * SEG, SEG), :][:, h : h + 1] for h in range(heads)], axis=0)
        valid = memory_valid(local, spread, live_ref[s], owner_ref[0])
        p = jnp.where(valid, jnp.exp(jnp.where(valid, scores, FAR) - log), 0.0)
        delta = jnp.sum(
            spread_b[...].astype(F32) * spread_o[...].astype(F32), axis=1, keepdims=True
        )
        ds = (p * (nt(spread_b[...], v[both, :]) - delta)).astype(BF)
        put(0, seg, fold_heads(nn(ds, k[both, :]), SEG) * SCALE)
        grad_k = tn(ds, spread_a[...])
        grad_v = tn(p.astype(BF), spread_b[...])
        put(1, tok, grad_k[:local])
        put(2, tok, grad_v[:local])
        put(1, seg, grad_k[local:] + mem_k)
        put(2, seg, grad_v[local:] + mem_v)
    grads.send()
    normed, inverse = normalize(state[...])
    total = None
    for j in range(4):
        add = nt(grads[:, pl.ds(j * 3 * HW, 3 * HW)], w[j][...])
        total = add if j == 0 else total + add
    gain_sum[...] = jnp.sum(total * normed, axis=0, keepdims=True)
    grad_end[...] = once_rows(share_ref, slots, local, grad_mid[...]) + norm_backward(
        normed, inverse, gain_row(gain, 1, 0), total
    )


def attention1_back(
    slots, local, share, live, owner, gain, grad_mid, state, mixed, logs, q, k, v, probs, weights, w
):
    rows, width = state.shape
    spread = (width // DH) * SEG
    return call(
        functools.partial(attention1_back_kernel, slots, local),
        (
            Away(rows, 3 * width),
            Away(rows, width, dtype=F32),
            like(1, width, dtype=F32),
        ),
        2 * rows * width * 4 * width + 20 * rows * width * spread,
        share,
        live,
        owner,
        gain,
        logs,
        Far(grad_mid),
        *[Far(x, (HW, width), [((pl.ds(0, HW),), ())]) for x in weights],
        *[Far(x) for x in (k, v, probs, q, mixed, state)],
        *[packed_qkv(x) for x in w],
        scratch=[
            pltpu.VMEM((rows, width), BF),
            pltpu.VMEM((spread, width), BF),
            pltpu.VMEM((spread, width), BF),
            pltpu.VMEM((spread, width), BF),
        ],
        name="attention1_back",
    )


def attention1_weights_kernel(slots, local, share_ref, gain, grad_mid, mixed, state, grads, kept, sent):
    low = once_rows(share_ref, slots, local, grad_mid[...].astype(BF))
    grad_out = tn(mixed[...], low)
    normed = (normalize(state[...])[0] * gain_row(gain, 1, 0)).astype(BF)
    for j in (1, 3, 0, 2):
        target = kept if j % 2 == 0 else sent
        target[j // 2, pl.ds(0, HW), :] = grad_out[j * HW : (j + 1) * HW].astype(BF)
        target[j // 2, pl.ds(HW, 3 * HW), :] = tn(grads[:, pl.ds(j * 3 * HW, 3 * HW)], normed).astype(BF)
        if j == 3:
            sent.send()


def attention1_weights(slots, local, share, gain, grad_mid, state, mixed, grads):
    rows, width = state.shape
    return call(
        functools.partial(attention1_weights_kernel, slots, local),
        (Away(2, 4 * HW, width), Away(2, 4 * HW, width)),
        2 * rows * width * 4 * width,
        share,
        gain,
        Far(grad_mid),
        Far(mixed),
        Far(state),
        Far(grads),
        name="attention1_weights",
    )


def on_device(
    tokens, lengths, memory, norm_gain, w_qkv, output_weight, w_up, w_down, cot_tokens, cot_memory
):
    slots, local, width = tokens.shape
    me = lax.axis_index("tensor")
    block = jnp.arange(4, dtype=jnp.int32)
    valid = jnp.clip(lengths[:, None] - (me ^ block)[None, :] * local, 0, local)
    live = valid[:, 0]
    owner = (me == 0).astype(jnp.int32)[None]
    share = (jnp.arange(slots, dtype=jnp.int32) % 4 == me).astype(jnp.int32)

    near = exchange(tokens, "tensor", 1)
    tok = [Chain(far_chain(tokens[s])) for s in range(slots)]
    fence(None, *tok)
    move0 = Chain(weights_chain(pack_weights(output_weight[0], w_up[0], w_down[0], w_qkv[1])))
    move1 = Chain(weights_chain(jnp.concatenate([output_weight[1], w_up[1], w_down[1]], axis=0)))
    fence(None, tok[0])
    finish(tok[0])
    saved, outs, out_moves = [], [], []
    beside = [[move0], [move1], [move0]]
    for s in range(slots):
        finish(tok[s])
        if s == 0:
            rest = [t.arrived for t in tok[1:]]
            received, rest = fence((tok[s].result, rest), move0)
            for t, arrived in zip(tok[1:], rest):
                t.arrived = arrived
        else:
            received = fence(tok[s].result, *out_moves, *beside[s])
        *out, qa, ka, va = attention0(s, valid[s], tokens, (near, *received), memory, norm_gain, w_qkv)
        out[0] = land(out[0], *tok[s + 1 : s + 2], *([move0, move1] if s == slots - 1 else []))
        saved.append((qa, ka, va))
        outs.append(out)
        out_moves.append(Chain(split_chain(*out[1:])))
    tok_blocks = [(near, *t.result) for t in tok]
    fence(None, *out_moves)
    finish(*out_moves, move0)
    weights0 = move0.result
    moved = [m.result for m in out_moves]
    moved = fence(moved, move1)
    mid0, state1, *hid0, mixed0 = ffn0(
        tokens, memory, norm_gain, [o[0] for o in outs], moved, weights0
    )
    attn1 = weights0
    q1, k1, v1, probs, out_tok, parts = attention1(slots, local, live, owner, state1, norm_gain, attn1)
    probs = land(probs, move1)
    parts = Chain(gather_chain(parts))
    finish(parts, move1)
    weights1 = move1.result
    res_tok, res_mem, kept1, sent1, grad_mid1, gain_f1, mixed1, logs = ffn1(
        share, live, norm_gain, state1, out_tok, cot_tokens, cot_memory, parts.result, weights1
    )

    sum1a = Chain(rows_chain(kept1, sent1))
    grad_mid1 = fence(grad_mid1, sum1a)
    proj1, grad1, gain_a1 = attention1_back(
        slots, local, share, live, owner, norm_gain, grad_mid1, state1, mixed1, logs, q1, k1, v1, probs,
        weights1, attn1,
    )
    proj1, grad1 = fence((proj1, grad1), sum1a)
    kept1, sent1 = attention1_weights(slots, local, share, norm_gain, grad_mid1, state1, mixed1, proj1)
    sum1b = Chain(rows_chain(kept1, sent1))
    grad1 = fence(grad1, sum1b)
    sent0, normed_sum = ffn0_back_sent(norm_gain, grad1, mid0, hid0, weights0)
    sum0 = Chain(core_chain([None, None], sent0))
    finish(sum1a)
    sum1a = Chain(halved(sum1a.result))
    normed_sum = fence(normed_sum, sum0, sum1a, sum1b)
    kept0, out_kept, out_sent, grad_tok, grad_mem, gain_f0, d_own, *d_moving = ffn0_back_kept(
        slots, local, norm_gain, grad1, normed_sum, mid0, hid0, mixed0, weights0
    )
    grad_mem = land(grad_mem, sum0, sum1a, sum1b)
    sum0o = Chain(core_chain(out_kept, out_sent))
    d_move = Chain(split_chain(*d_moving))
    fence(None, d_move)
    finish(sum1a, sum1b)
    sum1b = Chain(halved(sum1b.result))
    fence((), sum1b, sum0o)
    finish(sum0o)
    got = sum0.arrived[0]
    near = jnp.concatenate([added(kept0[0], got[0]), sum0o.result[0]])
    far = jnp.concatenate([added(kept0[1], got[1]), sum0o.result[1]])
    near, far, d_move.arrived = lax.optimization_barrier((near, far, d_move.arrived))
    sum0 = Chain(cross_chain(near, far))
    finish(d_move, sum1b)
    sum1 = Chain(two_halves(sum1a.result, sum1b.result))
    moved = [d_own, *d_move.result]
    before, row_sums = None, []
    for s in range(slots):
        moved = fence(moved, sum0, sum1, *row_sums)
        kept, sent, *before = attention0_back(
            s, tokens, tok_blocks[s], memory, norm_gain, w_qkv, saved[s], outs[s], moved, before
        )
        before[2] = land(before[2], sum0, sum1, *row_sums)
        row_sums.append(Chain(rows_chain(kept, sent)))
    grad_qkv0, mem_normed, gain_a0 = before
    small = [mem_normed[:M], grad_mem[:M], gain_a0, gain_a1, gain_f0, gain_f1]
    last = Chain(last_chain(grad_qkv0.astype(BF), jnp.concatenate(small, axis=0)))
    fence((), last, *row_sums)
    fence((), last, *row_sums, sum0)
    fence((), last, sum1)
    fence((), last, sum0)
    fence((), last)
    finish(last, sum0, sum1, *row_sums)
    sum0q, small = last.result
    sum1 = sum1.result
    sum0 = sum0.result
    rows = []
    for s in range(slots):
        normed, inverse = normalize(tokens[s].astype(F32))
        gain = norm_gain[0, 0].astype(F32)
        total = row_sums[s].result.astype(F32)
        rows.append(grad_tok[s] + norm_backward(normed, inverse, gain, total))
    normed, inverse = normalize(memory.astype(F32))
    grad_memory = small[M : 2 * M] + norm_backward(normed, inverse, gain, small[:M])
    gains = small[2 * M : 2 * M + 4]

    res_mem = res_mem[:, :M]
    res_mem = jnp.where(me % 2 == 0, res_mem, exchange(res_mem, "tensor", 1))
    res_mem = jnp.where(me // 2 == 0, res_mem, exchange(res_mem, "tensor", 2))

    def split_qkv(value):
        return jnp.swapaxes(value.reshape(3, HW, width), 1, 2)

    return (
        res_tok,
        res_mem,
        jnp.stack(rows),
        grad_memory,
        gains[0:2],
        gains[2:4],
        jnp.stack([split_qkv(sum0q), split_qkv(sum1[2 * width + HW :])]).astype(F32),
        jnp.stack([sum0[2 * width :], sum1[2 * width : 2 * width + HW]]).astype(F32),
        jnp.stack([sum0[:width], sum1[:width]]).astype(F32),
        jnp.stack([sum0[width : 2 * width], sum1[width : 2 * width]]).astype(F32),
    )


def solution(mesh):
    return jax.shard_map(
        on_device,
        mesh=mesh,
        in_specs=(
            P("dp", "tensor", None),
            P("dp"),
            P(),
            P(),
            P(None, None, None, "tensor"),
            P(None, "tensor", None),
            P(None, None, "tensor"),
            P(None, "tensor", None),
            P("dp", "tensor", None),
            P("dp", None, None),
        ),
        out_specs=(
            P("dp", "tensor", None),
            P("dp", None, None),
            P("dp", "tensor", None),
            P(),
            P(),
            P(),
            P(None, None, None, "tensor"),
            P(None, "tensor", None),
            P(None, None, "tensor"),
            P(None, "tensor", None),
        ),
        check_vma=False,
    )
```

```python
import functools

import jax
import jax.numpy as jnp
from jax import lax
from jax.experimental import pallas as pl
from jax.experimental.pallas import tpu as pltpu
from jax.sharding import PartitionSpec as P

DH = 64
M = 20
SEG = 32
HW = 2 * DH
EPS = 1e-05
SCALE = DH**-0.5
FAR = -1e30
BF = jnp.bfloat16
F32 = jnp.float32


def exchange(value, axis, mask):
    return lax.ppermute(value, axis, [(i, i ^ mask) for i in range(lax.axis_size(axis))])


class Chain:
    def __init__(self, generator):
        self.generator = generator
        self.arrived = None
        self.result = None
        self.wanted = []
        self.done = False

    def ask(self):
        try:
            self.wanted = self.generator.send(self.arrived)
        except StopIteration as stop:
            self.result = stop.value
            self.wanted = []
            self.done = True


def fence(inputs, *chains):
    chains = [c for c in chains if not c.done]
    for chain in chains:
        chain.ask()
    leaving = [[item[0] for item in chain.wanted] for chain in chains]
    if inputs is not None:
        inputs, leaving = lax.optimization_barrier((inputs, leaving))
    for chain, arrays in zip(chains, leaving):
        chain.arrived = [
            exchange(array, item[1], item[2]) for array, item in zip(arrays, chain.wanted)
        ]
    return inputs


def land(outputs, *chains):
    chains = [c for c in chains if not c.done]
    outputs, arrived = lax.optimization_barrier((outputs, [c.arrived for c in chains]))
    for chain, arrays in zip(chains, arrived):
        chain.arrived = arrays
    return outputs


def finish(*chains):
    while not all(c.done for c in chains):
        fence(None, *chains)


def far_chain(block):
    (far,) = yield [(block, "tensor", 2)]
    (last,) = yield [(far, "tensor", 1)]
    return [far, last]


def gather_chain(block):
    near, far = yield [(block, "tensor", 1), (block, "tensor", 2)]
    (last,) = yield [(far, "tensor", 1)]
    return [block, near, far, last]


def weights_chain(block):
    half = block.shape[0] // 2
    bit = lax.axis_index("dp") % 2
    (first,) = yield [(lax.dynamic_slice_in_dim(block, bit * half, half, 0), "tensor", 2)]
    (second,) = yield [(first, "dp", 1)]
    far = jnp.concatenate(
        [jnp.where(bit == 0, first, second), jnp.where(bit == 0, second, first)], axis=0
    )
    last, near = yield [(far, "tensor", 1), (block, "tensor", 1)]
    return [block, near, far, last]


def split_chain(near, pair):
    pair, near = yield [(pair, "tensor", 2), (near, "tensor", 1)]
    (other,) = yield [(pair, "tensor", 1)]
    return [near, pair, other]


def added(a, b):
    return (a.astype(F32) + b.astype(F32)).astype(BF)


def core_chain(kept, sent):
    (got,) = yield [(sent, "tensor", 1)]
    return (added(kept[0], got[0]), added(kept[1], got[1]))


def rows_chain(kept, sent):
    near, far = yield from core_chain(kept, sent)
    (got,) = yield [(far, "tensor", 2)]
    return added(near, got)


def dp_masks():
    size = lax.axis_size("dp")
    masks = []
    while 1 << len(masks) < size:
        masks.append(1 << len(masks))
    return masks


def dp_bit(mask):
    return (lax.axis_index("dp") // mask) % 2


def part(value, mask, other=False):
    half = value.shape[0] // 2
    bit = dp_bit(mask)
    return lax.dynamic_slice_in_dim(value, ((1 - bit) if other else bit) * half, half, 0)


def joined(value, got, mask):
    first = dp_bit(mask) == 0
    return jnp.concatenate([jnp.where(first, value, got), jnp.where(first, got, value)], axis=0)


def reduced(value, masks, whole):
    halves = masks[: len(masks) - whole]
    for mask in halves:
        (got,) = yield [(part(value, mask, True), "dp", mask)]
        value = added(part(value, mask), got)
    for mask in masks[len(halves) :]:
        (got,) = yield [(value, "dp", mask)]
        value = added(value, got)
    for mask in reversed(halves):
        (got,) = yield [(value, "dp", mask)]
        value = joined(value, got, mask)
    return value


def cross_steps(near, far):
    half = near.shape[0] // 2
    near_a, near_b = near[:half], near[half:]
    far_a, far_b = far[:half], far[half:]
    pair = jnp.stack([part(near_b, 1, True), part(far_b, 1, True)])
    got_a, got_b = yield [(far_a, "tensor", 2), (pair, "dp", 1)]
    near_a = added(near_a, got_a)
    near_b = added(part(near_b, 1), got_b[0])
    far_b = added(part(far_b, 1), got_b[1])
    got_a, got_b = yield [(part(near_a, 1, True), "dp", 1), (far_b, "tensor", 2)]
    return jnp.concatenate([added(part(near_a, 1), got_a), added(near_b, got_b)], axis=0)


def cross_joined(value, got):
    half = value.shape[0] // 2
    return jnp.concatenate([joined(value[:half], got[:half], 1), joined(value[half:], got[half:], 1)])


def cross_chain(near, far):
    value = yield from cross_steps(near, far)
    value = yield from reduced(value, dp_masks()[1:], 1)
    (got,) = yield [(value, "dp", 1)]
    return cross_joined(value, got)


def halved(value):
    (got,) = yield [(part(value, 1, True), "dp", 1)]
    return added(part(value, 1), got)


def two_halves(first, second):
    rows = first.shape[0]
    value = jnp.concatenate([first, second])
    value = yield from reduced(value, dp_masks()[1:], 1)
    (got,) = yield [(value, "dp", 1)]
    return jnp.concatenate([joined(value[:rows], got[:rows], 1), joined(value[rows:], got[rows:], 1)])


def copy_chain(value):
    me = lax.axis_index("tensor")
    (got,) = yield [(value, "tensor", 2)]
    value = jnp.where(me // 2 == 0, value, got)
    (got,) = yield [(value, "tensor", 1)]
    return jnp.where(me % 2 == 0, value, got)


def last_chain(grad, small):
    (got,) = yield [(small, "tensor", 1)]
    small = small + got
    got, far = yield [(part(grad, 1, True), "dp", 1), (small, "tensor", 2)]
    grad = added(part(grad, 1), got)
    small = small + far
    rows = grad.shape[0]
    value = jnp.concatenate([grad, small.astype(BF)])
    masks = dp_masks()[1:]
    value = yield from reduced(value, masks, len(masks))
    (got,) = yield [(value, "dp", 1)]
    return (joined(value[:rows], got[:rows], 1), value[rows:].astype(F32) + got[rows:].astype(F32))


def nn(a, b):
    return lax.dot_general(a, b, (((1,), (0,)), ((), ())), preferred_element_type=F32)


def nt(a, b):
    return lax.dot_general(a, b, (((1,), (1,)), ((), ())), preferred_element_type=F32)


def tn(a, b):
    return lax.dot_general(a, b, (((0,), (0,)), ((), ())), preferred_element_type=F32)


def normalize(state):
    center = jnp.mean(state, axis=-1, keepdims=True)
    shifted = state - center
    spread = jnp.mean(shifted * shifted, axis=-1, keepdims=True)
    inverse = lax.rsqrt(spread + EPS)
    return (shifted * inverse, inverse)


def norm_backward(normed, inverse, gain_row, grad_normed):
    scaled = grad_normed * gain_row
    return inverse * (
        scaled
        - jnp.mean(scaled, axis=-1, keepdims=True)
        - normed * jnp.mean(scaled * normed, axis=-1, keepdims=True)
    )


def gelu_parts(hidden, with_slope):
    c = 0.7978845608028654
    a = 0.044715
    square = hidden * hidden
    t = jnp.tanh(hidden * (c + (c * a) * square))
    up = 0.5 + 0.5 * t
    active = hidden * up
    if not with_slope:
        return active
    slope = up + hidden * (0.5 - 0.5 * t * t) * (c + (3.0 * c * a) * square)
    return (active, slope)


def iota(shape, axis):
    return lax.broadcasted_iota(jnp.int32, shape, axis)


class Far:
    def __init__(self, array, shape=None, pieces=None):
        self.array = array
        self.shape = array.shape if shape is None else shape
        self.pieces = [((), ())] if pieces is None else pieces


class Away:
    def __init__(self, *shape, dtype=BF):
        self.shape = shape
        self.dtype = dtype


def at(ref, index):
    return ref.at[index] if index else ref


class Incoming:
    def __init__(self, ref, copies):
        self.ref = ref
        self.copies = copies
        self.shape = ref.shape
        for copy in copies:
            copy.start()

    def wait(self):
        for copy in self.copies:
            copy.wait()
        self.copies = []

    def __getitem__(self, index):
        self.wait()
        return self.ref[index]


class Outgoing:
    def __init__(self, ref, copy):
        self.ref = ref
        self.copy = copy
        self.sent = False

    def __setitem__(self, index, value):
        self.ref[index] = value

    def __getitem__(self, index):
        return self.ref[index]

    def send(self):
        if not self.sent:
            self.copy.start()
        self.sent = True


def call(kernel, results, cost, *operands, scratch=(), name=None, limit=60):
    arrays = [o.array if isinstance(o, Far) else o for o in operands]
    specs, buffers, count = [], [], 0
    for o in operands:
        if isinstance(o, Far):
            specs.append(pl.BlockSpec(memory_space=pltpu.HBM))
            buffers.append(pltpu.VMEM(o.shape, o.array.dtype))
            count += len(o.pieces)
        else:
            space = pltpu.SMEM if o.dtype == jnp.int32 else pltpu.VMEM
            specs.append(pl.BlockSpec(memory_space=space))
    out_specs = []
    for r in results:
        away = isinstance(r, Away)
        out_specs.append(pl.BlockSpec(memory_space=pltpu.HBM if away else pltpu.VMEM))
        if away:
            buffers.append(pltpu.VMEM(r.shape, r.dtype))
            count += 1

    def body(*refs):
        ins = refs[: len(operands)]
        outs = refs[len(operands) : len(operands) + len(results)]
        rest = list(refs[len(operands) + len(results) :])
        sem = rest.pop()
        used = iter(range(count))
        local_buffers = iter(rest[: len(buffers)])
        given = []
        for o, ref in zip(operands, ins):
            if isinstance(o, Far):
                buffer = next(local_buffers)
                ref = Incoming(
                    buffer,
                    [
                        pltpu.make_async_copy(at(ref, src), at(buffer, dst), sem.at[next(used)])
                        for src, dst in o.pieces
                    ],
                )
            given.append(ref)
        taken = []
        for r, ref in zip(results, outs):
            if isinstance(r, Away):
                buffer = next(local_buffers)
                ref = Outgoing(buffer, pltpu.make_async_copy(buffer, ref, sem.at[next(used)]))
            taken.append(ref)
        kernel(*given, *taken, *rest[len(buffers) :])
        for ref in given:
            if isinstance(ref, Incoming):
                ref.wait()
        for ref in taken:
            if isinstance(ref, Outgoing):
                ref.send()
        for ref in taken:
            if isinstance(ref, Outgoing):
                ref.copy.wait()

    moved = sum(o.size * o.dtype.itemsize for o in arrays)
    return pl.pallas_call(
        body,
        out_shape=[jax.ShapeDtypeStruct(r.shape, r.dtype) for r in results],
        in_specs=specs,
        out_specs=out_specs,
        scratch_shapes=buffers + list(scratch) + [pltpu.SemaphoreType.DMA((max(count, 1),))],
        compiler_params=pltpu.CompilerParams(vmem_limit_bytes=limit * 1024 * 1024),
        cost_estimate=pl.CostEstimate(flops=cost // 64, bytes_accessed=moved // 64, transcendentals=0),
        name=name,
    )(*arrays)


def like(*shape, dtype=BF):
    return jax.ShapeDtypeStruct(shape, dtype)


def qkv_pieces(sources):
    return [
        (tuple(prefix) + (i,), (slice(None), pl.ds((3 * j + i) * HW, HW)))
        for j, prefix in enumerate(sources)
        for i in range(3)
    ]


def gain_row(gain_ref, layer, which):
    return gain_ref[layer, pl.ds(which, 1), :].astype(F32)


def pad_rows(scratch, value):
    scratch[...] = jnp.zeros_like(scratch)
    scratch[pl.ds(0, value.shape[0]), :] = value.astype(F32)


def head_lanes(rows, h):
    lane = iota((rows, HW), 1)
    inside = (lane >= h * DH) & (lane < (h + 1) * DH)
    return lane - (1 - h) * DH, inside


def attention0_kernel(
    local, valid_ref, mem, gain, x0, x1, x2, x3, w, own, near, pair, qa, ka, va, vh, mem_s
):
    keys = 4 * local + SEG
    tokens = [x0, x1, x2, x3]
    pad_rows(mem_s, mem[...])
    blocks = [(j * local, local, tokens[j]) for j in range(4)] + [(4 * local, SEG, mem_s)]
    for j, (start, size, ref) in enumerate(blocks):
        normed, _ = normalize(ref[...].astype(F32))
        normed = (normed * gain_row(gain, 0, 0)).astype(BF)
        proj = nn(normed, w[...]).astype(BF)
        q = proj[:, :HW] * jnp.asarray(SCALE, BF)
        k = proj[:, HW : 2 * HW]
        v = proj[:, 2 * HW :]
        rows = pl.ds(start, size)
        va[rows, :] = v
        valid = iota((size, HW), 0) < (valid_ref[j] if j < 4 else M)
        bias = jnp.where(valid, 0.0, FAR).astype(BF)
        for h in range(2):
            spare, inside = head_lanes(size, h)
            one = jnp.where(spare == 0, 1.0, 0.0).astype(BF)
            extra = jnp.where((spare >= 1) & (spare <= 3), 1.0, 0.0).astype(BF)
            ka[h, rows, :] = jnp.where(inside, k, jnp.where(spare == 0, bias, extra))
            qa[h, rows, :] = jnp.where(inside, q, one)
            vh[h, rows, :] = jnp.where(inside, v, one)
    ka.send()
    va.send()

    def chunk(start, size):
        rows = pl.ds(start, size)
        out = None
        for h in range(2):
            spare, inside = head_lanes(size, h)
            q = qa[h, rows, :]
            scores = nt(q, ka[h])
            top = jnp.max(scores, axis=1, keepdims=True)
            o = nn(jnp.exp(scores - top).astype(BF), vh[h])
            total = o[:, (1 - h) * DH : (1 - h) * DH + 1]
            col = -(top + jnp.log(total))
            hi = col.astype(BF).astype(F32)
            mid = (col - hi).astype(BF).astype(F32)
            low = col - hi - mid
            extra = jnp.where(spare == 1, hi, jnp.where(spare == 2, mid, jnp.where(spare == 3, low, 0.0)))
            qa[h, rows, :] = jnp.where(inside | (spare == 0), q, extra.astype(BF))
            o = o / total
            out = o if h == 0 else jnp.where(inside, o, out)
        return out.astype(BF)

    out = chunk(4 * local, SEG)
    rows = pl.ds(local, SEG)
    own[rows, :] = out
    near[rows, :] = out
    pair[0, rows, :] = out
    pair[1, rows, :] = out
    rows = pl.ds(0, local)
    out = chunk(2 * local, 2 * local)
    pair[0, rows, :] = out[:local]
    pair[1, rows, :] = out[local:]
    pair.send()
    out = chunk(0, 2 * local)
    own[rows, :] = out[:local]
    near[rows, :] = out[local:]


def pack_weights(out, up, down, qkv):
    parts = [up, down, jnp.concatenate([out[:, i * HW : (i + 1) * HW] for i in range(4)], axis=0)]
    return jnp.concatenate(parts + [qkv[i] for i in range(3)], axis=1)


def packed_out(width):
    lanes = pl.ds(2 * width, HW)
    return [((pl.ds(i * HW, HW), lanes), (pl.ds(0, HW), pl.ds(i * HW, HW))) for i in range(4)]


def packed_ffn(width):
    pieces = [
        ((slice(None), pl.ds(i * width, width)), (pl.ds(HW + i * width, width), slice(None)))
        for i in range(2)
    ]
    return packed_out(width) + pieces


def packed(block, only_out=False):
    width = block.shape[0]
    if only_out:
        return Far(block, (HW, width), packed_out(width))
    return Far(block, (HW + 2 * width, width), packed_ffn(width))


def packed_qkv(block):
    width = block.shape[0]
    return Far(block, (width, 3 * HW), [((slice(None), pl.ds(2 * width + HW, 3 * HW)), ())])


def token_blocks(s, tokens, blocks):
    shape = tokens.shape[1:]
    near, far, last = blocks
    own = Far(tokens, shape, [((s,), ())])
    return [own, Far(near, shape, [((s,), ())]), Far(far), Far(last)]


def attention0(s, valid, tokens, blocks, memory, gain, w_qkv):
    _, local, width = tokens.shape
    keys = 4 * local + SEG
    piece = local + SEG
    cost = 2 * keys * width * 3 * HW + 16 * keys * keys * HW
    return call(
        functools.partial(attention0_kernel, local),
        (
            Away(piece, HW),
            Away(piece, HW),
            Away(2, piece, HW),
            Away(2, keys, HW),
            Away(2, keys, HW),
            Away(keys, HW),
        ),
        cost,
        valid,
        memory,
        gain,
        *token_blocks(s, tokens, blocks),
        Far(w_qkv, (width, 3 * HW), qkv_pieces([(0,)])),
        scratch=[pltpu.VMEM((2, keys, HW), BF), pltpu.VMEM((SEG, width), F32)],
        name="attention0",
    )


def attention0_back_kernel(
    local, first_call, last_call, mem, gain, before_mem, before_gain, g_own, g_near, g_far, g_last,
    o_own, o_near, o_pair, va, ka, qa, x1, x3, x0, x2, w, before_w,
    kept, sent, grad_w, mem_normed, gain_sum,
    grads, va_s, da_s, d_s, acc_v, acc_k, mem_s,
):
    keys = 4 * local + SEG
    pad_rows(mem_s, mem[...])
    own = pl.ds(0, local)
    pieces = [
        (0, g_own[own, :], o_own[own, :]),
        (local, g_near[own, :], o_near[own, :]),
        (2 * local, g_far[own, :], o_pair[0, own, :]),
        (3 * local, g_last[own, :], o_pair[1, own, :]),
    ]
    tail = pl.ds(local, SEG)
    parts = [g[tail, :].astype(F32) for g in (g_own, g_near, g_far, g_last)]
    grad = ((parts[0] + parts[1]) + (parts[2] + parts[3])).astype(BF)
    pieces.append((4 * local, grad, o_own[tail, :]))
    for start, grad, out in pieces:
        size = grad.shape[0]
        rows = pl.ds(start, size)
        product = grad.astype(F32) * out.astype(F32)
        d_s[rows, :] = grad
        for h in range(2):
            spare, inside = head_lanes(size, h)
            col = -jnp.sum(jnp.where(inside, product, 0.0), axis=-1, keepdims=True)
            hi = col.astype(BF).astype(F32)
            extra = jnp.where(spare == 0, hi, jnp.where(spare == 1, col - hi, 0.0))
            da_s[h, rows, :] = jnp.where(inside, grad, extra.astype(BF))
    for h in range(2):
        spare, inside = head_lanes(keys, h)
        ones = jnp.where((spare == 0) | (spare == 1), 1.0, 0.0).astype(BF)
        va_s[h] = jnp.where(inside, va[...], ones)
    first = iota((keys, HW), 1) < DH
    key = jnp.where(first, ka[0], ka[1])

    def chunk(start, size, fresh):
        rows = pl.ds(start, size)
        turned = []
        for h in range(2):
            p = jnp.exp(nt(ka[h], qa[h, rows, :]))
            dp = nt(va_s[h], da_s[h, rows, :])
            ds = (p * dp).astype(BF)
            add_v = nn(p.astype(BF), d_s[rows, :])
            add_k = nn(ds, qa[h, rows, :])
            if fresh:
                acc_v[h] = add_v
                acc_k[h] = add_k
            else:
                acc_v[h] += add_v
                acc_k[h] += add_k
            turned.append(tn(ds, key))
        out = jnp.where(iota((size, HW), 1) < DH, turned[0], turned[1]) * SCALE
        grads[rows, :HW] = out.astype(BF)

    chunk(0, 2 * local, True)
    chunk(2 * local, 2 * local, False)
    chunk(4 * local, SEG, False)
    grads[:, HW : 2 * HW] = jnp.where(first, acc_k[0], acc_k[1]).astype(BF)
    grads[:, 2 * HW :] = jnp.where(first, acc_v[0], acc_v[1]).astype(BF)

    tokens = [x0, x1, x2, x3]
    total_w = None if first_call else before_w[...]
    total_gain = None if first_call else before_gain[...]
    for j in (1, 3, 0, 2, 4):
        size = local if j < 4 else SEG
        ref = tokens[j] if j < 4 else mem_s
        normed, _ = normalize(ref[...].astype(F32))
        low = (normed * gain_row(gain, 0, 0)).astype(BF)
        part = grads[pl.ds(j * local, size), :]
        add_w = tn(part, low)
        grad_normed = nt(part, w[...])
        add_gain = jnp.sum(grad_normed * normed, axis=0, keepdims=True)
        total_w = add_w if total_w is None else total_w + add_w
        total_gain = add_gain if total_gain is None else total_gain + add_gain
        if j == 4:
            mem_normed[...] = grad_normed if first_call else grad_normed + before_mem[...]
        else:
            target = kept if j % 2 == 0 else sent
            target[j // 2] = grad_normed.astype(BF)
            if j == 3:
                sent.send()
            if j == 2:
                kept.send()
    grad_w[...] = total_w.astype(BF if last_call else F32)
    gain_sum[...] = total_gain


def attention0_back(s, tokens, blocks, memory, gain, w_qkv, saved, outs, moved, before):
    slots, local, width = tokens.shape
    keys = 4 * local + SEG
    cost = 4 * keys * width * 3 * HW + 40 * keys * keys * HW
    first_call, last_call = before is None, s == slots - 1
    if first_call:
        before = [jnp.zeros((8, HW), F32)] * 3
    before_w, before_mem, before_gain = before
    qa, ka, va = saved
    block = (local + SEG, HW)
    return call(
        functools.partial(attention0_back_kernel, local, first_call, last_call),
        (
            Away(2, local, width),
            Away(2, local, width),
            Away(3 * HW, width, dtype=BF if last_call else F32),
            like(SEG, width, dtype=F32),
            like(1, width, dtype=F32),
        ),
        cost,
        memory,
        gain,
        before_mem,
        before_gain,
        *[Far(g, block, [((s,), ())]) for g in moved[:2]],
        Far(moved[2], block, [((0, s), ())]),
        Far(moved[3], block, [((1, s), ())]),
        *[Far(o) for o in outs],
        Far(va),
        Far(ka),
        Far(qa),
        *[token_blocks(s, tokens, blocks)[j] for j in (1, 3, 0, 2)],
        Far(w_qkv, (width, 3 * HW), qkv_pieces([(0,)])),
        Far(before_w),
        scratch=[
            pltpu.VMEM((keys, 3 * HW), BF),
            pltpu.VMEM((2, keys, HW), BF),
            pltpu.VMEM((2, keys, HW), BF),
            pltpu.VMEM((keys, HW), BF),
            pltpu.VMEM((2, keys, HW), F32),
            pltpu.VMEM((2, keys, HW), F32),
            pltpu.VMEM((SEG, width), F32),
        ],
        name="attention0_back",
    )


def ffn0_kernel(slots, local, mem, gain, *refs):
    tokens, own, refs = refs[0], refs[1 : 1 + slots], refs[1 + slots :]
    moved, weights = refs[: 3 * slots], refs[3 * slots : 4 + 3 * slots]
    mid, end, hid0, hid1, hid2, hid3, mixed, normed_s, mem_s = refs[4 + 3 * slots :]
    hid = [hid0, hid1, hid2, hid3]
    piece = local + SEG
    width = gain.shape[2]
    inner = weights[0].shape[0] - HW - width
    pad_rows(mem_s, mem[...])
    for s in range(slots):
        rows = pl.ds(s * piece, piece)
        state = jnp.concatenate([tokens[s].astype(F32), mem_s[...]], axis=0)
        for j in range(4):
            out = own[s][...] if j == 0 else moved[3 * s + j - 1][...]
            mixed[rows, pl.ds(j * HW, HW)] = out
            state += nn(out, weights[j][pl.ds(0, HW), :])
        mid[rows, :] = state
        end[rows, :] = state
        normed_s[rows, :] = (normalize(state)[0] * gain_row(gain, 0, 1)).astype(BF)
    mid.send()
    mixed.send()
    for j in range(4):
        hid[j][...] = nn(normed_s[...], weights[j][pl.ds(HW, width), :]).astype(BF)
        hid[j].send()
    for j in range(4):
        active = gelu_parts(hid[j][...].astype(F32), False).astype(BF)
        end[...] += nn(active, weights[j][pl.ds(HW + width, inner), :])


def ffn0(tokens, memory, gain, own, moved, weights):
    slots, local, width = tokens.shape
    rows = slots * (local + SEG)
    inner = width
    return call(
        functools.partial(ffn0_kernel, slots, local),
        (
            Away(rows, width, dtype=F32),
            Away(rows, width, dtype=F32),
            Away(rows, inner),
            Away(rows, inner),
            Away(rows, inner),
            Away(rows, inner),
            Away(rows, width),
        ),
        2 * rows * width * (width + 8 * inner),
        memory,
        gain,
        Far(tokens),
        *[Far(o) for o in own],
        *[
            Far(m, (local + SEG, HW), [((j,), ())] if m.ndim == 3 else None)
            for near, pair, other in moved
            for m, j in ((near, None), (pair, 0), (other, 1))
        ],
        *[packed(w) for w in weights],
        scratch=[pltpu.VMEM((rows, width), BF), pltpu.VMEM((SEG, width), F32)],
        name="ffn0",
    )


def ffn_back_core(weights, low, low_once, hidden_of, normed, normed_once, targets, with_output):
    width = normed.shape[1]
    inner = weights[targets[0][0]].shape[0] - HW - width
    total, output = None, None
    for j, target, slot in targets:
        up = weights[j][pl.ds(HW, width), :]
        down = weights[j][pl.ds(HW + width, inner), :]
        active, slope = gelu_parts(hidden_of(j), True)
        active = active.astype(BF)
        if with_output:
            add = nn(active, down)
            output = add if output is None else output + add
        grad_hidden = (nt(low, down) * slope).astype(BF)
        target[slot, pl.ds(0, width), :] = tn(normed_once, grad_hidden).astype(BF)
        target[slot, pl.ds(width, inner), :] = tn(active, low_once).astype(BF)
        if slot == 1:
            target.send()
        add = nt(grad_hidden, up)
        total = add if total is None else total + add
    return (total, output)


def once_rows(share_ref, slots, local, value):
    piece = local + SEG
    parts = []
    for s in range(slots):
        parts.append(value[s * piece : s * piece + local])
        tail = value[s * piece + local : (s + 1) * piece]
        parts.append(jnp.where(share_ref[s] > 0, tail, jnp.zeros_like(tail)))
    return jnp.concatenate(parts, axis=0)


def ffn1_kernel(slots, local, share_ref, live_ref, gain, cot_mem, *refs):
    parts, out_tok, cot, state, weights = refs[:4], refs[4], refs[5], refs[6], refs[7:11]
    (res_tok, res_mem, kept, sent, grad_mid, gain_sum, mixed, logs) = refs[11:19]
    normed_s, end_s, low_s, mem_s = refs[19:]
    piece = local + SEG
    width = gain.shape[2]
    heads = width // DH
    gain_f = gain_row(gain, 1, 1)
    lane = iota((SEG, HW), 1)
    mixed_rows = []
    for s in range(slots):
        seg = pl.ds(s * SEG, SEG)
        scale = {}
        log = jnp.zeros((SEG, HW), F32)
        extras = [parts[j][seg, pl.ds(width, HW)] for j in range(4)]
        for h in range(heads):
            source = [2 * ((h // 2) ^ j) + h % 2 for j in range(4)]
            tops = [extras[j][:, source[j] : source[j] + 1] for j in range(4)]
            sums = [extras[j][:, heads + source[j] : heads + source[j] + 1] for j in range(4)]
            peak = functools.reduce(jnp.maximum, tops)
            raised = [jnp.exp(t - peak) for t in tops]
            total = functools.reduce(jnp.add, [r * t for r, t in zip(raised, sums)])
            scale[h] = [r / total for r in raised]
            log = jnp.where(lane == h, peak + jnp.log(total), log)
        logs[seg, :] = log
        for b in range(4):
            merged = jnp.zeros((SEG, HW), F32)
            for j in range(4):
                factor = jnp.where(lane < DH, scale[2 * b][j], scale[2 * b + 1][j])
                merged += factor * parts[j][seg, pl.ds((b ^ j) * HW, HW)]
            mixed[pl.ds(s * piece + local, SEG), pl.ds(b * HW, HW)] = merged.astype(BF)
        rows = pl.ds(s * piece, local)
        mixed[rows, :] = out_tok[s]
        live = iota((local, 1), 0) < live_ref[s]
        low_s[rows, :] = jnp.where(live, cot[s], jnp.zeros_like(cot[s]))
        pad_rows(mem_s, cot_mem[s])
        low_s[pl.ds(s * piece + local, SEG), :] = mem_s[...].astype(BF)
    mixed.send()
    mid = state[...]
    for j in range(4):
        mid += nn(mixed[:, pl.ds(j * HW, HW)], weights[j][pl.ds(0, HW), :])
    end_s[...] = mid
    mid_normed, inverse = normalize(mid)
    normed = (mid_normed * gain_f).astype(BF)
    normed_s[...] = mid_normed
    low = low_s[...]
    grad_normed, output = ffn_back_core(
        weights,
        low,
        once_rows(share_ref, slots, local, low),
        lambda j: nn(normed, weights[j][pl.ds(HW, width), :]),
        normed,
        once_rows(share_ref, slots, local, normed),
        [(1, sent, 0), (3, sent, 1), (0, kept, 0), (2, kept, 1)],
        True,
    )
    end_s[...] += output
    for s in range(slots):
        res_tok[s] = end_s[pl.ds(s * piece, local), :].astype(BF)
        res_mem[s] = end_s[pl.ds(s * piece + local, SEG), :].astype(BF)
    res_tok.send()
    mid_normed = normed_s[...]
    gain_sum[...] = jnp.sum(
        once_rows(share_ref, slots, local, grad_normed * mid_normed), axis=0, keepdims=True
    )
    grad_mid[...] = low_s[...].astype(F32) + norm_backward(mid_normed, inverse, gain_f, grad_normed)


def ffn1(share, live, gain, state, out_tok, cot, cot_mem, parts, weights):
    slots, local, width = cot.shape
    rows = slots * (local + SEG)
    inner = weights[0].shape[0] - HW - width
    return call(
        functools.partial(ffn1_kernel, slots, local),
        (
            Away(slots, local, width),
            like(slots, SEG, width),
            Away(2, width + inner, width),
            Away(2, width + inner, width),
            Away(rows, width, dtype=F32),
            like(1, width, dtype=F32),
            Away(rows, width),
            like(slots * SEG, HW, dtype=F32),
        ),
        2 * rows * width * (width + 24 * inner),
        share,
        live,
        gain,
        cot_mem,
        *[Far(p) for p in parts],
        Far(out_tok),
        Far(cot),
        Far(state),
        *[Far(w) for w in weights],
        scratch=[
            pltpu.VMEM((rows, width), F32),
            pltpu.VMEM((rows, width), F32),
            pltpu.VMEM((rows, width), BF),
            pltpu.VMEM((SEG, width), F32),
        ],
        name="ffn1",
    )


def ffn0_back_sent_kernel(gain, grad_in, mid, hid_near, hid_last, w_near, w_last, sent, normed_sum):
    low = grad_in[...].astype(BF)
    normed = (normalize(mid[...])[0] * gain_row(gain, 0, 1)).astype(BF)
    hidden = {1: hid_near, 3: hid_last}
    normed_sum[...], _ = ffn_back_core(
        {1: w_near, 3: w_last},
        low,
        low,
        lambda j: hidden[j][...].astype(F32),
        normed,
        normed,
        [(1, sent, 0), (3, sent, 1)],
        False,
    )


def ffn0_back_sent(gain, grad_in, mid, hid, weights):
    rows, width = grad_in.shape
    inner = width
    return call(
        ffn0_back_sent_kernel,
        (Away(2, width + inner, width), Away(rows, width, dtype=F32)),
        2 * rows * width * (8 * inner),
        gain,
        Far(grad_in),
        Far(mid),
        Far(hid[1]),
        Far(hid[3]),
        packed(weights[1]),
        packed(weights[3]),
        name="ffn0_back_sent",
    )


def ffn0_back_kept_kernel(
    slots, local, gain, grad_in, mid, hid_own, hid_far, w0, w2, w1, w3, normed_sum, mixed,
    kept, out_kept, out_sent, grad_tok, grad_mem, gain_sum, d_own, d_near, d_pair
):
    weights = [w0, w1, w2, w3]
    piece = local + SEG
    width = gain.shape[2]
    low = grad_in[...].astype(BF)
    mid_normed, inverse = normalize(mid[...])
    normed = (mid_normed * gain_row(gain, 0, 1)).astype(BF)
    hidden = {0: hid_own, 2: hid_far}
    grad_normed, _ = ffn_back_core(
        weights,
        low,
        low,
        lambda j: hidden[j][...].astype(F32),
        normed,
        normed,
        [(0, kept, 0), (2, kept, 1)],
        False,
    )
    grad_normed += normed_sum[...]
    grad = grad_in[...] + norm_backward(mid_normed, inverse, gain_row(gain, 0, 1), grad_normed)
    low = grad.astype(BF)
    for j in (3, 2, 1, 0):
        back = nt(low, weights[j][pl.ds(0, HW), :]).astype(BF)
        for s in range(slots):
            value = back[s * piece : (s + 1) * piece]
            if j >= 2:
                d_pair[j - 2, s] = value
            else:
                (d_own, d_near)[j][s] = value
        if j < 3:
            (d_own, d_near, d_pair)[j].send()
    gain_sum[...] = jnp.sum(grad_normed * mid_normed, axis=0, keepdims=True)
    total = jnp.zeros((SEG, width), F32)
    for s in range(slots):
        grad_tok[s] = grad[s * piece : s * piece + local]
        total += grad[s * piece + local : (s + 1) * piece]
    grad_mem[...] = total
    grad_out = tn(mixed[...], low)
    for j in range(4):
        target = out_kept if j % 2 == 0 else out_sent
        target[j // 2] = grad_out[j * HW : (j + 1) * HW].astype(BF)


def ffn0_back_kept(slots, local, gain, grad_in, normed_sum, mid, hid, mixed, weights):
    rows, width = grad_in.shape
    inner = width
    return call(
        functools.partial(ffn0_back_kept_kernel, slots, local),
        (
            Away(2, width + inner, width),
            Away(2, HW, width),
            Away(2, HW, width),
            Away(slots, local, width, dtype=F32),
            like(SEG, width, dtype=F32),
            like(1, width, dtype=F32),
            Away(slots, local + SEG, HW),
            Away(slots, local + SEG, HW),
            Away(2, slots, local + SEG, HW),
        ),
        2 * rows * width * (2 * width + 8 * inner),
        gain,
        Far(grad_in),
        Far(mid),
        Far(hid[0]),
        Far(hid[2]),
        packed(weights[0]),
        packed(weights[2]),
        *[packed(weights[j], True) for j in (1, 3)],
        Far(normed_sum),
        Far(mixed),
        name="ffn0_back_kept",
    )


def spread_heads(target, value):
    size, width = value.shape
    lane = iota((size, width), 1) // DH
    for h in range(width // DH):
        target[pl.ds(h * size, size), :] = jnp.where(lane == h, value, jnp.zeros_like(value))


def fold_heads(value, size):
    width = value.shape[1]
    lane = iota((size, width), 1) // DH
    total = jnp.zeros((size, width), value.dtype)
    for h in range(width // DH):
        total += jnp.where(lane == h, value[h * size : (h + 1) * size], 0.0)
    return total


def memory_valid(local, rows, live, owner):
    lane = iota((rows, local + SEG), 1)
    return (lane < live) | ((lane >= local) & (lane < local + M) & (owner > 0))


def attention1_kernel(slots, local, live_ref, owner_ref, gain, state, *refs):
    w = refs[:4]
    q_o, k_o, v_o, probs, out_tok, part, spread_k, spread_v = refs[4:]
    piece = local + SEG
    width = gain.shape[2]
    heads = width // DH
    normed = (normalize(state[...])[0] * gain_row(gain, 1, 0)).astype(BF)
    for j in range(4):
        proj = nn(normed, w[j][...]).astype(BF)
        lanes = pl.ds(j * HW, HW)
        q_o[:, lanes] = proj[:, :HW] * jnp.asarray(SCALE, BF)
        k_o[:, lanes] = proj[:, HW : 2 * HW]
        v_o[:, lanes] = proj[:, 2 * HW :]
    for ref in (q_o, k_o, v_o):
        ref.send()
    for s in range(slots):
        tok = pl.ds(s * piece, local)
        seg = pl.ds(s * piece + local, SEG)
        both = pl.ds(s * piece, piece)
        spread_heads(spread_k, q_o[seg, :])
        scores = nt(spread_k[...], k_o[both, :])
        valid = memory_valid(local, heads * SEG, live_ref[s], owner_ref[0])
        scores = jnp.where(valid, scores, FAR)
        top = jnp.max(scores, axis=1, keepdims=True)
        p = jnp.where(valid, jnp.exp(scores - top), 0.0)
        total = jnp.sum(p, axis=1, keepdims=True)
        here = pl.ds(s * SEG, SEG)
        part[here, pl.ds(0, width)] = fold_heads(nn(p.astype(BF), v_o[both, :]), SEG)
        lane = iota((SEG, HW), 1)
        extra = jnp.zeros((SEG, HW), F32)
        for h in range(heads):
            extra = jnp.where(lane == h, top[h * SEG : (h + 1) * SEG], extra)
            extra = jnp.where(lane == heads + h, total[h * SEG : (h + 1) * SEG], extra)
        part[here, pl.ds(width, HW)] = extra
    part.send()
    for s in range(slots):
        tok = pl.ds(s * piece, local)
        seg = pl.ds(s * piece + local, SEG)
        spread_heads(spread_k, k_o[seg, :])
        spread_heads(spread_v, v_o[seg, :])
        st = nt(spread_k[...], q_o[tok, :])
        st = jnp.where(iota((heads * SEG, local), 0) % SEG < M, st, FAR)
        st = st.reshape(heads, SEG, local)
        p = jnp.exp(st - jnp.max(st, axis=1, keepdims=True))
        p = p / jnp.sum(p, axis=1, keepdims=True)
        p = p.reshape(heads * SEG, local).T
        probs[s] = p
        out_tok[s] = nn(p.astype(BF), spread_v[...]).astype(BF)


def attention1(slots, local, live, owner, state, gain, w):
    rows, width = state.shape
    spread = (width // DH) * SEG
    return call(
        functools.partial(attention1_kernel, slots, local),
        (
            Away(rows, width),
            Away(rows, width),
            Away(rows, width),
            Away(slots, local, spread, dtype=F32),
            Away(slots, local, width),
            Away(slots * SEG, width + HW, dtype=F32),
        ),
        2 * rows * width * 3 * width + 8 * rows * width * spread,
        live,
        owner,
        gain,
        Far(state),
        *[packed_qkv(x) for x in w],
        scratch=[pltpu.VMEM((spread, width), BF), pltpu.VMEM((spread, width), BF)],
        name="attention1",
    )


def attention1_back_kernel(
    slots, local, share_ref, live_ref, owner_ref, gain, logs, grad_mid, *refs
):
    weights, (k, v, probs, q, mixed, state), w = refs[:4], refs[4:10], refs[10:14]
    refs = refs[6:]
    grads, grad_end, gain_sum, back, spread_a, spread_b, spread_o = refs[8:]
    piece = local + SEG
    width = gain.shape[2]
    heads = width // DH
    spread = heads * SEG
    low = grad_mid[...].astype(BF)
    for j in range(4):
        back[:, pl.ds(j * HW, HW)] = nt(low, weights[j][pl.ds(0, HW), :]).astype(BF)
    same = (iota((spread, spread), 0) // SEG == iota((spread, spread), 1) // SEG).astype(BF)

    def put(i, at, value):
        value = value.astype(BF)
        for j in range(4):
            grads[at, pl.ds(j * 3 * HW + i * HW, HW)] = value[:, j * HW : (j + 1) * HW]

    for s in range(slots):
        tok = pl.ds(s * piece, local)
        seg = pl.ds(s * piece + local, SEG)
        both = pl.ds(s * piece, piece)
        spread_heads(spread_a, k[seg, :])
        spread_heads(spread_b, v[seg, :])
        p = probs[s]
        dp = nt(back[tok, :], spread_b[...])
        product = p * dp
        hi = product.astype(BF)
        rest = (product - hi.astype(F32)).astype(BF)
        ds = (p * (dp - nn(hi, same) - nn(rest, same))).astype(BF)
        put(0, tok, nn(ds, spread_a[...]) * SCALE)
        mem_k = fold_heads(tn(ds, q[tok, :]), SEG)
        mem_v = fold_heads(tn(p.astype(BF), back[tok, :]), SEG)
        spread_heads(spread_a, q[seg, :])
        spread_heads(spread_b, back[seg, :])
        spread_heads(spread_o, mixed[seg, :])
        scores = nt(spread_a[...], k[both, :])
        log = jnp.concatenate([logs[pl.ds(s * SEG, SEG), :][:, h : h + 1] for h in range(heads)], axis=0)
        valid = memory_valid(local, spread, live_ref[s], owner_ref[0])
        p = jnp.where(valid, jnp.exp(jnp.where(valid, scores, FAR) - log), 0.0)
        delta = jnp.sum(
            spread_b[...].astype(F32) * spread_o[...].astype(F32), axis=1, keepdims=True
        )
        ds = (p * (nt(spread_b[...], v[both, :]) - delta)).astype(BF)
        put(0, seg, fold_heads(nn(ds, k[both, :]), SEG) * SCALE)
        grad_k = tn(ds, spread_a[...])
        grad_v = tn(p.astype(BF), spread_b[...])
        put(1, tok, grad_k[:local])
        put(2, tok, grad_v[:local])
        put(1, seg, grad_k[local:] + mem_k)
        put(2, seg, grad_v[local:] + mem_v)
    grads.send()
    normed, inverse = normalize(state[...])
    total = None
    for j in range(4):
        add = nt(grads[:, pl.ds(j * 3 * HW, 3 * HW)], w[j][...])
        total = add if j == 0 else total + add
    gain_sum[...] = jnp.sum(total * normed, axis=0, keepdims=True)
    grad_end[...] = once_rows(share_ref, slots, local, grad_mid[...]) + norm_backward(
        normed, inverse, gain_row(gain, 1, 0), total
    )


def attention1_back(
    slots, local, share, live, owner, gain, grad_mid, state, mixed, logs, q, k, v, probs, weights, w
):
    rows, width = state.shape
    spread = (width // DH) * SEG
    return call(
        functools.partial(attention1_back_kernel, slots, local),
        (
            Away(rows, 3 * width),
            Away(rows, width, dtype=F32),
            like(1, width, dtype=F32),
        ),
        2 * rows * width * 4 * width + 20 * rows * width * spread,
        share,
        live,
        owner,
        gain,
        logs,
        Far(grad_mid),
        *[Far(x, (HW, width), [((pl.ds(0, HW),), ())]) for x in weights],
        *[Far(x) for x in (k, v, probs, q, mixed, state)],
        *[packed_qkv(x) for x in w],
        scratch=[
            pltpu.VMEM((rows, width), BF),
            pltpu.VMEM((spread, width), BF),
            pltpu.VMEM((spread, width), BF),
            pltpu.VMEM((spread, width), BF),
        ],
        name="attention1_back",
    )


def attention1_weights_kernel(slots, local, share_ref, gain, grad_mid, mixed, state, grads, kept, sent):
    low = once_rows(share_ref, slots, local, grad_mid[...].astype(BF))
    grad_out = tn(mixed[...], low)
    normed = (normalize(state[...])[0] * gain_row(gain, 1, 0)).astype(BF)
    for j in (1, 3, 0, 2):
        target = kept if j % 2 == 0 else sent
        target[j // 2, pl.ds(0, HW), :] = grad_out[j * HW : (j + 1) * HW].astype(BF)
        target[j // 2, pl.ds(HW, 3 * HW), :] = tn(grads[:, pl.ds(j * 3 * HW, 3 * HW)], normed).astype(BF)
        if j == 3:
            sent.send()


def attention1_weights(slots, local, share, gain, grad_mid, state, mixed, grads):
    rows, width = state.shape
    return call(
        functools.partial(attention1_weights_kernel, slots, local),
        (Away(2, 4 * HW, width), Away(2, 4 * HW, width)),
        2 * rows * width * 4 * width,
        share,
        gain,
        Far(grad_mid),
        Far(mixed),
        Far(state),
        Far(grads),
        name="attention1_weights",
    )


def on_device(
    tokens, lengths, memory, norm_gain, w_qkv, output_weight, w_up, w_down, cot_tokens, cot_memory
):
    slots, local, width = tokens.shape
    me = lax.axis_index("tensor")
    block = jnp.arange(4, dtype=jnp.int32)
    valid = jnp.clip(lengths[:, None] - (me ^ block)[None, :] * local, 0, local)
    live = valid[:, 0]
    owner = (me == 0).astype(jnp.int32)[None]
    share = (jnp.arange(slots, dtype=jnp.int32) % 4 == me).astype(jnp.int32)

    near = exchange(tokens, "tensor", 1)
    tok = [Chain(far_chain(tokens[s])) for s in range(slots)]
    fence(None, *tok)
    move0 = Chain(weights_chain(pack_weights(output_weight[0], w_up[0], w_down[0], w_qkv[1])))
    move1 = Chain(weights_chain(jnp.concatenate([output_weight[1], w_up[1], w_down[1]], axis=0)))
    fence(None, tok[0])
    finish(tok[0])
    saved, outs, out_moves = [], [], []
    beside = [[move0], [], [move0, move1]]
    for s in range(slots):
        finish(tok[s])
        rest = [t.arrived for t in tok[2:]] if s == 1 else []
        received, rest = fence((tok[s].result, rest), *out_moves, *beside[s])
        for t, arrived in zip(tok[2:], rest):
            t.arrived = arrived
        *out, qa, ka, va = attention0(s, valid[s], tokens, (near, *received), memory, norm_gain, w_qkv)
        out[0] = land(out[0], *tok[s + 1 : s + 2], *([move0, move1] if s == slots - 1 else []))
        saved.append((qa, ka, va))
        outs.append(out)
        out_moves.append(Chain(split_chain(*out[1:])))
    tok_blocks = [(near, *t.result) for t in tok]
    fence(None, *out_moves)
    finish(*out_moves, move0)
    weights0 = move0.result
    moved = [m.result for m in out_moves]
    moved = fence(moved, move1)
    mid0, state1, *hid0, mixed0 = ffn0(
        tokens, memory, norm_gain, [o[0] for o in outs], moved, weights0
    )
    attn1 = weights0
    q1, k1, v1, probs, out_tok, parts = attention1(slots, local, live, owner, state1, norm_gain, attn1)
    probs = land(probs, move1)
    parts = Chain(gather_chain(parts))
    finish(parts, move1)
    weights1 = move1.result
    res_tok, res_mem, kept1, sent1, grad_mid1, gain_f1, mixed1, logs = ffn1(
        share, live, norm_gain, state1, out_tok, cot_tokens, cot_memory, parts.result, weights1
    )

    sum1a = Chain(rows_chain(kept1, sent1))
    copied = Chain(copy_chain(res_mem[:, :M]))
    grad_mid1 = fence(grad_mid1, sum1a, copied)
    proj1, grad1, gain_a1 = attention1_back(
        slots, local, share, live, owner, norm_gain, grad_mid1, state1, mixed1, logs, q1, k1, v1, probs,
        weights1, attn1,
    )
    proj1, grad1 = fence((proj1, grad1), sum1a, copied)
    kept1, sent1 = attention1_weights(slots, local, share, norm_gain, grad_mid1, state1, mixed1, proj1)
    sum1b = Chain(rows_chain(kept1, sent1))
    finish(copied)
    grad1, res_mem = fence((grad1, copied.result), sum1b)
    sent0, normed_sum = ffn0_back_sent(norm_gain, grad1, mid0, hid0, weights0)
    sum0 = Chain(core_chain([None, None], sent0))
    finish(sum1a)
    sum1a = Chain(halved(sum1a.result))
    normed_sum = fence(normed_sum, sum0, sum1a, sum1b)
    kept0, out_kept, out_sent, grad_tok, grad_mem, gain_f0, d_own, *d_moving = ffn0_back_kept(
        slots, local, norm_gain, grad1, normed_sum, mid0, hid0, mixed0, weights0
    )
    grad_mem = land(grad_mem, sum0, sum1a, sum1b)
    sum0o = Chain(core_chain(out_kept, out_sent))
    d_move = Chain(split_chain(*d_moving))
    fence(None, d_move)
    finish(sum1a, sum1b)
    sum1b = Chain(halved(sum1b.result))
    fence((), sum1b, sum0o)
    finish(sum0o)
    got = sum0.arrived[0]
    near = jnp.concatenate([added(kept0[0], got[0]), sum0o.result[0]])
    far = jnp.concatenate([added(kept0[1], got[1]), sum0o.result[1]])
    near, far, d_move.arrived = lax.optimization_barrier((near, far, d_move.arrived))
    sum0 = Chain(cross_chain(near, far))
    finish(d_move, sum1b)
    sum1 = Chain(two_halves(sum1a.result, sum1b.result))
    moved = [d_own, *d_move.result]
    before, row_sums = None, []
    for s in range(slots):
        moved = fence(moved, sum0, sum1, *row_sums)
        kept, sent, *before = attention0_back(
            s, tokens, tok_blocks[s], memory, norm_gain, w_qkv, saved[s], outs[s], moved, before
        )
        before[2] = land(before[2], sum0, sum1, *row_sums)
        row_sums.append(Chain(rows_chain(kept, sent)))
    grad_qkv0, mem_normed, gain_a0 = before
    small = [mem_normed[:M], grad_mem[:M], gain_a0, gain_a1, gain_f0, gain_f1]
    last = Chain(last_chain(grad_qkv0, jnp.concatenate(small, axis=0)))
    fence((), last, *row_sums)
    fence((), last, *row_sums, sum0)
    fence((), last, sum1)
    fence((), last, sum0)
    fence((), last)
    finish(last, sum0, sum1, *row_sums)
    sum0q, small = last.result
    sum1 = sum1.result
    sum0 = sum0.result
    rows = []
    for s in range(slots):
        normed, inverse = normalize(tokens[s].astype(F32))
        gain = norm_gain[0, 0].astype(F32)
        total = row_sums[s].result.astype(F32)
        rows.append(grad_tok[s] + norm_backward(normed, inverse, gain, total))
    normed, inverse = normalize(memory.astype(F32))
    grad_memory = small[M : 2 * M] + norm_backward(normed, inverse, gain, small[:M])
    gains = small[2 * M : 2 * M + 4]

    def split_qkv(value):
        return jnp.swapaxes(value.reshape(3, HW, width), 1, 2)

    return (
        res_tok,
        res_mem,
        jnp.stack(rows),
        grad_memory,
        gains[0:2],
        gains[2:4],
        jnp.stack([split_qkv(sum0q), split_qkv(sum1[2 * width + HW :])]).astype(F32),
        jnp.stack([sum0[2 * width :], sum1[2 * width : 2 * width + HW]]).astype(F32),
        jnp.stack([sum0[:width], sum1[:width]]).astype(F32),
        jnp.stack([sum0[width : 2 * width], sum1[width : 2 * width]]).astype(F32),
    )


def solution(mesh):
    return jax.shard_map(
        on_device,
        mesh=mesh,
        in_specs=(
            P("dp", "tensor", None),
            P("dp"),
            P(),
            P(),
            P(None, None, None, "tensor"),
            P(None, "tensor", None),
            P(None, None, "tensor"),
            P(None, "tensor", None),
            P("dp", "tensor", None),
            P("dp", None, None),
        ),
        out_specs=(
            P("dp", "tensor", None),
            P("dp", None, None),
            P("dp", "tensor", None),
            P(),
            P(),
            P(),
            P(None, None, None, "tensor"),
            P(None, "tensor", None),
            P(None, None, "tensor"),
            P(None, "tensor", None),
        ),
        check_vma=False,
    )
```

```python
import functools

import jax
import jax.numpy as jnp
from jax import lax
from jax.experimental import pallas as pl
from jax.experimental.pallas import tpu as pltpu
from jax.sharding import PartitionSpec as P

DH = 64
M = 20
SEG = 32
HW = 2 * DH
EPS = 1e-05
SCALE = DH**-0.5
FAR = -1e30
BF = jnp.bfloat16
F32 = jnp.float32


def exchange(value, axis, mask):
    return lax.ppermute(value, axis, [(i, i ^ mask) for i in range(lax.axis_size(axis))])


class Chain:
    def __init__(self, generator):
        self.generator = generator
        self.arrived = None
        self.result = None
        self.wanted = []
        self.done = False

    def ask(self):
        try:
            self.wanted = self.generator.send(self.arrived)
        except StopIteration as stop:
            self.result = stop.value
            self.wanted = []
            self.done = True


def fence(inputs, *chains):
    chains = [c for c in chains if not c.done]
    for chain in chains:
        chain.ask()
    leaving = [[item[0] for item in chain.wanted] for chain in chains]
    if inputs is not None:
        inputs, leaving = lax.optimization_barrier((inputs, leaving))
    for chain, arrays in zip(chains, leaving):
        chain.arrived = [
            exchange(array, item[1], item[2]) for array, item in zip(arrays, chain.wanted)
        ]
    return inputs


def land(outputs, *chains):
    chains = [c for c in chains if not c.done]
    outputs, arrived = lax.optimization_barrier((outputs, [c.arrived for c in chains]))
    for chain, arrays in zip(chains, arrived):
        chain.arrived = arrays
    return outputs


def finish(*chains):
    while not all(c.done for c in chains):
        fence(None, *chains)


def far_chain(block):
    (far,) = yield [(block, "tensor", 2)]
    (last,) = yield [(far, "tensor", 1)]
    return [far, last]


def gather_chain(block):
    near, far = yield [(block, "tensor", 1), (block, "tensor", 2)]
    (last,) = yield [(far, "tensor", 1)]
    return [block, near, far, last]


def weights_chain(block):
    half = block.shape[0] // 2
    bit = lax.axis_index("dp") % 2
    (first,) = yield [(lax.dynamic_slice_in_dim(block, bit * half, half, 0), "tensor", 2)]
    (second,) = yield [(first, "dp", 1)]
    far = jnp.concatenate(
        [jnp.where(bit == 0, first, second), jnp.where(bit == 0, second, first)], axis=0
    )
    last, near = yield [(far, "tensor", 1), (block, "tensor", 1)]
    return [block, near, far, last]


def split_chain(near, pair):
    pair, near = yield [(pair, "tensor", 2), (near, "tensor", 1)]
    (other,) = yield [(pair, "tensor", 1)]
    return [near, pair, other]


def added(a, b):
    return (a.astype(F32) + b.astype(F32)).astype(BF)


def core_chain(kept, sent):
    (got,) = yield [(sent, "tensor", 1)]
    return (added(kept[0], got[0]), added(kept[1], got[1]))


def rows_chain(kept, sent):
    near, far = yield from core_chain(kept, sent)
    (got,) = yield [(far, "tensor", 2)]
    return added(near, got)


def dp_masks():
    size = lax.axis_size("dp")
    masks = []
    while 1 << len(masks) < size:
        masks.append(1 << len(masks))
    return masks


def dp_bit(mask):
    return (lax.axis_index("dp") // mask) % 2


def part(value, mask, other=False):
    half = value.shape[0] // 2
    bit = dp_bit(mask)
    return lax.dynamic_slice_in_dim(value, ((1 - bit) if other else bit) * half, half, 0)


def joined(value, got, mask):
    first = dp_bit(mask) == 0
    return jnp.concatenate([jnp.where(first, value, got), jnp.where(first, got, value)], axis=0)


def reduced(value, masks, whole):
    halves = masks[: len(masks) - whole]
    for mask in halves:
        (got,) = yield [(part(value, mask, True), "dp", mask)]
        value = added(part(value, mask), got)
    for mask in masks[len(halves) :]:
        (got,) = yield [(value, "dp", mask)]
        value = added(value, got)
    for mask in reversed(halves):
        (got,) = yield [(value, "dp", mask)]
        value = joined(value, got, mask)
    return value


def cross_steps(near, far):
    half = near.shape[0] // 2
    near_a, near_b = near[:half], near[half:]
    far_a, far_b = far[:half], far[half:]
    pair = jnp.stack([part(near_b, 1, True), part(far_b, 1, True)])
    got_a, got_b = yield [(far_a, "tensor", 2), (pair, "dp", 1)]
    near_a = added(near_a, got_a)
    near_b = added(part(near_b, 1), got_b[0])
    far_b = added(part(far_b, 1), got_b[1])
    got_a, got_b = yield [(part(near_a, 1, True), "dp", 1), (far_b, "tensor", 2)]
    return jnp.concatenate([added(part(near_a, 1), got_a), added(near_b, got_b)], axis=0)


def cross_joined(value, got):
    half = value.shape[0] // 2
    return jnp.concatenate([joined(value[:half], got[:half], 1), joined(value[half:], got[half:], 1)])


def cross_chain(near, far):
    value = yield from cross_steps(near, far)
    value = yield from reduced(value, dp_masks()[1:], 1)
    (got,) = yield [(value, "dp", 1)]
    return cross_joined(value, got)


def halved(value):
    (got,) = yield [(part(value, 1, True), "dp", 1)]
    return added(part(value, 1), got)


def two_halves(first, second):
    rows = first.shape[0]
    value = jnp.concatenate([first, second])
    value = yield from reduced(value, dp_masks()[1:], 1)
    (got,) = yield [(value, "dp", 1)]
    return jnp.concatenate([joined(value[:rows], got[:rows], 1), joined(value[rows:], got[rows:], 1)])


def copy_chain(value):
    me = lax.axis_index("tensor")
    (got,) = yield [(value, "tensor", 2)]
    value = jnp.where(me // 2 == 0, value, got)
    (got,) = yield [(value, "tensor", 1)]
    return jnp.where(me % 2 == 0, value, got)


def last_chain(grad, small):
    (got,) = yield [(small, "tensor", 1)]
    small = small + got
    got, far = yield [(part(grad, 1, True), "dp", 1), (small, "tensor", 2)]
    grad = added(part(grad, 1), got)
    small = small + far
    rows = grad.shape[0]
    value = jnp.concatenate([grad, small.astype(BF)])
    masks = dp_masks()[1:]
    value = yield from reduced(value, masks, len(masks))
    (got,) = yield [(value, "dp", 1)]
    return (joined(value[:rows], got[:rows], 1), value[rows:].astype(F32) + got[rows:].astype(F32))


def nn(a, b):
    return lax.dot_general(a, b, (((1,), (0,)), ((), ())), preferred_element_type=F32)


def nt(a, b):
    return lax.dot_general(a, b, (((1,), (1,)), ((), ())), preferred_element_type=F32)


def tn(a, b):
    return lax.dot_general(a, b, (((0,), (0,)), ((), ())), preferred_element_type=F32)


def normalize(state):
    center = jnp.mean(state, axis=-1, keepdims=True)
    shifted = state - center
    spread = jnp.mean(shifted * shifted, axis=-1, keepdims=True)
    inverse = lax.rsqrt(spread + EPS)
    return (shifted * inverse, inverse)


def norm_backward(normed, inverse, gain_row, grad_normed):
    scaled = grad_normed * gain_row
    return inverse * (
        scaled
        - jnp.mean(scaled, axis=-1, keepdims=True)
        - normed * jnp.mean(scaled * normed, axis=-1, keepdims=True)
    )


def gelu_parts(hidden, with_slope):
    c = 0.7978845608028654
    a = 0.044715
    square = hidden * hidden
    t = jnp.tanh(hidden * (c + (c * a) * square))
    up = 0.5 + 0.5 * t
    active = hidden * up
    if not with_slope:
        return active
    slope = up + hidden * (0.5 - 0.5 * t * t) * (c + (3.0 * c * a) * square)
    return (active, slope)


def iota(shape, axis):
    return lax.broadcasted_iota(jnp.int32, shape, axis)


class Far:
    def __init__(self, array, shape=None, pieces=None):
        self.array = array
        self.shape = array.shape if shape is None else shape
        self.pieces = [((), ())] if pieces is None else pieces


class Away:
    def __init__(self, *shape, dtype=BF):
        self.shape = shape
        self.dtype = dtype


def at(ref, index):
    return ref.at[index] if index else ref


class Incoming:
    def __init__(self, ref, copies):
        self.ref = ref
        self.copies = copies
        self.shape = ref.shape
        for copy in copies:
            copy.start()

    def wait(self):
        for copy in self.copies:
            copy.wait()
        self.copies = []

    def __getitem__(self, index):
        self.wait()
        return self.ref[index]


class Outgoing:
    def __init__(self, ref, copy, early):
        self.ref = ref
        self.copy = copy
        self.early = early
        self.sent = False

    def __setitem__(self, index, value):
        self.ref[index] = value

    def __getitem__(self, index):
        return self.ref[index]

    def send(self):
        if self.early:
            self.start()

    def start(self):
        if not self.sent:
            self.copy.start()
        self.sent = True


def call(kernel, results, cost, *operands, scratch=(), name=None, limit=60, early=False):
    arrays = [o.array if isinstance(o, Far) else o for o in operands]
    specs, buffers, count = [], [], 0
    for o in operands:
        if isinstance(o, Far):
            specs.append(pl.BlockSpec(memory_space=pltpu.HBM))
            buffers.append(pltpu.VMEM(o.shape, o.array.dtype))
            count += len(o.pieces)
        else:
            space = pltpu.SMEM if o.dtype == jnp.int32 else pltpu.VMEM
            specs.append(pl.BlockSpec(memory_space=space))
    out_specs = []
    for r in results:
        away = isinstance(r, Away)
        out_specs.append(pl.BlockSpec(memory_space=pltpu.HBM if away else pltpu.VMEM))
        if away:
            buffers.append(pltpu.VMEM(r.shape, r.dtype))
            count += 1

    def body(*refs):
        ins = refs[: len(operands)]
        outs = refs[len(operands) : len(operands) + len(results)]
        rest = list(refs[len(operands) + len(results) :])
        sem = rest.pop()
        used = iter(range(count))
        local_buffers = iter(rest[: len(buffers)])
        given = []
        for o, ref in zip(operands, ins):
            if isinstance(o, Far):
                buffer = next(local_buffers)
                ref = Incoming(
                    buffer,
                    [
                        pltpu.make_async_copy(at(ref, src), at(buffer, dst), sem.at[next(used)])
                        for src, dst in o.pieces
                    ],
                )
            given.append(ref)
        taken = []
        for r, ref in zip(results, outs):
            if isinstance(r, Away):
                buffer = next(local_buffers)
                ref = Outgoing(buffer, pltpu.make_async_copy(buffer, ref, sem.at[next(used)]), early)
            taken.append(ref)
        if not early:
            for ref in given:
                if isinstance(ref, Incoming):
                    ref.wait()
        kernel(*given, *taken, *rest[len(buffers) :])
        for ref in given:
            if isinstance(ref, Incoming):
                ref.wait()
        for ref in taken:
            if isinstance(ref, Outgoing):
                ref.start()
        for ref in taken:
            if isinstance(ref, Outgoing):
                ref.copy.wait()

    moved = sum(o.size * o.dtype.itemsize for o in arrays)
    return pl.pallas_call(
        body,
        out_shape=[jax.ShapeDtypeStruct(r.shape, r.dtype) for r in results],
        in_specs=specs,
        out_specs=out_specs,
        scratch_shapes=buffers + list(scratch) + [pltpu.SemaphoreType.DMA((max(count, 1),))],
        compiler_params=pltpu.CompilerParams(vmem_limit_bytes=limit * 1024 * 1024),
        cost_estimate=pl.CostEstimate(flops=cost // 64, bytes_accessed=moved // 64, transcendentals=0),
        name=name,
    )(*arrays)


def like(*shape, dtype=BF):
    return jax.ShapeDtypeStruct(shape, dtype)


def qkv_pieces(sources):
    return [
        (tuple(prefix) + (i,), (slice(None), pl.ds((3 * j + i) * HW, HW)))
        for j, prefix in enumerate(sources)
        for i in range(3)
    ]


def gain_row(gain_ref, layer, which):
    return gain_ref[layer, pl.ds(which, 1), :].astype(F32)


def pad_rows(scratch, value):
    scratch[...] = jnp.zeros_like(scratch)
    scratch[pl.ds(0, value.shape[0]), :] = value.astype(F32)


def head_lanes(rows, h):
    lane = iota((rows, HW), 1)
    inside = (lane >= h * DH) & (lane < (h + 1) * DH)
    return lane - (1 - h) * DH, inside


def attention0_kernel(
    local, valid_ref, mem, gain, x0, x1, x2, x3, w, own, near, pair, qa, ka, va, vh, mem_s
):
    keys = 4 * local + SEG
    tokens = [x0, x1, x2, x3]
    pad_rows(mem_s, mem[...])
    blocks = [(j * local, local, tokens[j]) for j in range(4)] + [(4 * local, SEG, mem_s)]
    for j, (start, size, ref) in enumerate(blocks):
        normed, _ = normalize(ref[...].astype(F32))
        normed = (normed * gain_row(gain, 0, 0)).astype(BF)
        proj = nn(normed, w[...]).astype(BF)
        q = proj[:, :HW] * jnp.asarray(SCALE, BF)
        k = proj[:, HW : 2 * HW]
        v = proj[:, 2 * HW :]
        rows = pl.ds(start, size)
        va[rows, :] = v
        valid = iota((size, HW), 0) < (valid_ref[j] if j < 4 else M)
        bias = jnp.where(valid, 0.0, FAR).astype(BF)
        for h in range(2):
            spare, inside = head_lanes(size, h)
            one = jnp.where(spare == 0, 1.0, 0.0).astype(BF)
            extra = jnp.where((spare >= 1) & (spare <= 3), 1.0, 0.0).astype(BF)
            ka[h, rows, :] = jnp.where(inside, k, jnp.where(spare == 0, bias, extra))
            qa[h, rows, :] = jnp.where(inside, q, one)
            vh[h, rows, :] = jnp.where(inside, v, one)
    ka.send()
    va.send()

    def chunk(start, size):
        rows = pl.ds(start, size)
        out = None
        for h in range(2):
            spare, inside = head_lanes(size, h)
            q = qa[h, rows, :]
            scores = nt(q, ka[h])
            top = jnp.max(scores, axis=1, keepdims=True)
            o = nn(jnp.exp(scores - top).astype(BF), vh[h])
            total = o[:, (1 - h) * DH : (1 - h) * DH + 1]
            col = -(top + jnp.log(total))
            hi = col.astype(BF).astype(F32)
            mid = (col - hi).astype(BF).astype(F32)
            low = col - hi - mid
            extra = jnp.where(spare == 1, hi, jnp.where(spare == 2, mid, jnp.where(spare == 3, low, 0.0)))
            qa[h, rows, :] = jnp.where(inside | (spare == 0), q, extra.astype(BF))
            o = o / total
            out = o if h == 0 else jnp.where(inside, o, out)
        return out.astype(BF)

    out = chunk(4 * local, SEG)
    rows = pl.ds(local, SEG)
    own[rows, :] = out
    near[rows, :] = out
    pair[0, rows, :] = out
    pair[1, rows, :] = out
    rows = pl.ds(0, local)
    out = chunk(2 * local, 2 * local)
    pair[0, rows, :] = out[:local]
    pair[1, rows, :] = out[local:]
    pair.send()
    out = chunk(0, 2 * local)
    own[rows, :] = out[:local]
    near[rows, :] = out[local:]


def pack_weights(out, up, down, qkv):
    parts = [up, down, jnp.concatenate([out[:, i * HW : (i + 1) * HW] for i in range(4)], axis=0)]
    return jnp.concatenate(parts + [qkv[i] for i in range(3)], axis=1)


def packed_out(width):
    lanes = pl.ds(2 * width, HW)
    return [((pl.ds(i * HW, HW), lanes), (pl.ds(0, HW), pl.ds(i * HW, HW))) for i in range(4)]


def packed_ffn(width):
    pieces = [
        ((slice(None), pl.ds(i * width, width)), (pl.ds(HW + i * width, width), slice(None)))
        for i in range(2)
    ]
    return packed_out(width) + pieces


def packed(block, only_out=False):
    width = block.shape[0]
    if only_out:
        return Far(block, (HW, width), packed_out(width))
    return Far(block, (HW + 2 * width, width), packed_ffn(width))


def packed_qkv(block):
    width = block.shape[0]
    return Far(block, (width, 3 * HW), [((slice(None), pl.ds(2 * width + HW, 3 * HW)), ())])


def token_blocks(s, tokens, blocks):
    shape = tokens.shape[1:]
    near, far, last = blocks
    own = Far(tokens, shape, [((s,), ())])
    return [own, Far(near, shape, [((s,), ())]), Far(far), Far(last)]


def attention0(s, valid, tokens, blocks, memory, gain, w_qkv):
    _, local, width = tokens.shape
    keys = 4 * local + SEG
    piece = local + SEG
    cost = 2 * keys * width * 3 * HW + 16 * keys * keys * HW
    return call(
        functools.partial(attention0_kernel, local),
        (
            Away(piece, HW),
            Away(piece, HW),
            Away(2, piece, HW),
            Away(2, keys, HW),
            Away(2, keys, HW),
            Away(keys, HW),
        ),
        cost,
        valid,
        memory,
        gain,
        *token_blocks(s, tokens, blocks),
        Far(w_qkv, (width, 3 * HW), qkv_pieces([(0,)])),
        scratch=[pltpu.VMEM((2, keys, HW), BF), pltpu.VMEM((SEG, width), F32)],
        name="attention0",
    )


def attention0_back_kernel(
    local, first_call, last_call, mem, gain, before_mem, before_gain, g_own, g_near, g_far, g_last,
    o_own, o_near, o_pair, va, ka, qa, x1, x3, x0, x2, w, before_w,
    kept, sent, grad_w, mem_normed, gain_sum,
    grads, va_s, da_s, d_s, acc_v, acc_k, mem_s,
):
    keys = 4 * local + SEG
    pad_rows(mem_s, mem[...])
    own = pl.ds(0, local)
    pieces = [
        (0, g_own[own, :], o_own[own, :]),
        (local, g_near[own, :], o_near[own, :]),
        (2 * local, g_far[own, :], o_pair[0, own, :]),
        (3 * local, g_last[own, :], o_pair[1, own, :]),
    ]
    tail = pl.ds(local, SEG)
    parts = [g[tail, :].astype(F32) for g in (g_own, g_near, g_far, g_last)]
    grad = ((parts[0] + parts[1]) + (parts[2] + parts[3])).astype(BF)
    pieces.append((4 * local, grad, o_own[tail, :]))
    for start, grad, out in pieces:
        size = grad.shape[0]
        rows = pl.ds(start, size)
        product = grad.astype(F32) * out.astype(F32)
        d_s[rows, :] = grad
        for h in range(2):
            spare, inside = head_lanes(size, h)
            col = -jnp.sum(jnp.where(inside, product, 0.0), axis=-1, keepdims=True)
            hi = col.astype(BF).astype(F32)
            extra = jnp.where(spare == 0, hi, jnp.where(spare == 1, col - hi, 0.0))
            da_s[h, rows, :] = jnp.where(inside, grad, extra.astype(BF))
    for h in range(2):
        spare, inside = head_lanes(keys, h)
        ones = jnp.where((spare == 0) | (spare == 1), 1.0, 0.0).astype(BF)
        va_s[h] = jnp.where(inside, va[...], ones)
    first = iota((keys, HW), 1) < DH
    key = jnp.where(first, ka[0], ka[1])

    def chunk(start, size, fresh):
        rows = pl.ds(start, size)
        turned = []
        for h in range(2):
            p = jnp.exp(nt(ka[h], qa[h, rows, :]))
            dp = nt(va_s[h], da_s[h, rows, :])
            ds = (p * dp).astype(BF)
            add_v = nn(p.astype(BF), d_s[rows, :])
            add_k = nn(ds, qa[h, rows, :])
            if fresh:
                acc_v[h] = add_v
                acc_k[h] = add_k
            else:
                acc_v[h] += add_v
                acc_k[h] += add_k
            turned.append(tn(ds, key))
        out = jnp.where(iota((size, HW), 1) < DH, turned[0], turned[1]) * SCALE
        grads[rows, :HW] = out.astype(BF)

    chunk(0, 2 * local, True)
    chunk(2 * local, 2 * local, False)
    rows = pl.ds(4 * local, SEG)
    turned = []
    for h in range(2):
        p = jnp.exp(nt(qa[h, rows, :], ka[h]))
        ds = (p * nt(da_s[h, rows, :], va_s[h])).astype(BF)
        acc_v[h] += tn(p.astype(BF), d_s[rows, :])
        acc_k[h] += tn(ds, qa[h, rows, :])
        turned.append(nn(ds, key))
    out = jnp.where(iota((SEG, HW), 1) < DH, turned[0], turned[1]) * SCALE
    grads[rows, :HW] = out.astype(BF)
    grads[:, HW : 2 * HW] = jnp.where(first, acc_k[0], acc_k[1]).astype(BF)
    grads[:, 2 * HW :] = jnp.where(first, acc_v[0], acc_v[1]).astype(BF)

    tokens = [x0, x1, x2, x3]
    total_w = None if first_call else before_w[...]
    total_gain = None if first_call else before_gain[...]
    for j in (1, 3, 0, 2, 4):
        size = local if j < 4 else SEG
        ref = tokens[j] if j < 4 else mem_s
        normed, _ = normalize(ref[...].astype(F32))
        low = (normed * gain_row(gain, 0, 0)).astype(BF)
        part = grads[pl.ds(j * local, size), :]
        add_w = tn(part, low)
        grad_normed = nt(part, w[...])
        add_gain = jnp.sum(grad_normed * normed, axis=0, keepdims=True)
        total_w = add_w if total_w is None else total_w + add_w
        total_gain = add_gain if total_gain is None else total_gain + add_gain
        if j == 4:
            mem_normed[...] = grad_normed if first_call else grad_normed + before_mem[...]
        else:
            target = kept if j % 2 == 0 else sent
            target[j // 2] = grad_normed.astype(BF)
            if j == 3:
                sent.send()
            if j == 2:
                kept.send()
    grad_w[...] = total_w.astype(BF if last_call else F32)
    gain_sum[...] = total_gain


def attention0_back(s, tokens, blocks, memory, gain, w_qkv, saved, outs, moved, before):
    slots, local, width = tokens.shape
    keys = 4 * local + SEG
    cost = 4 * keys * width * 3 * HW + 40 * keys * keys * HW
    first_call, last_call = before is None, s == slots - 1
    if first_call:
        before = [memory] * 3
    before_w, before_mem, before_gain = before
    qa, ka, va = saved
    block = (local + SEG, HW)
    return call(
        functools.partial(attention0_back_kernel, local, first_call, last_call),
        (
            Away(2, local, width),
            Away(2, local, width),
            Away(3 * HW, width, dtype=BF if last_call else F32),
            like(SEG, width, dtype=F32),
            like(1, width, dtype=F32),
        ),
        cost,
        memory,
        gain,
        before_mem,
        before_gain,
        *[Far(g, block, [((s,), ())]) for g in moved[:2]],
        Far(moved[2], block, [((0, s), ())]),
        Far(moved[3], block, [((1, s), ())]),
        *[Far(o) for o in outs],
        Far(va),
        Far(ka),
        Far(qa),
        *[token_blocks(s, tokens, blocks)[j] for j in (1, 3, 0, 2)],
        Far(w_qkv, (width, 3 * HW), qkv_pieces([(0,)])),
        Far(before_w),
        scratch=[
            pltpu.VMEM((keys, 3 * HW), BF),
            pltpu.VMEM((2, keys, HW), BF),
            pltpu.VMEM((2, keys, HW), BF),
            pltpu.VMEM((keys, HW), BF),
            pltpu.VMEM((2, keys, HW), F32),
            pltpu.VMEM((2, keys, HW), F32),
            pltpu.VMEM((SEG, width), F32),
        ],
        name="attention0_back",
    )


def ffn0_kernel(slots, local, mem, gain, *refs):
    tokens, own, refs = refs[0], refs[1 : 1 + slots], refs[1 + slots :]
    moved, weights = refs[: 3 * slots], refs[3 * slots : 4 + 3 * slots]
    mid, end, hid0, hid1, hid2, hid3, mixed, normed_s, mem_s = refs[4 + 3 * slots :]
    hid = [hid0, hid1, hid2, hid3]
    piece = local + SEG
    width = gain.shape[2]
    inner = weights[0].shape[0] - HW - width
    pad_rows(mem_s, mem[...])
    for s in range(slots):
        rows = pl.ds(s * piece, piece)
        state = jnp.concatenate([tokens[s].astype(F32), mem_s[...]], axis=0)
        for j in range(4):
            out = own[s][...] if j == 0 else moved[3 * s + j - 1][...]
            mixed[rows, pl.ds(j * HW, HW)] = out
            state += nn(out, weights[j][pl.ds(0, HW), :])
        mid[rows, :] = state
        end[rows, :] = state
        normed_s[rows, :] = (normalize(state)[0] * gain_row(gain, 0, 1)).astype(BF)
    mid.send()
    mixed.send()
    for j in range(4):
        hid[j][...] = nn(normed_s[...], weights[j][pl.ds(HW, width), :]).astype(BF)
        hid[j].send()
    for j in range(4):
        active = gelu_parts(hid[j][...].astype(F32), False).astype(BF)
        end[...] += nn(active, weights[j][pl.ds(HW + width, inner), :])


def ffn0(tokens, memory, gain, own, moved, weights):
    slots, local, width = tokens.shape
    rows = slots * (local + SEG)
    inner = width
    return call(
        functools.partial(ffn0_kernel, slots, local),
        (
            Away(rows, width, dtype=F32),
            Away(rows, width, dtype=F32),
            Away(rows, inner),
            Away(rows, inner),
            Away(rows, inner),
            Away(rows, inner),
            Away(rows, width),
        ),
        2 * rows * width * (width + 8 * inner),
        memory,
        gain,
        Far(tokens),
        *[Far(o) for o in own],
        *[
            Far(m, (local + SEG, HW), [((j,), ())] if m.ndim == 3 else None)
            for near, pair, other in moved
            for m, j in ((near, None), (pair, 0), (other, 1))
        ],
        *[packed(w) for w in weights],
        scratch=[pltpu.VMEM((rows, width), BF), pltpu.VMEM((SEG, width), F32)],
        name="ffn0",
        early=True,
    )


def ffn_back_core(weights, low, low_once, hidden_of, normed, normed_once, targets, with_output):
    width = normed.shape[1]
    inner = weights[targets[0][0]].shape[0] - HW - width
    total, output = None, None
    for j, target, slot in targets:
        up = weights[j][pl.ds(HW, width), :]
        down = weights[j][pl.ds(HW + width, inner), :]
        active, slope = gelu_parts(hidden_of(j), True)
        active = active.astype(BF)
        if with_output:
            add = nn(active, down)
            output = add if output is None else output + add
        grad_hidden = (nt(low, down) * slope).astype(BF)
        target[slot, pl.ds(0, width), :] = tn(normed_once, grad_hidden).astype(BF)
        target[slot, pl.ds(width, inner), :] = tn(active, low_once).astype(BF)
        if slot == 1:
            target.send()
        add = nt(grad_hidden, up)
        total = add if total is None else total + add
    return (total, output)


def once_rows(share_ref, slots, local, value):
    piece = local + SEG
    parts = []
    for s in range(slots):
        parts.append(value[s * piece : s * piece + local])
        tail = value[s * piece + local : (s + 1) * piece]
        parts.append(jnp.where(share_ref[s] > 0, tail, jnp.zeros_like(tail)))
    return jnp.concatenate(parts, axis=0)


def ffn1_kernel(slots, local, share_ref, live_ref, gain, cot_mem, *refs):
    parts, out_tok, cot, state, weights = refs[:4], refs[4], refs[5], refs[6], refs[7:11]
    (res_tok, res_mem, kept, sent, grad_mid, gain_sum, mixed, logs) = refs[11:19]
    normed_s, end_s, low_s, mem_s = refs[19:]
    piece = local + SEG
    width = gain.shape[2]
    heads = width // DH
    gain_f = gain_row(gain, 1, 1)
    lane = iota((SEG, HW), 1)
    mixed_rows = []
    for s in range(slots):
        seg = pl.ds(s * SEG, SEG)
        scale = {}
        log = jnp.zeros((SEG, HW), F32)
        extras = [parts[j][seg, pl.ds(width, HW)] for j in range(4)]
        for h in range(heads):
            source = [2 * ((h // 2) ^ j) + h % 2 for j in range(4)]
            tops = [extras[j][:, source[j] : source[j] + 1] for j in range(4)]
            sums = [extras[j][:, heads + source[j] : heads + source[j] + 1] for j in range(4)]
            peak = functools.reduce(jnp.maximum, tops)
            raised = [jnp.exp(t - peak) for t in tops]
            total = functools.reduce(jnp.add, [r * t for r, t in zip(raised, sums)])
            scale[h] = [r / total for r in raised]
            log = jnp.where(lane == h, peak + jnp.log(total), log)
        logs[seg, :] = log
        for b in range(4):
            merged = jnp.zeros((SEG, HW), F32)
            for j in range(4):
                factor = jnp.where(lane < DH, scale[2 * b][j], scale[2 * b + 1][j])
                merged += factor * parts[j][seg, pl.ds((b ^ j) * HW, HW)]
            mixed[pl.ds(s * piece + local, SEG), pl.ds(b * HW, HW)] = merged.astype(BF)
        rows = pl.ds(s * piece, local)
        mixed[rows, :] = out_tok[s]
        live = iota((local, 1), 0) < live_ref[s]
        low_s[rows, :] = jnp.where(live, cot[s], jnp.zeros_like(cot[s]))
        pad_rows(mem_s, cot_mem[s])
        low_s[pl.ds(s * piece + local, SEG), :] = mem_s[...].astype(BF)
    mixed.send()
    mid = state[...]
    for j in range(4):
        mid += nn(mixed[:, pl.ds(j * HW, HW)], weights[j][pl.ds(0, HW), :])
    end_s[...] = mid
    mid_normed, inverse = normalize(mid)
    normed = (mid_normed * gain_f).astype(BF)
    normed_s[...] = mid_normed
    low = low_s[...]
    grad_normed, output = ffn_back_core(
        weights,
        low,
        once_rows(share_ref, slots, local, low),
        lambda j: nn(normed, weights[j][pl.ds(HW, width), :]),
        normed,
        once_rows(share_ref, slots, local, normed),
        [(1, sent, 0), (3, sent, 1), (0, kept, 0), (2, kept, 1)],
        True,
    )
    end_s[...] += output
    for s in range(slots):
        res_tok[s] = end_s[pl.ds(s * piece, local), :].astype(BF)
        res_mem[s] = end_s[pl.ds(s * piece + local, M), :].astype(BF)
    res_tok.send()
    mid_normed = normed_s[...]
    gain_sum[...] = jnp.sum(
        once_rows(share_ref, slots, local, grad_normed * mid_normed), axis=0, keepdims=True
    )
    grad_mid[...] = low_s[...].astype(F32) + norm_backward(mid_normed, inverse, gain_f, grad_normed)


def ffn1(share, live, gain, state, out_tok, cot, cot_mem, parts, weights):
    slots, local, width = cot.shape
    rows = slots * (local + SEG)
    inner = weights[0].shape[0] - HW - width
    return call(
        functools.partial(ffn1_kernel, slots, local),
        (
            Away(slots, local, width),
            like(slots, M, width),
            Away(2, width + inner, width),
            Away(2, width + inner, width),
            Away(rows, width, dtype=F32),
            like(1, width, dtype=F32),
            Away(rows, width),
            like(slots * SEG, HW, dtype=F32),
        ),
        2 * rows * width * (width + 24 * inner),
        share,
        live,
        gain,
        cot_mem,
        *[Far(p) for p in parts],
        Far(out_tok),
        Far(cot),
        Far(state),
        *[Far(w) for w in weights],
        scratch=[
            pltpu.VMEM((rows, width), F32),
            pltpu.VMEM((rows, width), F32),
            pltpu.VMEM((rows, width), BF),
            pltpu.VMEM((SEG, width), F32),
        ],
        name="ffn1",
        early=True,
    )


def ffn0_back_sent_kernel(gain, grad_in, mid, hid_near, hid_last, w_near, w_last, sent, normed_sum):
    low = grad_in[...].astype(BF)
    normed = (normalize(mid[...])[0] * gain_row(gain, 0, 1)).astype(BF)
    hidden = {1: hid_near, 3: hid_last}
    normed_sum[...], _ = ffn_back_core(
        {1: w_near, 3: w_last},
        low,
        low,
        lambda j: hidden[j][...].astype(F32),
        normed,
        normed,
        [(1, sent, 0), (3, sent, 1)],
        False,
    )


def ffn0_back_sent(gain, grad_in, mid, hid, weights):
    rows, width = grad_in.shape
    inner = width
    return call(
        ffn0_back_sent_kernel,
        (Away(2, width + inner, width), Away(rows, width, dtype=F32)),
        2 * rows * width * (8 * inner),
        gain,
        Far(grad_in),
        Far(mid),
        Far(hid[1]),
        Far(hid[3]),
        packed(weights[1]),
        packed(weights[3]),
        name="ffn0_back_sent",
        early=True,
    )


def ffn0_back_kept_kernel(
    slots, local, gain, grad_in, mid, hid_own, hid_far, w0, w2, w1, w3, normed_sum, mixed,
    kept, out_kept, out_sent, grad_tok, grad_mem, gain_sum, d_own, d_near, d_pair
):
    weights = [w0, w1, w2, w3]
    piece = local + SEG
    width = gain.shape[2]
    low = grad_in[...].astype(BF)
    mid_normed, inverse = normalize(mid[...])
    normed = (mid_normed * gain_row(gain, 0, 1)).astype(BF)
    hidden = {0: hid_own, 2: hid_far}
    grad_normed, _ = ffn_back_core(
        weights,
        low,
        low,
        lambda j: hidden[j][...].astype(F32),
        normed,
        normed,
        [(0, kept, 0), (2, kept, 1)],
        False,
    )
    grad_normed += normed_sum[...]
    grad = grad_in[...] + norm_backward(mid_normed, inverse, gain_row(gain, 0, 1), grad_normed)
    low = grad.astype(BF)
    for j in (3, 2, 1, 0):
        back = nt(low, weights[j][pl.ds(0, HW), :]).astype(BF)
        for s in range(slots):
            value = back[s * piece : (s + 1) * piece]
            if j >= 2:
                d_pair[j - 2, s] = value
            else:
                (d_own, d_near)[j][s] = value
        if j < 3:
            (d_own, d_near, d_pair)[j].send()
    gain_sum[...] = jnp.sum(grad_normed * mid_normed, axis=0, keepdims=True)
    total = jnp.zeros((SEG, width), F32)
    for s in range(slots):
        grad_tok[s] = grad[s * piece : s * piece + local]
        total += grad[s * piece + local : (s + 1) * piece]
    grad_mem[...] = total
    grad_out = tn(mixed[...], low)
    for j in range(4):
        target = out_kept if j % 2 == 0 else out_sent
        target[j // 2] = grad_out[j * HW : (j + 1) * HW].astype(BF)


def ffn0_back_kept(slots, local, gain, grad_in, normed_sum, mid, hid, mixed, weights):
    rows, width = grad_in.shape
    inner = width
    return call(
        functools.partial(ffn0_back_kept_kernel, slots, local),
        (
            Away(2, width + inner, width),
            Away(2, HW, width),
            Away(2, HW, width),
            Away(slots, local, width, dtype=F32),
            like(SEG, width, dtype=F32),
            like(1, width, dtype=F32),
            Away(slots, local + SEG, HW),
            Away(slots, local + SEG, HW),
            Away(2, slots, local + SEG, HW),
        ),
        2 * rows * width * (2 * width + 8 * inner),
        gain,
        Far(grad_in),
        Far(mid),
        Far(hid[0]),
        Far(hid[2]),
        packed(weights[0]),
        packed(weights[2]),
        *[packed(weights[j], True) for j in (1, 3)],
        Far(normed_sum),
        Far(mixed),
        name="ffn0_back_kept",
        early=True,
    )


def spread_heads(target, value):
    size, width = value.shape
    lane = iota((size, width), 1) // DH
    for h in range(width // DH):
        target[pl.ds(h * size, size), :] = jnp.where(lane == h, value, jnp.zeros_like(value))


def fold_heads(value, size):
    width = value.shape[1]
    lane = iota((size, width), 1) // DH
    total = jnp.zeros((size, width), value.dtype)
    for h in range(width // DH):
        total += jnp.where(lane == h, value[h * size : (h + 1) * size], 0.0)
    return total


def memory_valid(local, rows, live, owner):
    lane = iota((rows, local + SEG), 1)
    return (lane < live) | ((lane >= local) & (lane < local + M) & (owner > 0))


def attention1_kernel(slots, local, live_ref, owner_ref, gain, state, *refs):
    w = refs[:4]
    q_o, k_o, v_o, probs, out_tok, part, spread_k, spread_v = refs[4:]
    piece = local + SEG
    width = gain.shape[2]
    heads = width // DH
    normed = (normalize(state[...])[0] * gain_row(gain, 1, 0)).astype(BF)
    for j in range(4):
        proj = nn(normed, w[j][...]).astype(BF)
        lanes = pl.ds(j * HW, HW)
        q_o[:, lanes] = proj[:, :HW] * jnp.asarray(SCALE, BF)
        k_o[:, lanes] = proj[:, HW : 2 * HW]
        v_o[:, lanes] = proj[:, 2 * HW :]
    for ref in (q_o, k_o, v_o):
        ref.send()
    for s in range(slots):
        tok = pl.ds(s * piece, local)
        seg = pl.ds(s * piece + local, SEG)
        both = pl.ds(s * piece, piece)
        spread_heads(spread_k, q_o[seg, :])
        scores = nt(spread_k[...], k_o[both, :])
        valid = memory_valid(local, heads * SEG, live_ref[s], owner_ref[0])
        scores = jnp.where(valid, scores, FAR)
        top = jnp.max(scores, axis=1, keepdims=True)
        p = jnp.where(valid, jnp.exp(scores - top), 0.0)
        total = jnp.sum(p, axis=1, keepdims=True)
        here = pl.ds(s * SEG, SEG)
        part[here, pl.ds(0, width)] = fold_heads(nn(p.astype(BF), v_o[both, :]), SEG)
        lane = iota((SEG, HW), 1)
        extra = jnp.zeros((SEG, HW), F32)
        for h in range(heads):
            extra = jnp.where(lane == h, top[h * SEG : (h + 1) * SEG], extra)
            extra = jnp.where(lane == heads + h, total[h * SEG : (h + 1) * SEG], extra)
        part[here, pl.ds(width, HW)] = extra
    part.send()
    for s in range(slots):
        tok = pl.ds(s * piece, local)
        seg = pl.ds(s * piece + local, SEG)
        spread_heads(spread_k, k_o[seg, :])
        spread_heads(spread_v, v_o[seg, :])
        st = nt(spread_k[...], q_o[tok, :])
        st = jnp.where(iota((heads * SEG, local), 0) % SEG < M, st, FAR)
        st = st.reshape(heads, SEG, local)
        p = jnp.exp(st - jnp.max(st, axis=1, keepdims=True))
        p = p / jnp.sum(p, axis=1, keepdims=True)
        p = p.reshape(heads * SEG, local).T
        probs[s] = p
        out_tok[s] = nn(p.astype(BF), spread_v[...]).astype(BF)


def attention1(slots, local, live, owner, state, gain, w):
    rows, width = state.shape
    spread = (width // DH) * SEG
    return call(
        functools.partial(attention1_kernel, slots, local),
        (
            Away(rows, width),
            Away(rows, width),
            Away(rows, width),
            Away(slots, local, spread, dtype=F32),
            Away(slots, local, width),
            Away(slots * SEG, width + HW, dtype=F32),
        ),
        2 * rows * width * 3 * width + 8 * rows * width * spread,
        live,
        owner,
        gain,
        Far(state),
        *[packed_qkv(x) for x in w],
        scratch=[pltpu.VMEM((spread, width), BF), pltpu.VMEM((spread, width), BF)],
        name="attention1",
    )


def attention1_back_kernel(
    slots, local, share_ref, live_ref, owner_ref, gain, logs, grad_mid, *refs
):
    weights, (k, v, probs, q, mixed, state), w = refs[:4], refs[4:10], refs[10:14]
    refs = refs[6:]
    grads, grad_end, gain_sum, back, spread_a, spread_b, spread_o = refs[8:]
    piece = local + SEG
    width = gain.shape[2]
    heads = width // DH
    spread = heads * SEG
    low = grad_mid[...].astype(BF)
    for j in range(4):
        back[:, pl.ds(j * HW, HW)] = nt(low, weights[j][pl.ds(0, HW), :]).astype(BF)
    same = (iota((spread, spread), 0) // SEG == iota((spread, spread), 1) // SEG).astype(BF)

    def put(i, at, value):
        value = value.astype(BF)
        for j in range(4):
            grads[at, pl.ds(j * 3 * HW + i * HW, HW)] = value[:, j * HW : (j + 1) * HW]

    for s in range(slots):
        tok = pl.ds(s * piece, local)
        seg = pl.ds(s * piece + local, SEG)
        both = pl.ds(s * piece, piece)
        spread_heads(spread_a, k[seg, :])
        spread_heads(spread_b, v[seg, :])
        p = probs[s]
        dp = nt(back[tok, :], spread_b[...])
        product = p * dp
        hi = product.astype(BF)
        rest = (product - hi.astype(F32)).astype(BF)
        ds = (p * (dp - nn(hi, same) - nn(rest, same))).astype(BF)
        put(0, tok, nn(ds, spread_a[...]) * SCALE)
        mem_k = fold_heads(tn(ds, q[tok, :]), SEG)
        mem_v = fold_heads(tn(p.astype(BF), back[tok, :]), SEG)
        spread_heads(spread_a, q[seg, :])
        spread_heads(spread_b, back[seg, :])
        spread_heads(spread_o, mixed[seg, :])
        scores = nt(spread_a[...], k[both, :])
        log = jnp.concatenate([logs[pl.ds(s * SEG, SEG), :][:, h : h + 1] for h in range(heads)], axis=0)
        valid = memory_valid(local, spread, live_ref[s], owner_ref[0])
        p = jnp.where(valid, jnp.exp(jnp.where(valid, scores, FAR) - log), 0.0)
        delta = jnp.sum(
            spread_b[...].astype(F32) * spread_o[...].astype(F32), axis=1, keepdims=True
        )
        ds = (p * (nt(spread_b[...], v[both, :]) - delta)).astype(BF)
        put(0, seg, fold_heads(nn(ds, k[both, :]), SEG) * SCALE)
        grad_k = tn(ds, spread_a[...])
        grad_v = tn(p.astype(BF), spread_b[...])
        put(1, tok, grad_k[:local])
        put(2, tok, grad_v[:local])
        put(1, seg, grad_k[local:] + mem_k)
        put(2, seg, grad_v[local:] + mem_v)
    grads.send()
    normed, inverse = normalize(state[...])
    total = None
    for j in range(4):
        add = nt(grads[:, pl.ds(j * 3 * HW, 3 * HW)], w[j][...])
        total = add if j == 0 else total + add
    gain_sum[...] = jnp.sum(total * normed, axis=0, keepdims=True)
    grad_end[...] = once_rows(share_ref, slots, local, grad_mid[...]) + norm_backward(
        normed, inverse, gain_row(gain, 1, 0), total
    )


def attention1_back(
    slots, local, share, live, owner, gain, grad_mid, state, mixed, logs, q, k, v, probs, weights, w
):
    rows, width = state.shape
    spread = (width // DH) * SEG
    return call(
        functools.partial(attention1_back_kernel, slots, local),
        (
            Away(rows, 3 * width),
            Away(rows, width, dtype=F32),
            like(1, width, dtype=F32),
        ),
        2 * rows * width * 4 * width + 20 * rows * width * spread,
        share,
        live,
        owner,
        gain,
        logs,
        Far(grad_mid),
        *[Far(x, (HW, width), [((pl.ds(0, HW),), ())]) for x in weights],
        *[Far(x) for x in (k, v, probs, q, mixed, state)],
        *[packed_qkv(x) for x in w],
        scratch=[
            pltpu.VMEM((rows, width), BF),
            pltpu.VMEM((spread, width), BF),
            pltpu.VMEM((spread, width), BF),
            pltpu.VMEM((spread, width), BF),
        ],
        name="attention1_back",
    )


def attention1_weights_kernel(slots, local, share_ref, gain, grad_mid, mixed, state, grads, kept, sent):
    low = once_rows(share_ref, slots, local, grad_mid[...].astype(BF))
    grad_out = tn(mixed[...], low)
    normed = (normalize(state[...])[0] * gain_row(gain, 1, 0)).astype(BF)
    for j in (1, 3, 0, 2):
        target = kept if j % 2 == 0 else sent
        target[j // 2, pl.ds(0, HW), :] = grad_out[j * HW : (j + 1) * HW].astype(BF)
        target[j // 2, pl.ds(HW, 3 * HW), :] = tn(grads[:, pl.ds(j * 3 * HW, 3 * HW)], normed).astype(BF)
        if j == 3:
            sent.send()


def attention1_weights(slots, local, share, gain, grad_mid, state, mixed, grads):
    rows, width = state.shape
    return call(
        functools.partial(attention1_weights_kernel, slots, local),
        (Away(2, 4 * HW, width), Away(2, 4 * HW, width)),
        2 * rows * width * 4 * width,
        share,
        gain,
        Far(grad_mid),
        Far(mixed),
        Far(state),
        Far(grads),
        name="attention1_weights",
        early=True,
    )


def on_device(
    tokens, lengths, memory, norm_gain, w_qkv, output_weight, w_up, w_down, cot_tokens, cot_memory
):
    slots, local, width = tokens.shape
    me = lax.axis_index("tensor")
    block = jnp.arange(4, dtype=jnp.int32)
    valid = jnp.clip(lengths[:, None] - (me ^ block)[None, :] * local, 0, local)
    live = valid[:, 0]
    owner = (me == 0).astype(jnp.int32)[None]
    share = (jnp.arange(slots, dtype=jnp.int32) % 4 == me).astype(jnp.int32)

    near = exchange(tokens, "tensor", 1)
    tok = [Chain(far_chain(tokens[s])) for s in range(slots)]
    fence(None, *tok)
    move0 = Chain(weights_chain(pack_weights(output_weight[0], w_up[0], w_down[0], w_qkv[1])))
    move1 = Chain(weights_chain(jnp.concatenate([output_weight[1], w_up[1], w_down[1]], axis=0)))
    fence(None, tok[0])
    finish(tok[0])
    saved, outs, out_moves = [], [], []
    beside = [[move0], [], [move0, move1]]
    for s in range(slots):
        finish(tok[s])
        rest = [t.arrived for t in tok[2:]] if s == 1 else []
        received, rest = fence((tok[s].result, rest), *out_moves, *beside[s])
        for t, arrived in zip(tok[2:], rest):
            t.arrived = arrived
        *out, qa, ka, va = attention0(s, valid[s], tokens, (near, *received), memory, norm_gain, w_qkv)
        out[0] = land(out[0], *tok[s + 1 : s + 2], *([move0, move1] if s == slots - 1 else []))
        saved.append((qa, ka, va))
        outs.append(out)
        out_moves.append(Chain(split_chain(*out[1:])))
    tok_blocks = [(near, *t.result) for t in tok]
    fence(None, *out_moves)
    finish(*out_moves, move0)
    weights0 = move0.result
    moved = [m.result for m in out_moves]
    moved = fence(moved, move1)
    mid0, state1, *hid0, mixed0 = ffn0(
        tokens, memory, norm_gain, [o[0] for o in outs], moved, weights0
    )
    attn1 = weights0
    q1, k1, v1, probs, out_tok, parts = attention1(slots, local, live, owner, state1, norm_gain, attn1)
    probs = land(probs, move1)
    parts = Chain(gather_chain(parts))
    finish(parts, move1)
    weights1 = move1.result
    res_tok, res_mem, kept1, sent1, grad_mid1, gain_f1, mixed1, logs = ffn1(
        share, live, norm_gain, state1, out_tok, cot_tokens, cot_memory, parts.result, weights1
    )

    sum1a = Chain(rows_chain(kept1, sent1))
    copied = Chain(copy_chain(res_mem))
    grad_mid1 = fence(grad_mid1, sum1a, copied)
    proj1, grad1, gain_a1 = attention1_back(
        slots, local, share, live, owner, norm_gain, grad_mid1, state1, mixed1, logs, q1, k1, v1, probs,
        weights1, attn1,
    )
    proj1, grad1 = fence((proj1, grad1), sum1a, copied)
    kept1, sent1 = attention1_weights(slots, local, share, norm_gain, grad_mid1, state1, mixed1, proj1)
    sum1b = Chain(rows_chain(kept1, sent1))
    finish(copied)
    grad1, res_mem = fence((grad1, copied.result), sum1b)
    sent0, normed_sum = ffn0_back_sent(norm_gain, grad1, mid0, hid0, weights0)
    sum0 = Chain(core_chain([None, None], sent0))
    finish(sum1a)
    sum1a = Chain(halved(sum1a.result))
    normed_sum = fence(normed_sum, sum0, sum1a, sum1b)
    kept0, out_kept, out_sent, grad_tok, grad_mem, gain_f0, d_own, *d_moving = ffn0_back_kept(
        slots, local, norm_gain, grad1, normed_sum, mid0, hid0, mixed0, weights0
    )
    grad_mem = land(grad_mem, sum0, sum1a, sum1b)
    sum0o = Chain(core_chain(out_kept, out_sent))
    d_move = Chain(split_chain(*d_moving))
    fence(None, d_move)
    finish(sum1a, sum1b)
    sum1b = Chain(halved(sum1b.result))
    fence((), sum1b, sum0o)
    finish(sum0o)
    got = sum0.arrived[0]
    near = jnp.concatenate([added(kept0[0], got[0]), sum0o.result[0]])
    far = jnp.concatenate([added(kept0[1], got[1]), sum0o.result[1]])
    near, far, d_move.arrived = lax.optimization_barrier((near, far, d_move.arrived))
    sum0 = Chain(cross_chain(near, far))
    finish(d_move, sum1b)
    sum1 = Chain(two_halves(sum1a.result, sum1b.result))
    moved = [d_own, *d_move.result]
    before, row_sums = None, []
    for s in range(slots):
        moved = fence(moved, sum0, sum1, *row_sums)
        kept, sent, *before = attention0_back(
            s, tokens, tok_blocks[s], memory, norm_gain, w_qkv, saved[s], outs[s], moved, before
        )
        before[2] = land(before[2], sum0, sum1, *row_sums)
        row_sums.append(Chain(rows_chain(kept, sent)))
    grad_qkv0, mem_normed, gain_a0 = before
    small = [mem_normed[:M], grad_mem[:M], gain_a0, gain_a1, gain_f0, gain_f1]
    last = Chain(last_chain(grad_qkv0, jnp.concatenate(small, axis=0)))
    fence((), last, *row_sums)
    fence((), last, *row_sums, sum0)
    fence((), last, sum1)
    fence((), last, sum0)
    fence((), last)
    finish(last, sum0, sum1, *row_sums)
    sum0q, small = last.result
    sum1 = sum1.result
    sum0 = sum0.result
    rows = []
    for s in range(slots):
        normed, inverse = normalize(tokens[s].astype(F32))
        gain = norm_gain[0, 0].astype(F32)
        total = row_sums[s].result.astype(F32)
        rows.append(grad_tok[s] + norm_backward(normed, inverse, gain, total))
    normed, inverse = normalize(memory.astype(F32))
    grad_memory = small[M : 2 * M] + norm_backward(normed, inverse, gain, small[:M])
    gains = small[2 * M : 2 * M + 4]

    def split_qkv(value):
        return jnp.swapaxes(value.reshape(3, HW, width), 1, 2)

    return (
        res_tok,
        res_mem,
        jnp.stack(rows),
        grad_memory,
        gains[0:2],
        gains[2:4],
        jnp.stack([split_qkv(sum0q), split_qkv(sum1[2 * width + HW :])]).astype(F32),
        jnp.stack([sum0[2 * width :], sum1[2 * width : 2 * width + HW]]).astype(F32),
        jnp.stack([sum0[:width], sum1[:width]]).astype(F32),
        jnp.stack([sum0[width : 2 * width], sum1[width : 2 * width]]).astype(F32),
    )


def solution(mesh):
    return jax.shard_map(
        on_device,
        mesh=mesh,
        in_specs=(
            P("dp", "tensor", None),
            P("dp"),
            P(),
            P(),
            P(None, None, None, "tensor"),
            P(None, "tensor", None),
            P(None, None, "tensor"),
            P(None, "tensor", None),
            P("dp", "tensor", None),
            P("dp", None, None),
        ),
        out_specs=(
            P("dp", "tensor", None),
            P("dp", None, None),
            P("dp", "tensor", None),
            P(),
            P(),
            P(),
            P(None, None, None, "tensor"),
            P(None, "tensor", None),
            P(None, None, "tensor"),
            P(None, "tensor", None),
        ),
        check_vma=False,
    )
```

```python
import functools

import jax
import jax.numpy as jnp
from jax import lax
from jax.experimental import pallas as pl
from jax.experimental.pallas import tpu as pltpu
from jax.sharding import PartitionSpec as P

DH = 64
M = 20
SEG = 32
HW = 2 * DH
EPS = 1e-05
SCALE = DH**-0.5
FAR = -1e30
BF = jnp.bfloat16
F32 = jnp.float32


def exchange(value, axis, mask):
    return lax.ppermute(value, axis, [(i, i ^ mask) for i in range(lax.axis_size(axis))])


class Chain:
    def __init__(self, generator):
        self.generator = generator
        self.arrived = None
        self.result = None
        self.wanted = []
        self.done = False

    def ask(self):
        try:
            self.wanted = self.generator.send(self.arrived)
        except StopIteration as stop:
            self.result = stop.value
            self.wanted = []
            self.done = True


def fence(inputs, *chains):
    chains = [c for c in chains if not c.done]
    for chain in chains:
        chain.ask()
    leaving = [[item[0] for item in chain.wanted] for chain in chains]
    if inputs is not None:
        inputs, leaving = lax.optimization_barrier((inputs, leaving))
    for chain, arrays in zip(chains, leaving):
        chain.arrived = [
            exchange(array, item[1], item[2]) for array, item in zip(arrays, chain.wanted)
        ]
    return inputs


def land(outputs, *chains):
    chains = [c for c in chains if not c.done]
    outputs, arrived = lax.optimization_barrier((outputs, [c.arrived for c in chains]))
    for chain, arrays in zip(chains, arrived):
        chain.arrived = arrays
    return outputs


def finish(*chains):
    while not all(c.done for c in chains):
        fence(None, *chains)


def far_chain(block):
    (far,) = yield [(block, "tensor", 2)]
    (last,) = yield [(far, "tensor", 1)]
    return [far, last]


def gather_chain(block):
    near, far = yield [(block, "tensor", 1), (block, "tensor", 2)]
    (last,) = yield [(far, "tensor", 1)]
    return [block, near, far, last]


def weights_chain(block):
    half = block.shape[0] // 2
    bit = lax.axis_index("dp") % 2
    (first,) = yield [(lax.dynamic_slice_in_dim(block, bit * half, half, 0), "tensor", 2)]
    (second,) = yield [(first, "dp", 1)]
    far = jnp.concatenate(
        [jnp.where(bit == 0, first, second), jnp.where(bit == 0, second, first)], axis=0
    )
    last, near = yield [(far, "tensor", 1), (block, "tensor", 1)]
    return [block, near, far, last]


def split_chain(near, pair):
    pair, near = yield [(pair, "tensor", 2), (near, "tensor", 1)]
    (other,) = yield [(pair, "tensor", 1)]
    return [near, pair, other]


def added(a, b):
    return (a.astype(F32) + b.astype(F32)).astype(BF)


def core_chain(kept, sent):
    (got,) = yield [(sent, "tensor", 1)]
    return (added(kept[0], got[0]), added(kept[1], got[1]))


def rows_chain(kept, sent):
    near, far = yield from core_chain(kept, sent)
    (got,) = yield [(far, "tensor", 2)]
    return added(near, got)


def dp_masks():
    size = lax.axis_size("dp")
    masks = []
    while 1 << len(masks) < size:
        masks.append(1 << len(masks))
    return masks


def dp_bit(mask):
    return (lax.axis_index("dp") // mask) % 2


def part(value, mask, other=False):
    half = value.shape[0] // 2
    bit = dp_bit(mask)
    return lax.dynamic_slice_in_dim(value, ((1 - bit) if other else bit) * half, half, 0)


def joined(value, got, mask):
    first = dp_bit(mask) == 0
    return jnp.concatenate([jnp.where(first, value, got), jnp.where(first, got, value)], axis=0)


def reduced(value, masks, whole):
    halves = masks[: len(masks) - whole]
    for mask in halves:
        (got,) = yield [(part(value, mask, True), "dp", mask)]
        value = added(part(value, mask), got)
    for mask in masks[len(halves) :]:
        (got,) = yield [(value, "dp", mask)]
        value = added(value, got)
    for mask in reversed(halves):
        (got,) = yield [(value, "dp", mask)]
        value = joined(value, got, mask)
    return value


def cross_steps(near, far):
    half = near.shape[0] // 2
    near_a, near_b = near[:half], near[half:]
    far_a, far_b = far[:half], far[half:]
    pair = jnp.stack([part(near_b, 1, True), part(far_b, 1, True)])
    got_a, got_b = yield [(far_a, "tensor", 2), (pair, "dp", 1)]
    near_a = added(near_a, got_a)
    near_b = added(part(near_b, 1), got_b[0])
    far_b = added(part(far_b, 1), got_b[1])
    got_a, got_b = yield [(part(near_a, 1, True), "dp", 1), (far_b, "tensor", 2)]
    return jnp.concatenate([added(part(near_a, 1), got_a), added(near_b, got_b)], axis=0)


def cross_joined(value, got):
    half = value.shape[0] // 2
    return jnp.concatenate([joined(value[:half], got[:half], 1), joined(value[half:], got[half:], 1)])


def cross_chain(near, far):
    value = yield from cross_steps(near, far)
    value = yield from reduced(value, dp_masks()[1:], 1)
    (got,) = yield [(value, "dp", 1)]
    return cross_joined(value, got)


def halved(value):
    (got,) = yield [(part(value, 1, True), "dp", 1)]
    return added(part(value, 1), got)


def two_halves(first, second):
    rows = first.shape[0]
    value = jnp.concatenate([first, second])
    value = yield from reduced(value, dp_masks()[1:], 1)
    (got,) = yield [(value, "dp", 1)]
    return jnp.concatenate([joined(value[:rows], got[:rows], 1), joined(value[rows:], got[rows:], 1)])


def copy_chain(value):
    me = lax.axis_index("tensor")
    (got,) = yield [(value, "tensor", 2)]
    value = jnp.where(me // 2 == 0, value, got)
    (got,) = yield [(value, "tensor", 1)]
    return jnp.where(me % 2 == 0, value, got)


def last_chain(grad, small):
    (got,) = yield [(small, "tensor", 1)]
    small = small + got
    got, far = yield [(part(grad, 1, True), "dp", 1), (small, "tensor", 2)]
    grad = added(part(grad, 1), got)
    small = small + far
    rows = grad.shape[0]
    value = jnp.concatenate([grad, small.astype(BF)])
    masks = dp_masks()[1:]
    value = yield from reduced(value, masks, len(masks))
    (got,) = yield [(value, "dp", 1)]
    return (joined(value[:rows], got[:rows], 1), value[rows:].astype(F32) + got[rows:].astype(F32))


def nn(a, b):
    return lax.dot_general(a, b, (((1,), (0,)), ((), ())), preferred_element_type=F32)


def nt(a, b):
    return lax.dot_general(a, b, (((1,), (1,)), ((), ())), preferred_element_type=F32)


def tn(a, b):
    return lax.dot_general(a, b, (((0,), (0,)), ((), ())), preferred_element_type=F32)


def normalize(state):
    center = jnp.mean(state, axis=-1, keepdims=True)
    shifted = state - center
    spread = jnp.mean(shifted * shifted, axis=-1, keepdims=True)
    inverse = lax.rsqrt(spread + EPS)
    return (shifted * inverse, inverse)


def norm_backward(normed, inverse, gain_row, grad_normed):
    scaled = grad_normed * gain_row
    return inverse * (
        scaled
        - jnp.mean(scaled, axis=-1, keepdims=True)
        - normed * jnp.mean(scaled * normed, axis=-1, keepdims=True)
    )


def gelu_parts(hidden, with_slope):
    c = 0.7978845608028654
    a = 0.044715
    square = hidden * hidden
    t = jnp.tanh(hidden * (c + (c * a) * square))
    up = 0.5 + 0.5 * t
    active = hidden * up
    if not with_slope:
        return active
    slope = up + hidden * (0.5 - 0.5 * t * t) * (c + (3.0 * c * a) * square)
    return (active, slope)


def iota(shape, axis):
    return lax.broadcasted_iota(jnp.int32, shape, axis)


class Far:
    def __init__(self, array, shape=None, pieces=None):
        self.array = array
        self.shape = array.shape if shape is None else shape
        self.pieces = [((), ())] if pieces is None else pieces


class Away:
    def __init__(self, *shape, dtype=BF):
        self.shape = shape
        self.dtype = dtype


def at(ref, index):
    return ref.at[index] if index else ref


class Incoming:
    def __init__(self, ref, copies):
        self.ref = ref
        self.copies = copies
        self.shape = ref.shape
        for copy in copies:
            copy.start()

    def wait(self):
        for copy in self.copies:
            copy.wait()
        self.copies = []

    def __getitem__(self, index):
        self.wait()
        return self.ref[index]


class Outgoing:
    def __init__(self, ref, copy, early):
        self.ref = ref
        self.copy = copy
        self.early = early
        self.sent = False

    def __setitem__(self, index, value):
        self.ref[index] = value

    def __getitem__(self, index):
        return self.ref[index]

    def send(self):
        if self.early:
            self.start()

    def start(self):
        if not self.sent:
            self.copy.start()
        self.sent = True


def call(kernel, results, cost, *operands, scratch=(), name=None, limit=60, early=False):
    arrays = [o.array if isinstance(o, Far) else o for o in operands]
    specs, buffers, count = [], [], 0
    for o in operands:
        if isinstance(o, Far):
            specs.append(pl.BlockSpec(memory_space=pltpu.HBM))
            buffers.append(pltpu.VMEM(o.shape, o.array.dtype))
            count += len(o.pieces)
        else:
            space = pltpu.SMEM if o.dtype == jnp.int32 else pltpu.VMEM
            specs.append(pl.BlockSpec(memory_space=space))
    out_specs = []
    for r in results:
        away = isinstance(r, Away)
        out_specs.append(pl.BlockSpec(memory_space=pltpu.HBM if away else pltpu.VMEM))
        if away:
            buffers.append(pltpu.VMEM(r.shape, r.dtype))
            count += 1

    def body(*refs):
        ins = refs[: len(operands)]
        outs = refs[len(operands) : len(operands) + len(results)]
        rest = list(refs[len(operands) + len(results) :])
        sem = rest.pop()
        used = iter(range(count))
        local_buffers = iter(rest[: len(buffers)])
        given = []
        for o, ref in zip(operands, ins):
            if isinstance(o, Far):
                buffer = next(local_buffers)
                ref = Incoming(
                    buffer,
                    [
                        pltpu.make_async_copy(at(ref, src), at(buffer, dst), sem.at[next(used)])
                        for src, dst in o.pieces
                    ],
                )
            given.append(ref)
        taken = []
        for r, ref in zip(results, outs):
            if isinstance(r, Away):
                buffer = next(local_buffers)
                ref = Outgoing(buffer, pltpu.make_async_copy(buffer, ref, sem.at[next(used)]), early)
            taken.append(ref)
        if not early:
            for ref in given:
                if isinstance(ref, Incoming):
                    ref.wait()
        kernel(*given, *taken, *rest[len(buffers) :])
        for ref in given:
            if isinstance(ref, Incoming):
                ref.wait()
        for ref in taken:
            if isinstance(ref, Outgoing):
                ref.start()
        for ref in taken:
            if isinstance(ref, Outgoing):
                ref.copy.wait()

    moved = sum(o.size * o.dtype.itemsize for o in arrays)
    return pl.pallas_call(
        body,
        out_shape=[jax.ShapeDtypeStruct(r.shape, r.dtype) for r in results],
        in_specs=specs,
        out_specs=out_specs,
        scratch_shapes=buffers + list(scratch) + [pltpu.SemaphoreType.DMA((max(count, 1),))],
        compiler_params=pltpu.CompilerParams(vmem_limit_bytes=limit * 1024 * 1024),
        cost_estimate=pl.CostEstimate(flops=cost // 64, bytes_accessed=moved // 64, transcendentals=0),
        name=name,
    )(*arrays)


def like(*shape, dtype=BF):
    return jax.ShapeDtypeStruct(shape, dtype)


def qkv_pieces(sources):
    return [
        (tuple(prefix) + (i,), (slice(None), pl.ds((3 * j + i) * HW, HW)))
        for j, prefix in enumerate(sources)
        for i in range(3)
    ]


def gain_row(gain_ref, layer, which):
    return gain_ref[layer, pl.ds(which, 1), :].astype(F32)


def pad_rows(scratch, value):
    scratch[...] = jnp.zeros_like(scratch)
    scratch[pl.ds(0, value.shape[0]), :] = value.astype(F32)


def head_lanes(rows, h):
    lane = iota((rows, HW), 1)
    inside = (lane >= h * DH) & (lane < (h + 1) * DH)
    return lane - (1 - h) * DH, inside


def attention0_kernel(
    local, valid_ref, mem, gain, x0, x1, x2, x3, w, own, near, pair, qa, ka, va, vh, mem_s
):
    keys = 4 * local + SEG
    tokens = [x0, x1, x2, x3]
    pad_rows(mem_s, mem[...])
    blocks = [(j * local, local, tokens[j]) for j in range(4)] + [(4 * local, SEG, mem_s)]
    for j, (start, size, ref) in enumerate(blocks):
        normed, _ = normalize(ref[...].astype(F32))
        normed = (normed * gain_row(gain, 0, 0)).astype(BF)
        proj = nn(normed, w[...]).astype(BF)
        q = proj[:, :HW] * jnp.asarray(SCALE, BF)
        k = proj[:, HW : 2 * HW]
        v = proj[:, 2 * HW :]
        rows = pl.ds(start, size)
        va[rows, :] = v
        valid = iota((size, HW), 0) < (valid_ref[j] if j < 4 else M)
        bias = jnp.where(valid, 0.0, FAR).astype(BF)
        for h in range(2):
            spare, inside = head_lanes(size, h)
            one = jnp.where(spare == 0, 1.0, 0.0).astype(BF)
            extra = jnp.where((spare >= 1) & (spare <= 3), 1.0, 0.0).astype(BF)
            ka[h, rows, :] = jnp.where(inside, k, jnp.where(spare == 0, bias, extra))
            qa[h, rows, :] = jnp.where(inside, q, one)
            vh[h, rows, :] = jnp.where(inside, v, one)
    ka.send()
    va.send()

    def chunk(start, size):
        rows = pl.ds(start, size)
        out = None
        for h in range(2):
            spare, inside = head_lanes(size, h)
            q = qa[h, rows, :]
            scores = nt(q, ka[h])
            top = jnp.max(scores, axis=1, keepdims=True)
            o = nn(jnp.exp(scores - top).astype(BF), vh[h])
            total = o[:, (1 - h) * DH : (1 - h) * DH + 1]
            col = -(top + jnp.log(total))
            hi = col.astype(BF).astype(F32)
            mid = (col - hi).astype(BF).astype(F32)
            low = col - hi - mid
            extra = jnp.where(spare == 1, hi, jnp.where(spare == 2, mid, jnp.where(spare == 3, low, 0.0)))
            qa[h, rows, :] = jnp.where(inside | (spare == 0), q, extra.astype(BF))
            o = o / total
            out = o if h == 0 else jnp.where(inside, o, out)
        return out.astype(BF)

    out = chunk(4 * local, SEG)
    rows = pl.ds(local, SEG)
    own[rows, :] = out
    near[rows, :] = out
    pair[0, rows, :] = out
    pair[1, rows, :] = out
    rows = pl.ds(0, local)
    out = chunk(2 * local, 2 * local)
    pair[0, rows, :] = out[:local]
    pair[1, rows, :] = out[local:]
    pair.send()
    out = chunk(0, 2 * local)
    own[rows, :] = out[:local]
    near[rows, :] = out[local:]


def pack_weights(out, up, down, qkv):
    parts = [up, down, jnp.concatenate([out[:, i * HW : (i + 1) * HW] for i in range(4)], axis=0)]
    return jnp.concatenate(parts + [qkv[i] for i in range(3)], axis=1)


def packed_out(width):
    lanes = pl.ds(2 * width, HW)
    return [((pl.ds(i * HW, HW), lanes), (pl.ds(0, HW), pl.ds(i * HW, HW))) for i in range(4)]


def packed_ffn(width):
    pieces = [
        ((slice(None), pl.ds(i * width, width)), (pl.ds(HW + i * width, width), slice(None)))
        for i in range(2)
    ]
    return packed_out(width) + pieces


def packed(block, only_out=False):
    width = block.shape[0]
    if only_out:
        return Far(block, (HW, width), packed_out(width))
    return Far(block, (HW + 2 * width, width), packed_ffn(width))


def packed_qkv(block):
    width = block.shape[0]
    return Far(block, (width, 3 * HW), [((slice(None), pl.ds(2 * width + HW, 3 * HW)), ())])


def token_blocks(s, tokens, blocks):
    shape = tokens.shape[1:]
    near, far, last = blocks
    own = Far(tokens, shape, [((s,), ())])
    return [own, Far(near, shape, [((s,), ())]), Far(far), Far(last)]


def attention0(s, valid, tokens, blocks, memory, gain, w_qkv):
    _, local, width = tokens.shape
    keys = 4 * local + SEG
    piece = local + SEG
    cost = 2 * keys * width * 3 * HW + 16 * keys * keys * HW
    return call(
        functools.partial(attention0_kernel, local),
        (
            Away(piece, HW),
            Away(piece, HW),
            Away(2, piece, HW),
            Away(2, keys, HW),
            Away(2, keys, HW),
            Away(keys, HW),
        ),
        cost,
        valid,
        memory,
        gain,
        *token_blocks(s, tokens, blocks),
        Far(w_qkv, (width, 3 * HW), qkv_pieces([(0,)])),
        scratch=[pltpu.VMEM((2, keys, HW), BF), pltpu.VMEM((SEG, width), F32)],
        name="attention0",
    )


def attention0_back_kernel(
    local, first_call, last_call, mem, gain, before_mem, before_gain, g_own, g_near, g_far, g_last,
    o_own, o_near, o_pair, va, ka, qa, x1, x3, x0, x2, w, before_w,
    kept, sent, grad_w, mem_normed, gain_sum,
    grads, va_s, da_s, d_s, acc_v, acc_k, mem_s,
):
    keys = 4 * local + SEG
    pad_rows(mem_s, mem[...])
    own = pl.ds(0, local)
    pieces = [
        (0, g_own[own, :], o_own[own, :]),
        (local, g_near[own, :], o_near[own, :]),
        (2 * local, g_far[own, :], o_pair[0, own, :]),
        (3 * local, g_last[own, :], o_pair[1, own, :]),
    ]
    tail = pl.ds(local, SEG)
    parts = [g[tail, :].astype(F32) for g in (g_own, g_near, g_far, g_last)]
    grad = ((parts[0] + parts[1]) + (parts[2] + parts[3])).astype(BF)
    pieces.append((4 * local, grad, o_own[tail, :]))
    for start, grad, out in pieces:
        size = grad.shape[0]
        rows = pl.ds(start, size)
        product = grad.astype(F32) * out.astype(F32)
        d_s[rows, :] = grad
        for h in range(2):
            spare, inside = head_lanes(size, h)
            col = -jnp.sum(jnp.where(inside, product, 0.0), axis=-1, keepdims=True)
            hi = col.astype(BF).astype(F32)
            extra = jnp.where(spare == 0, hi, jnp.where(spare == 1, col - hi, 0.0))
            da_s[h, rows, :] = jnp.where(inside, grad, extra.astype(BF))
    for h in range(2):
        spare, inside = head_lanes(keys, h)
        ones = jnp.where((spare == 0) | (spare == 1), 1.0, 0.0).astype(BF)
        va_s[h] = jnp.where(inside, va[...], ones)
    first = iota((keys, HW), 1) < DH
    key = jnp.where(first, ka[0], ka[1])

    def chunk(start, size, fresh):
        rows = pl.ds(start, size)
        turned = []
        for h in range(2):
            p = jnp.exp(nt(ka[h], qa[h, rows, :]))
            dp = nt(va_s[h], da_s[h, rows, :])
            ds = (p * dp).astype(BF)
            add_v = nn(p.astype(BF), d_s[rows, :])
            add_k = nn(ds, qa[h, rows, :])
            if fresh:
                acc_v[h] = add_v
                acc_k[h] = add_k
            else:
                acc_v[h] += add_v
                acc_k[h] += add_k
            turned.append(tn(ds, key))
        out = jnp.where(iota((size, HW), 1) < DH, turned[0], turned[1]) * SCALE
        grads[rows, :HW] = out.astype(BF)

    chunk(0, 2 * local, True)
    chunk(2 * local, 2 * local, False)
    rows = pl.ds(4 * local, SEG)
    turned = []
    for h in range(2):
        p = jnp.exp(nt(qa[h, rows, :], ka[h]))
        ds = (p * nt(da_s[h, rows, :], va_s[h])).astype(BF)
        acc_v[h] += tn(p.astype(BF), d_s[rows, :])
        acc_k[h] += tn(ds, qa[h, rows, :])
        turned.append(nn(ds, key))
    out = jnp.where(iota((SEG, HW), 1) < DH, turned[0], turned[1]) * SCALE
    grads[rows, :HW] = out.astype(BF)
    grads[:, HW : 2 * HW] = jnp.where(first, acc_k[0], acc_k[1]).astype(BF)
    grads[:, 2 * HW :] = jnp.where(first, acc_v[0], acc_v[1]).astype(BF)

    tokens = [x0, x1, x2, x3]
    total_w = None if first_call else before_w[...]
    total_gain = None if first_call else before_gain[...]
    for j in (1, 3, 0, 2, 4):
        size = local if j < 4 else SEG
        ref = tokens[j] if j < 4 else mem_s
        normed, _ = normalize(ref[...].astype(F32))
        low = (normed * gain_row(gain, 0, 0)).astype(BF)
        part = grads[pl.ds(j * local, size), :]
        add_w = tn(part, low)
        grad_normed = nt(part, w[...])
        add_gain = jnp.sum(grad_normed * normed, axis=0, keepdims=True)
        total_w = add_w if total_w is None else total_w + add_w
        total_gain = add_gain if total_gain is None else total_gain + add_gain
        if j == 4:
            mem_normed[...] = grad_normed if first_call else grad_normed + before_mem[...]
        else:
            target = kept if j % 2 == 0 else sent
            target[j // 2] = grad_normed.astype(BF)
            if j == 3:
                sent.send()
            if j == 2:
                kept.send()
    grad_w[...] = total_w.astype(BF if last_call else F32)
    gain_sum[...] = total_gain


def attention0_back(s, tokens, blocks, memory, gain, w_qkv, saved, outs, moved, before):
    slots, local, width = tokens.shape
    keys = 4 * local + SEG
    cost = 4 * keys * width * 3 * HW + 40 * keys * keys * HW
    first_call, last_call = before is None, s == slots - 1
    if first_call:
        before = [memory] * 3
    before_w, before_mem, before_gain = before
    qa, ka, va = saved
    block = (local + SEG, HW)
    return call(
        functools.partial(attention0_back_kernel, local, first_call, last_call),
        (
            Away(2, local, width),
            Away(2, local, width),
            Away(3 * HW, width, dtype=BF if last_call else F32),
            like(SEG, width, dtype=F32),
            like(1, width, dtype=F32),
        ),
        cost,
        memory,
        gain,
        before_mem,
        before_gain,
        *[Far(g, block, [((s,), ())]) for g in moved[:2]],
        Far(moved[2], block, [((0, s), ())]),
        Far(moved[3], block, [((1, s), ())]),
        *[Far(o) for o in outs],
        Far(va),
        Far(ka),
        Far(qa),
        *[token_blocks(s, tokens, blocks)[j] for j in (1, 3, 0, 2)],
        Far(w_qkv, (width, 3 * HW), qkv_pieces([(0,)])),
        Far(before_w),
        scratch=[
            pltpu.VMEM((keys, 3 * HW), BF),
            pltpu.VMEM((2, keys, HW), BF),
            pltpu.VMEM((2, keys, HW), BF),
            pltpu.VMEM((keys, HW), BF),
            pltpu.VMEM((2, keys, HW), F32),
            pltpu.VMEM((2, keys, HW), F32),
            pltpu.VMEM((SEG, width), F32),
        ],
        name="attention0_back",
    )


def ffn0_kernel(slots, local, mem, gain, *refs):
    tokens, own, refs = refs[0], refs[1 : 1 + slots], refs[1 + slots :]
    moved, weights = refs[: 3 * slots], refs[3 * slots : 4 + 3 * slots]
    mid, end, hid0, hid1, hid2, hid3, mixed, normed_s, mem_s = refs[4 + 3 * slots :]
    hid = [hid0, hid1, hid2, hid3]
    piece = local + SEG
    width = gain.shape[2]
    inner = weights[0].shape[0] - HW - width
    pad_rows(mem_s, mem[...])
    for s in range(slots):
        rows = pl.ds(s * piece, piece)
        state = jnp.concatenate([tokens[s].astype(F32), mem_s[...]], axis=0)
        for j in range(4):
            out = own[s][...] if j == 0 else moved[3 * s + j - 1][...]
            mixed[rows, pl.ds(j * HW, HW)] = out
            state += nn(out, weights[j][pl.ds(0, HW), :])
        mid[rows, :] = state
        end[rows, :] = state
        normed_s[rows, :] = (normalize(state)[0] * gain_row(gain, 0, 1)).astype(BF)
    mid.send()
    mixed.send()
    for j in range(4):
        hid[j][...] = nn(normed_s[...], weights[j][pl.ds(HW, width), :]).astype(BF)
        hid[j].send()
    for j in range(4):
        active = gelu_parts(hid[j][...].astype(F32), False).astype(BF)
        end[...] += nn(active, weights[j][pl.ds(HW + width, inner), :])


def ffn0(tokens, memory, gain, own, moved, weights):
    slots, local, width = tokens.shape
    rows = slots * (local + SEG)
    inner = width
    return call(
        functools.partial(ffn0_kernel, slots, local),
        (
            Away(rows, width, dtype=F32),
            Away(rows, width, dtype=F32),
            Away(rows, inner),
            Away(rows, inner),
            Away(rows, inner),
            Away(rows, inner),
            Away(rows, width),
        ),
        2 * rows * width * (width + 8 * inner),
        memory,
        gain,
        Far(tokens),
        *[Far(o) for o in own],
        *[
            Far(m, (local + SEG, HW), [((j,), ())] if m.ndim == 3 else None)
            for near, pair, other in moved
            for m, j in ((near, None), (pair, 0), (other, 1))
        ],
        *[packed(w) for w in weights],
        scratch=[pltpu.VMEM((rows, width), BF), pltpu.VMEM((SEG, width), F32)],
        name="ffn0",
        early=True,
    )


def ffn_back_core(weights, low, low_once, hidden_of, normed, normed_once, targets, with_output):
    width = normed.shape[1]
    inner = weights[targets[0][0]].shape[0] - HW - width
    total, output = None, None
    for j, target, slot in targets:
        up = weights[j][pl.ds(HW, width), :]
        down = weights[j][pl.ds(HW + width, inner), :]
        active, slope = gelu_parts(hidden_of(j), True)
        active = active.astype(BF)
        if with_output:
            add = nn(active, down)
            output = add if output is None else output + add
        grad_hidden = (nt(low, down) * slope).astype(BF)
        target[slot, pl.ds(0, width), :] = tn(normed_once, grad_hidden).astype(BF)
        target[slot, pl.ds(width, inner), :] = tn(active, low_once).astype(BF)
        if slot == 1:
            target.send()
        add = nt(grad_hidden, up)
        total = add if total is None else total + add
    return (total, output)


def once_rows(share_ref, slots, local, value):
    piece = local + SEG
    parts = []
    for s in range(slots):
        parts.append(value[s * piece : s * piece + local])
        tail = value[s * piece + local : (s + 1) * piece]
        parts.append(jnp.where(share_ref[s] > 0, tail, jnp.zeros_like(tail)))
    return jnp.concatenate(parts, axis=0)


def ffn1_kernel(slots, local, share_ref, live_ref, gain, cot_mem, *refs):
    parts, out_tok, cot, state, weights = refs[:4], refs[4], refs[5], refs[6], refs[7:11]
    (res_tok, res_mem, kept, sent, grad_mid, gain_sum, mixed, logs) = refs[11:19]
    normed_s, end_s, low_s, mem_s = refs[19:]
    piece = local + SEG
    width = gain.shape[2]
    heads = width // DH
    gain_f = gain_row(gain, 1, 1)
    lane = iota((SEG, HW), 1)
    mixed_rows = []
    for s in range(slots):
        seg = pl.ds(s * SEG, SEG)
        scale = {}
        log = jnp.zeros((SEG, HW), F32)
        extras = [parts[j][seg, pl.ds(width, HW)] for j in range(4)]
        for h in range(heads):
            source = [2 * ((h // 2) ^ j) + h % 2 for j in range(4)]
            tops = [extras[j][:, source[j] : source[j] + 1] for j in range(4)]
            sums = [extras[j][:, heads + source[j] : heads + source[j] + 1] for j in range(4)]
            peak = functools.reduce(jnp.maximum, tops)
            raised = [jnp.exp(t - peak) for t in tops]
            total = functools.reduce(jnp.add, [r * t for r, t in zip(raised, sums)])
            scale[h] = [r / total for r in raised]
            log = jnp.where(lane == h, peak + jnp.log(total), log)
        logs[seg, :] = log
        for b in range(4):
            merged = jnp.zeros((SEG, HW), F32)
            for j in range(4):
                factor = jnp.where(lane < DH, scale[2 * b][j], scale[2 * b + 1][j])
                merged += factor * parts[j][seg, pl.ds((b ^ j) * HW, HW)]
            mixed[pl.ds(s * piece + local, SEG), pl.ds(b * HW, HW)] = merged.astype(BF)
        rows = pl.ds(s * piece, local)
        mixed[rows, :] = out_tok[s]
        live = iota((local, 1), 0) < live_ref[s]
        low_s[rows, :] = jnp.where(live, cot[s], jnp.zeros_like(cot[s]))
        pad_rows(mem_s, cot_mem[s])
        low_s[pl.ds(s * piece + local, SEG), :] = mem_s[...].astype(BF)
    mixed.send()
    mid = state[...]
    for j in range(4):
        mid += nn(mixed[:, pl.ds(j * HW, HW)], weights[j][pl.ds(0, HW), :])
    end_s[...] = mid
    mid_normed, inverse = normalize(mid)
    normed = (mid_normed * gain_f).astype(BF)
    normed_s[...] = mid_normed
    low = low_s[...]
    grad_normed, output = ffn_back_core(
        weights,
        low,
        once_rows(share_ref, slots, local, low),
        lambda j: nn(normed, weights[j][pl.ds(HW, width), :]),
        normed,
        once_rows(share_ref, slots, local, normed),
        [(1, sent, 0), (3, sent, 1), (0, kept, 0), (2, kept, 1)],
        True,
    )
    end_s[...] += output
    for s in range(slots):
        res_tok[s] = end_s[pl.ds(s * piece, local), :].astype(BF)
        res_mem[s] = end_s[pl.ds(s * piece + local, M), :].astype(BF)
    res_tok.send()
    mid_normed = normed_s[...]
    gain_sum[...] = jnp.sum(
        once_rows(share_ref, slots, local, grad_normed * mid_normed), axis=0, keepdims=True
    )
    grad_mid[...] = low_s[...].astype(F32) + norm_backward(mid_normed, inverse, gain_f, grad_normed)


def ffn1(share, live, gain, state, out_tok, cot, cot_mem, parts, weights):
    slots, local, width = cot.shape
    rows = slots * (local + SEG)
    inner = weights[0].shape[0] - HW - width
    return call(
        functools.partial(ffn1_kernel, slots, local),
        (
            Away(slots, local, width),
            like(slots, M, width),
            Away(2, width + inner, width),
            Away(2, width + inner, width),
            Away(rows, width, dtype=F32),
            like(1, width, dtype=F32),
            Away(rows, width),
            like(slots * SEG, HW, dtype=F32),
        ),
        2 * rows * width * (width + 24 * inner),
        share,
        live,
        gain,
        cot_mem,
        *[Far(p) for p in parts],
        Far(out_tok),
        Far(cot),
        Far(state),
        *[Far(w) for w in weights],
        scratch=[
            pltpu.VMEM((rows, width), F32),
            pltpu.VMEM((rows, width), F32),
            pltpu.VMEM((rows, width), BF),
            pltpu.VMEM((SEG, width), F32),
        ],
        name="ffn1",
        early=True,
    )


def ffn0_back_sent_kernel(gain, grad_in, mid, hid_near, hid_last, w_near, w_last, sent, normed_sum):
    low = grad_in[...].astype(BF)
    normed = (normalize(mid[...])[0] * gain_row(gain, 0, 1)).astype(BF)
    hidden = {1: hid_near, 3: hid_last}
    normed_sum[...], _ = ffn_back_core(
        {1: w_near, 3: w_last},
        low,
        low,
        lambda j: hidden[j][...].astype(F32),
        normed,
        normed,
        [(1, sent, 0), (3, sent, 1)],
        False,
    )


def ffn0_back_sent(gain, grad_in, mid, hid, weights):
    rows, width = grad_in.shape
    inner = width
    return call(
        ffn0_back_sent_kernel,
        (Away(2, width + inner, width), Away(rows, width, dtype=F32)),
        2 * rows * width * (8 * inner),
        gain,
        Far(grad_in),
        Far(mid),
        Far(hid[1]),
        Far(hid[3]),
        packed(weights[1]),
        packed(weights[3]),
        name="ffn0_back_sent",
        early=True,
    )


def ffn0_back_kept_kernel(
    slots, local, gain, grad_in, mid, hid_own, hid_far, w0, w2, w1, w3, normed_sum, mixed,
    kept, out_kept, out_sent, grad_tok, grad_mem, gain_sum, d_own, d_near, d_pair
):
    weights = [w0, w1, w2, w3]
    piece = local + SEG
    width = gain.shape[2]
    low = grad_in[...].astype(BF)
    mid_normed, inverse = normalize(mid[...])
    normed = (mid_normed * gain_row(gain, 0, 1)).astype(BF)
    hidden = {0: hid_own, 2: hid_far}
    grad_normed, _ = ffn_back_core(
        weights,
        low,
        low,
        lambda j: hidden[j][...].astype(F32),
        normed,
        normed,
        [(0, kept, 0), (2, kept, 1)],
        False,
    )
    grad_normed += normed_sum[...]
    grad = grad_in[...] + norm_backward(mid_normed, inverse, gain_row(gain, 0, 1), grad_normed)
    low = grad.astype(BF)
    for j in (3, 2, 1, 0):
        back = nt(low, weights[j][pl.ds(0, HW), :]).astype(BF)
        for s in range(slots):
            value = back[s * piece : (s + 1) * piece]
            if j >= 2:
                d_pair[j - 2, s] = value
            else:
                (d_own, d_near)[j][s] = value
        if j < 3:
            (d_own, d_near, d_pair)[j].send()
    gain_sum[...] = jnp.sum(grad_normed * mid_normed, axis=0, keepdims=True)
    total = jnp.zeros((SEG, width), F32)
    for s in range(slots):
        grad_tok[s] = grad[s * piece : s * piece + local]
        total += grad[s * piece + local : (s + 1) * piece]
    grad_mem[...] = total
    grad_out = tn(mixed[...], low)
    for j in range(4):
        target = out_kept if j % 2 == 0 else out_sent
        target[j // 2] = grad_out[j * HW : (j + 1) * HW].astype(BF)


def ffn0_back_kept(slots, local, gain, grad_in, normed_sum, mid, hid, mixed, weights):
    rows, width = grad_in.shape
    inner = width
    return call(
        functools.partial(ffn0_back_kept_kernel, slots, local),
        (
            Away(2, width + inner, width),
            Away(2, HW, width),
            Away(2, HW, width),
            Away(slots, local, width, dtype=F32),
            like(SEG, width, dtype=F32),
            like(1, width, dtype=F32),
            Away(slots, local + SEG, HW),
            Away(slots, local + SEG, HW),
            Away(2, slots, local + SEG, HW),
        ),
        2 * rows * width * (2 * width + 8 * inner),
        gain,
        Far(grad_in),
        Far(mid),
        Far(hid[0]),
        Far(hid[2]),
        packed(weights[0]),
        packed(weights[2]),
        *[packed(weights[j], True) for j in (1, 3)],
        Far(normed_sum),
        Far(mixed),
        name="ffn0_back_kept",
        early=True,
    )


def spread_heads(target, value):
    size, width = value.shape
    lane = iota((size, width), 1) // DH
    for h in range(width // DH):
        target[pl.ds(h * size, size), :] = jnp.where(lane == h, value, jnp.zeros_like(value))


def fold_heads(value, size):
    width = value.shape[1]
    lane = iota((size, width), 1) // DH
    total = jnp.zeros((size, width), value.dtype)
    for h in range(width // DH):
        total += jnp.where(lane == h, value[h * size : (h + 1) * size], 0.0)
    return total


def memory_valid(local, rows, live, owner):
    lane = iota((rows, local + SEG), 1)
    return (lane < live) | ((lane >= local) & (lane < local + M) & (owner > 0))


def attention1_kernel(slots, local, live_ref, owner_ref, gain, state, *refs):
    w = refs[:4]
    q_o, k_o, v_o, probs, out_tok, part, spread_k, spread_v = refs[4:]
    piece = local + SEG
    width = gain.shape[2]
    heads = width // DH
    normed = (normalize(state[...])[0] * gain_row(gain, 1, 0)).astype(BF)
    for j in range(4):
        proj = nn(normed, w[j][...]).astype(BF)
        lanes = pl.ds(j * HW, HW)
        q_o[:, lanes] = proj[:, :HW] * jnp.asarray(SCALE, BF)
        k_o[:, lanes] = proj[:, HW : 2 * HW]
        v_o[:, lanes] = proj[:, 2 * HW :]
    for ref in (q_o, k_o, v_o):
        ref.send()
    for s in range(slots):
        tok = pl.ds(s * piece, local)
        seg = pl.ds(s * piece + local, SEG)
        both = pl.ds(s * piece, piece)
        spread_heads(spread_k, q_o[seg, :])
        scores = nt(spread_k[...], k_o[both, :])
        valid = memory_valid(local, heads * SEG, live_ref[s], owner_ref[0])
        scores = jnp.where(valid, scores, FAR)
        top = jnp.max(scores, axis=1, keepdims=True)
        p = jnp.where(valid, jnp.exp(scores - top), 0.0)
        total = jnp.sum(p, axis=1, keepdims=True)
        here = pl.ds(s * SEG, SEG)
        part[here, pl.ds(0, width)] = fold_heads(nn(p.astype(BF), v_o[both, :]), SEG)
        lane = iota((SEG, HW), 1)
        extra = jnp.zeros((SEG, HW), F32)
        for h in range(heads):
            extra = jnp.where(lane == h, top[h * SEG : (h + 1) * SEG], extra)
            extra = jnp.where(lane == heads + h, total[h * SEG : (h + 1) * SEG], extra)
        part[here, pl.ds(width, HW)] = extra
    part.send()
    for s in range(slots):
        tok = pl.ds(s * piece, local)
        seg = pl.ds(s * piece + local, SEG)
        spread_heads(spread_k, k_o[seg, :])
        spread_heads(spread_v, v_o[seg, :])
        st = nt(spread_k[...], q_o[tok, :])
        st = jnp.where(iota((heads * SEG, local), 0) % SEG < M, st, FAR)
        st = st.reshape(heads, SEG, local)
        p = jnp.exp(st - jnp.max(st, axis=1, keepdims=True))
        p = p / jnp.sum(p, axis=1, keepdims=True)
        p = p.reshape(heads * SEG, local).T
        probs[s] = p
        out_tok[s] = nn(p.astype(BF), spread_v[...]).astype(BF)


def attention1(slots, local, live, owner, state, gain, w):
    rows, width = state.shape
    spread = (width // DH) * SEG
    return call(
        functools.partial(attention1_kernel, slots, local),
        (
            Away(rows, width),
            Away(rows, width),
            Away(rows, width),
            Away(slots, local, spread, dtype=F32),
            Away(slots, local, width),
            Away(slots * SEG, width + HW, dtype=F32),
        ),
        2 * rows * width * 3 * width + 8 * rows * width * spread,
        live,
        owner,
        gain,
        Far(state),
        *[packed_qkv(x) for x in w],
        scratch=[pltpu.VMEM((spread, width), BF), pltpu.VMEM((spread, width), BF)],
        name="attention1",
    )


def attention1_back_kernel(
    slots, local, share_ref, live_ref, owner_ref, gain, logs, grad_mid, *refs
):
    weights, (k, v, probs, q, mixed, state), w = refs[:4], refs[4:10], refs[10:14]
    refs = refs[6:]
    grads, grad_end, gain_sum, back, spread_a, spread_b, spread_o = refs[8:]
    piece = local + SEG
    width = gain.shape[2]
    heads = width // DH
    spread = heads * SEG
    low = grad_mid[...].astype(BF)
    for j in range(4):
        back[:, pl.ds(j * HW, HW)] = nt(low, weights[j][pl.ds(0, HW), :]).astype(BF)
    same = (iota((spread, spread), 0) // SEG == iota((spread, spread), 1) // SEG).astype(BF)

    def put(i, at, value):
        value = value.astype(BF)
        for j in range(4):
            grads[at, pl.ds(j * 3 * HW + i * HW, HW)] = value[:, j * HW : (j + 1) * HW]

    for s in range(slots):
        tok = pl.ds(s * piece, local)
        seg = pl.ds(s * piece + local, SEG)
        both = pl.ds(s * piece, piece)
        spread_heads(spread_a, k[seg, :])
        spread_heads(spread_b, v[seg, :])
        p = probs[s]
        dp = nt(back[tok, :], spread_b[...])
        product = p * dp
        hi = product.astype(BF)
        rest = (product - hi.astype(F32)).astype(BF)
        ds = (p * (dp - nn(hi, same) - nn(rest, same))).astype(BF)
        put(0, tok, nn(ds, spread_a[...]) * SCALE)
        mem_k = fold_heads(tn(ds, q[tok, :]), SEG)
        mem_v = fold_heads(tn(p.astype(BF), back[tok, :]), SEG)
        spread_heads(spread_a, q[seg, :])
        spread_heads(spread_b, back[seg, :])
        spread_heads(spread_o, mixed[seg, :])
        scores = nt(spread_a[...], k[both, :])
        log = jnp.concatenate([logs[pl.ds(s * SEG, SEG), :][:, h : h + 1] for h in range(heads)], axis=0)
        valid = memory_valid(local, spread, live_ref[s], owner_ref[0])
        p = jnp.where(valid, jnp.exp(jnp.where(valid, scores, FAR) - log), 0.0)
        delta = jnp.sum(
            spread_b[...].astype(F32) * spread_o[...].astype(F32), axis=1, keepdims=True
        )
        ds = (p * (nt(spread_b[...], v[both, :]) - delta)).astype(BF)
        put(0, seg, fold_heads(nn(ds, k[both, :]), SEG) * SCALE)
        grad_k = tn(ds, spread_a[...])
        grad_v = tn(p.astype(BF), spread_b[...])
        put(1, tok, grad_k[:local])
        put(2, tok, grad_v[:local])
        put(1, seg, grad_k[local:] + mem_k)
        put(2, seg, grad_v[local:] + mem_v)
    grads.send()
    normed, inverse = normalize(state[...])
    total = None
    for j in range(4):
        add = nt(grads[:, pl.ds(j * 3 * HW, 3 * HW)], w[j][...])
        total = add if j == 0 else total + add
    gain_sum[...] = jnp.sum(total * normed, axis=0, keepdims=True)
    grad_end[...] = once_rows(share_ref, slots, local, grad_mid[...]) + norm_backward(
        normed, inverse, gain_row(gain, 1, 0), total
    )


def attention1_back(
    slots, local, share, live, owner, gain, grad_mid, state, mixed, logs, q, k, v, probs, weights, w
):
    rows, width = state.shape
    spread = (width // DH) * SEG
    return call(
        functools.partial(attention1_back_kernel, slots, local),
        (
            Away(rows, 3 * width),
            Away(rows, width, dtype=F32),
            like(1, width, dtype=F32),
        ),
        2 * rows * width * 4 * width + 20 * rows * width * spread,
        share,
        live,
        owner,
        gain,
        logs,
        Far(grad_mid),
        *[Far(x, (HW, width), [((pl.ds(0, HW),), ())]) for x in weights],
        *[Far(x) for x in (k, v, probs, q, mixed, state)],
        *[packed_qkv(x) for x in w],
        scratch=[
            pltpu.VMEM((rows, width), BF),
            pltpu.VMEM((spread, width), BF),
            pltpu.VMEM((spread, width), BF),
            pltpu.VMEM((spread, width), BF),
        ],
        name="attention1_back",
    )


def attention1_weights_kernel(slots, local, share_ref, gain, grad_mid, mixed, state, grads, kept, sent):
    low = once_rows(share_ref, slots, local, grad_mid[...].astype(BF))
    grad_out = tn(mixed[...], low)
    normed = (normalize(state[...])[0] * gain_row(gain, 1, 0)).astype(BF)
    for j in (1, 3, 0, 2):
        target = kept if j % 2 == 0 else sent
        target[j // 2, pl.ds(0, HW), :] = grad_out[j * HW : (j + 1) * HW].astype(BF)
        target[j // 2, pl.ds(HW, 3 * HW), :] = tn(grads[:, pl.ds(j * 3 * HW, 3 * HW)], normed).astype(BF)
        if j == 3:
            sent.send()


def attention1_weights(slots, local, share, gain, grad_mid, state, mixed, grads):
    rows, width = state.shape
    return call(
        functools.partial(attention1_weights_kernel, slots, local),
        (Away(2, 4 * HW, width), Away(2, 4 * HW, width)),
        2 * rows * width * 4 * width,
        share,
        gain,
        Far(grad_mid),
        Far(mixed),
        Far(state),
        Far(grads),
        name="attention1_weights",
        early=True,
    )


def on_device(
    tokens, lengths, memory, norm_gain, w_qkv, output_weight, w_up, w_down, cot_tokens, cot_memory
):
    slots, local, width = tokens.shape
    me = lax.axis_index("tensor")
    block = jnp.arange(4, dtype=jnp.int32)
    valid = jnp.clip(lengths[:, None] - (me ^ block)[None, :] * local, 0, local)
    live = valid[:, 0]
    owner = (me == 0).astype(jnp.int32)[None]
    share = (jnp.arange(slots, dtype=jnp.int32) % 4 == me).astype(jnp.int32)

    near = exchange(tokens, "tensor", 1)
    tok = [Chain(far_chain(tokens[s])) for s in range(slots)]
    fence(None, *tok)
    move0 = Chain(weights_chain(pack_weights(output_weight[0], w_up[0], w_down[0], w_qkv[1])))
    move1 = Chain(weights_chain(jnp.concatenate([output_weight[1], w_up[1], w_down[1]], axis=0)))
    fence(None, tok[0])
    finish(tok[0])
    saved, outs, out_moves = [], [], []
    beside = [[move0], [], [move0, move1]]
    for s in range(slots):
        finish(tok[s])
        rest = [t.arrived for t in tok[2:]] if s == 1 else []
        received, rest = fence((tok[s].result, rest), *out_moves, *beside[s])
        for t, arrived in zip(tok[2:], rest):
            t.arrived = arrived
        *out, qa, ka, va = attention0(s, valid[s], tokens, (near, *received), memory, norm_gain, w_qkv)
        out[0] = land(out[0], *tok[s + 1 : s + 2], *([move0, move1] if s == slots - 1 else []))
        saved.append((qa, ka, va))
        outs.append(out)
        out_moves.append(Chain(split_chain(*out[1:])))
    tok_blocks = [(near, *t.result) for t in tok]
    fence(None, *out_moves)
    finish(*out_moves, move0)
    weights0 = move0.result
    moved = [m.result for m in out_moves]
    moved = fence(moved, move1)
    mid0, state1, *hid0, mixed0 = ffn0(
        tokens, memory, norm_gain, [o[0] for o in outs], moved, weights0
    )
    attn1 = weights0
    q1, k1, v1, probs, out_tok, parts = attention1(slots, local, live, owner, state1, norm_gain, attn1)
    probs = land(probs, move1)
    parts = Chain(gather_chain(parts))
    finish(parts, move1)
    weights1 = move1.result
    res_tok, res_mem, kept1, sent1, grad_mid1, gain_f1, mixed1, logs = ffn1(
        share, live, norm_gain, state1, out_tok, cot_tokens, cot_memory, parts.result, weights1
    )

    sum1a = Chain(rows_chain(kept1, sent1))
    copied = Chain(copy_chain(res_mem))
    grad_mid1 = fence(grad_mid1, sum1a, copied)
    proj1, grad1, gain_a1 = attention1_back(
        slots, local, share, live, owner, norm_gain, grad_mid1, state1, mixed1, logs, q1, k1, v1, probs,
        weights1, attn1,
    )
    proj1, grad1 = fence((proj1, grad1), sum1a, copied)
    kept1, sent1 = attention1_weights(slots, local, share, norm_gain, grad_mid1, state1, mixed1, proj1)
    sum1b = Chain(rows_chain(kept1, sent1))
    finish(copied)
    grad1, res_mem = fence((grad1, copied.result), sum1b)
    sent0, normed_sum = ffn0_back_sent(norm_gain, grad1, mid0, hid0, weights0)
    sum0 = Chain(core_chain([None, None], sent0))
    finish(sum1a)
    sum1a = Chain(halved(sum1a.result))
    normed_sum = fence(normed_sum, sum0, sum1a, sum1b)
    kept0, out_kept, out_sent, grad_tok, grad_mem, gain_f0, d_own, *d_moving = ffn0_back_kept(
        slots, local, norm_gain, grad1, normed_sum, mid0, hid0, mixed0, weights0
    )
    grad_mem = land(grad_mem, sum0, sum1a, sum1b)
    sum0o = Chain(core_chain(out_kept, out_sent))
    d_move = Chain(split_chain(*d_moving))
    fence(None, d_move)
    finish(sum1a, sum1b)
    sum1b = Chain(halved(sum1b.result))
    fence((), sum1b, sum0o)
    finish(sum0o)
    got = sum0.arrived[0]
    near = jnp.concatenate([added(kept0[0], got[0]), sum0o.result[0]])
    far = jnp.concatenate([added(kept0[1], got[1]), sum0o.result[1]])
    near, far, d_move.arrived = lax.optimization_barrier((near, far, d_move.arrived))
    sum0 = Chain(cross_chain(near, far))
    finish(d_move, sum1b)
    sum1 = Chain(two_halves(sum1a.result, sum1b.result))
    moved = [d_own, *d_move.result]
    before, row_sums = None, []
    for s in range(slots):
        moved = fence(moved, sum0, sum1, *row_sums)
        kept, sent, *before = attention0_back(
            s, tokens, tok_blocks[s], memory, norm_gain, w_qkv, saved[s], outs[s], moved, before
        )
        before[2] = land(before[2], sum0, sum1, *row_sums)
        row_sums.append(Chain(rows_chain(kept, sent)))
    grad_qkv0, mem_normed, gain_a0 = before
    small = [mem_normed[:M], grad_mem[:M], gain_a0, gain_a1, gain_f0, gain_f1]
    last = Chain(last_chain(grad_qkv0, jnp.concatenate(small, axis=0)))
    fence((), last, *row_sums)
    fence((), last, *row_sums, sum0)
    fence((), last, sum1)
    fence((), sum0, last)
    fence(None, sum0)
    fence((), last)
    finish(sum0, last, sum1, *row_sums)
    sum0q, small = last.result
    sum1 = sum1.result
    sum0 = sum0.result
    rows = []
    for s in range(slots):
        normed, inverse = normalize(tokens[s].astype(F32))
        gain = norm_gain[0, 0].astype(F32)
        total = row_sums[s].result.astype(F32)
        rows.append(grad_tok[s] + norm_backward(normed, inverse, gain, total))
    normed, inverse = normalize(memory.astype(F32))
    grad_memory = small[M : 2 * M] + norm_backward(normed, inverse, gain, small[:M])
    gains = small[2 * M : 2 * M + 4]

    def split_qkv(value):
        return jnp.swapaxes(value.reshape(3, HW, width), 1, 2)

    return (
        res_tok,
        res_mem,
        jnp.stack(rows),
        grad_memory,
        gains[0:2],
        gains[2:4],
        jnp.stack([split_qkv(sum0q), split_qkv(sum1[2 * width + HW :])]).astype(F32),
        jnp.stack([sum0[2 * width :], sum1[2 * width : 2 * width + HW]]).astype(F32),
        jnp.stack([sum0[:width], sum1[:width]]).astype(F32),
        jnp.stack([sum0[width : 2 * width], sum1[width : 2 * width]]).astype(F32),
    )


def solution(mesh):
    return jax.shard_map(
        on_device,
        mesh=mesh,
        in_specs=(
            P("dp", "tensor", None),
            P("dp"),
            P(),
            P(),
            P(None, None, None, "tensor"),
            P(None, "tensor", None),
            P(None, None, "tensor"),
            P(None, "tensor", None),
            P("dp", "tensor", None),
            P("dp", None, None),
        ),
        out_specs=(
            P("dp", "tensor", None),
            P("dp", None, None),
            P("dp", "tensor", None),
            P(),
            P(),
            P(),
            P(None, None, None, "tensor"),
            P(None, "tensor", None),
            P(None, None, "tensor"),
            P(None, "tensor", None),
        ),
        check_vma=False,
    )
```
